32 devices in a mesh: space: 4 (over y, core), tm: 8 (over z, x).
Axes of the slice: x: 2, y: 2, z: 4, core: 2. Of those that a mesh axis runs over, the one named last changes fastest.
Arguments:
- eigenvectors: bfloat16 [8, 2, 3, 4, 256, 256], P('tm', None, None, 'space'), may hold values from -0.078125 to 0.078125
- momenta: int32 [6, 3], replicated, may hold values from -2 to 2
- displacement: int32 [6], replicated, may hold values from 0 to 3, as said below
- source_times: int32 [4], replicated, may hold values from 0 to 7
- perambulators: bfloat16 [8, 4, 2, 256, 256], P('tm', None, None, 'space'), may hold values from -1 to 1
Outputs:
- correlator: float32 [8, 4, 2, 6, 6], P('tm')
- two_meson: float32 [8, 4, 2, 6, 6], P('tm')
The draws below stay inside these ranges and needn't reach their ends.
Inputs may be any that keep to these rules, and one draw needn't show every extreme that they name: `displacement`: 0 keeps the site, 1, 2, 3 move one site forward along x, y, z; each of the four values is used by some operator.
All inputs are finite; a program needn't handle non-finite values.
Results may differ from the reference program's by a relative error of at most 0.0078.
Values may be sent and summed in bfloat16 or wider, within the bound.
No kernel may reach another device: no remote copies, remote signals or barrier semaphores. Data moves between devices by JAX's collectives and lax.ppermute only.
A program may use at most 64 MiB of HBM per device.

```python
import math
import jax
import jax.numpy as jnp
from jax import lax

NVEC = 256
OPS = 6
LX = 16
LY = 16
NSRC = 4
NZ = 4
NT = 8


def draw_displacement(key, part):
    leading = jax.random.permutation(jax.random.fold_in(key, 11), 4).astype(jnp.int32)
    remaining = jax.random.randint(jax.random.fold_in(key, 12), (OPS - 4,), 0, 4, dtype=jnp.int32)
    shuffle = jax.random.permutation(jax.random.fold_in(key, 13), OPS)
    return jnp.concatenate([leading, remaining])[shuffle].astype(jnp.int32)


def place_ends(array, stream_key, low, largest):
    place = [jax.random.randint(jax.random.fold_in(stream_key, axis), (), 0, length) for axis, length in enumerate(array.shape)]
    widest = array.shape.index(max(array.shape))
    neighbour = place[:widest] + [(place[widest] + 1) % array.shape[widest]] + place[widest + 1:]
    return array.at[tuple(place)].set(low).at[tuple(neighbour)].set(largest)


def levels(own_key, extent, shards, least, high):
    def one(axis_at, blocks):
        draws = jax.random.uniform(jax.random.fold_in(jax.random.fold_in(own_key, 6), axis_at), (blocks,), jnp.float32, least / len(shards), high / len(shards))
        return jnp.repeat(jnp.exp(draws), extent[axis_at] // blocks).reshape((-1,) + (1,) * (len(extent) - axis_at - 1))

    gain = one(*shards[0])
    for cut in shards[1:]:
        gain = gain * one(*cut)
    return gain


def centred(stream_key, dims, spread, most, cuts=(), kind=jnp.bfloat16):
    entries = spread * jax.random.normal(stream_key, dims, jnp.float32)
    if cuts:
        entries = entries * levels(stream_key, dims, cuts, -0.22, 0.18)
    return jnp.clip(entries, -most, most).astype(kind)


def setup_inputs(seed: int = 0) -> dict:
    splits = jax.random.split(jax.random.key(seed), 6)
    return {
        "eigenvectors": centred(splits[0], (NT, 2, 3, NZ, LY * LX, NVEC), (6 * LX * LY * NZ) ** -0.5, 0.078125, ((0, 8), (3, 4))),
        "momenta": place_ends(jax.random.randint(splits[1], (OPS, 3), -2, 3), jax.random.fold_in(splits[1], 1), -2, 2).astype(jnp.int32),
        "displacement": draw_displacement(jax.random.fold_in(splits[5], 71), 0),
        "source_times": place_ends(jax.random.randint(splits[3], (NSRC,), 0, NT), jax.random.fold_in(splits[3], 1), 0, NT - 1).astype(jnp.int32),
        "perambulators": centred(splits[4], (NT, NSRC, 2, NVEC, NVEC), (max(1, 2 * NVEC * NVEC // (3 * LX * LY * NZ))) ** -0.5, 1.0, ((0, 8), (3, 4))),
    }


def contract(formula, left, right):
    return jnp.einsum(formula, left.astype(jnp.float32), right.astype(jnp.float32), precision=lax.Precision.HIGHEST, preferred_element_type=jnp.float32)


def complex_product(formula, left, right, conjugate):
    if conjugate:
        real_part = contract(formula, left[0], right[0]) + contract(formula, left[1], right[1])
        imaginary_part = contract(formula, left[1], right[0]) - contract(formula, left[0], right[1])
    else:
        real_part = contract(formula, left[0], right[0]) - contract(formula, left[1], right[1])
        imaginary_part = contract(formula, left[0], right[1]) + contract(formula, left[1], right[0])
    return real_part, imaginary_part


def plane_angles(momenta, operator, z_coords, z_extent):
    plane = jnp.arange(LY * LX, dtype=jnp.int32)
    along_x = ((momenta[operator, 0] * (plane % LX)) % LX).astype(jnp.float32) * (2.0 * math.pi / LX)
    along_y = ((momenta[operator, 1] * (plane // LX)) % LY).astype(jnp.float32) * (2.0 * math.pi / LY)
    along_z = ((momenta[operator, 2] * z_coords) % z_extent).astype(jnp.float32) * (2.0 * math.pi / z_extent)
    return (along_x + along_y)[None, :] + along_z[:, None]


def shift_first(field):
    layout = field.shape
    opened = field.reshape(layout[:-2] + (LY, LX, layout[-1]))
    return jnp.roll(opened, -1, axis=-2).reshape(layout)


def shift_second(field):
    layout = field.shape
    opened = field.reshape(layout[:-2] + (LY, LX, layout[-1]))
    return jnp.roll(opened, -1, axis=-3).reshape(layout)


def shift_third(field):
    return jnp.roll(field, -1, axis=-3)


def unmoved(field):
    return field


def weighted(real_in, imaginary_in, angles):
    cosine = jnp.cos(angles)[:, :, None]
    sine = jnp.sin(angles)[:, :, None]
    real_wide = real_in.astype(jnp.float32)
    imaginary_wide = imaginary_in.astype(jnp.float32)
    w_real = (cosine * real_wide + sine * imaginary_wide).astype(jnp.bfloat16)
    w_imaginary = (cosine * imaginary_wide - sine * real_wide).astype(jnp.bfloat16)
    return w_real, w_imaginary


def reference(eigenvectors, momenta, displacement, source_times, perambulators):
    z_coords = jnp.arange(NZ, dtype=jnp.int32)

    def time_elementals(field):
        results = []
        for operator in range(OPS):
            shifted = lax.switch(displacement[operator], [unmoved, shift_first, shift_second, shift_third], field)
            angles = plane_angles(momenta, operator, z_coords, NZ)
            w_real, w_imaginary = weighted(shifted[0], shifted[1], angles)
            pair = complex_product('kn,kc->cn', (w_real.reshape(-1, NVEC), w_imaginary.reshape(-1, NVEC)), (field[0].reshape(-1, NVEC), field[1].reshape(-1, NVEC)), True)
            results.append(jnp.stack(pair))
        return jnp.stack(results)

    elements = lax.map(time_elementals, eigenvectors).astype(jnp.bfloat16)

    def time_traces(inputs):
        sink, peram_slice = inputs
        collected = []
        for source in range(NSRC):
            source_block = lax.dynamic_index_in_dim(elements, source_times[source].astype(jnp.int32), 0, keepdims=False)
            peram_pair = (peram_slice[source, 0], peram_slice[source, 1])
            left = complex_product('aij,jk->aik', (sink[:, 0], sink[:, 1]), peram_pair, False)
            right = complex_product('bkl,il->bki', (source_block[:, 0], source_block[:, 1]), peram_pair, True)
            traces = complex_product('aik,bki->ab', left, right, False)
            collected.append(jnp.stack(traces))
        return jnp.stack(collected)

    correlator = lax.map(time_traces, (elements, perambulators))
    diagonal = jnp.diagonal(correlator, axis1=3, axis2=4)
    diag_real = diagonal[:, :, 0]
    diag_imaginary = diagonal[:, :, 1]
    pair_real = diag_real[:, :, :, None] * diag_real[:, :, None, :] - diag_imaginary[:, :, :, None] * diag_imaginary[:, :, None, :]
    pair_imaginary = diag_real[:, :, :, None] * diag_imaginary[:, :, None, :] + diag_imaginary[:, :, :, None] * diag_real[:, :, None, :]
    two_meson = jnp.stack([pair_real, pair_imaginary], axis=2)
    return correlator, two_meson
```

```python
import functools
import math

import jax
import jax.numpy as jnp
from jax import lax
from jax.experimental import pallas as pl
from jax.experimental.pallas import tpu as pltpu
from jax.sharding import PartitionSpec as P

LX = 16
LY = 16
PLANE = LX * LY
LANES = 128
F32 = jnp.float32
BF16 = jnp.bfloat16
VMEM_LIMIT = 58 * 1024 * 1024

ANY = pl.BlockSpec(memory_space=pl.ANY)
SMEM = pl.BlockSpec(memory_space=pltpu.SMEM)
VMEM = pl.BlockSpec(memory_space=pltpu.VMEM)


def swap_bit(block, axis, mask):
    count = lax.axis_size(axis)
    return lax.ppermute(block, axis, [(i, i ^ mask) for i in range(count)])


def along_line(block, distance, line):
    route = [
        (2 * z + x, 2 * (z + distance) + x)
        for z in range(line)
        for x in range(2)
        if 0 <= z + distance < line
    ]
    return lax.ppermute(block, "tm", route)


def gather_by_swaps(block):
    count = lax.axis_size("space")
    held = {0: block}
    mask = count // 2
    while mask:
        for key in sorted(held):
            held[key | mask] = swap_bit(held[key], "space", mask)
        mask //= 2
    return [held[key] for key in range(count)]


def params():
    return pltpu.CompilerParams(vmem_limit_bytes=VMEM_LIMIT)


def elemental_kernel(slots, held, stage, last, *refs):
    do_ref, src_ref, off_ref, where_ref, zphase_ref, phase_ref = refs[:6]
    slab_refs = refs[6 : 6 + held]
    rest = refs[6 + held :]
    if stage:
        prior_ref, rest = rest[0], rest[1:]
    if last:
        full_ref, keep_ref, send_ref = rest[:3]
        rest = rest[3:]
    else:
        out_ref, rest = rest[0], rest[1:]
    slabs, turned, acc, sems = rest
    operators, vectors = acc.shape[0], acc.shape[1]
    colours = turned.shape[0]

    copies = []
    for m in range(held):
        copies.append(
            pltpu.make_async_copy(
                slab_refs[m], slabs.at[m, :, pl.ds(0, PLANE), :], sems.at[2 * m]
            )
        )
        copies.append(
            pltpu.make_async_copy(
                slab_refs[m].at[:, pl.ds(0, LX), :],
                slabs.at[m, :, pl.ds(PLANE, LX), :],
                sems.at[2 * m + 1],
            )
        )
    for copy in copies:
        copy.start()
    if stage:
        acc[...] = prior_ref[...]
    else:
        acc[...] = jnp.zeros_like(acc)
    for copy in copies:
        copy.wait()

    row = lax.broadcasted_iota(jnp.int32, (PLANE, PLANE), 0)
    column = lax.broadcasted_iota(jnp.int32, (PLANE, PLANE), 1)
    wanted = jnp.where(row % LX == LX - 1, row - (LX - 1), row + 1)
    step_x = (column == wanted).astype(F32).astype(BF16)

    def one_slab(m, carry):
        for colour in range(colours):
            for part in range(2):
                block = slabs[m, part * colours + colour, pl.ds(0, PLANE), :]
                turned[colour, :, pl.ds(part * PLANE, PLANE)] = block.T
                moved = jnp.dot(step_x, block, preferred_element_type=F32)
                slabs[held, part * colours + colour, pl.ds(0, PLANE), :] = moved.astype(BF16)

        def one_operator(o, inner):
            @pl.when(do_ref[m, o] == stage)
            def _():
                src = src_ref[m, o]
                off = pl.multiple_of(off_ref[o], LX)
                cos_z, sin_z = zphase_ref[0, m, o], zphase_ref[1, m, o]
                cos_p, sin_p = phase_ref[o, 0], phase_ref[o, 1]
                cosine = cos_p * cos_z - sin_p * sin_z
                sine = sin_p * cos_z + cos_p * sin_z
                wide = vectors // LANES
                cosine = jnp.concatenate([cosine] * wide, axis=1)
                sine = jnp.concatenate([sine] * wide, axis=1)
                total = None
                for colour in range(colours):
                    real = slabs[src, colour, pl.ds(off, PLANE), :].astype(F32)
                    imaginary = slabs[src, colours + colour, pl.ds(off, PLANE), :].astype(F32)
                    w_real = (cosine * real + sine * imaginary).astype(BF16)
                    w_imaginary = (cosine * imaginary - sine * real).astype(BF16)
                    right = jnp.concatenate(
                        [
                            jnp.concatenate([w_real, w_imaginary], axis=1),
                            jnp.concatenate([w_imaginary, -w_real], axis=1),
                        ],
                        axis=0,
                    )
                    term = jnp.dot(turned[colour], right, preferred_element_type=F32)
                    total = term if total is None else total + term
                acc[o] += total

            return inner

        return lax.fori_loop(0, operators, one_operator, carry)

    lax.fori_loop(0, held, one_slab, 0)

    if last:
        block_rows = keep_ref.shape[2]
        first = pl.multiple_of(where_ref[0] * block_rows, block_rows)
        half = where_ref[1]
        for o in range(operators):
            full_ref[o] = acc[o].astype(BF16)
        for o in range(operators):
            for part in range(2):
                own = full_ref[o, pl.ds(first, block_rows), pl.ds(part * vectors, vectors)]
                low, high = own[:, :LANES], own[:, LANES:]
                keep_ref[part, o] = jnp.where(half == 0, low, high)
                send_ref[part, o] = jnp.where(half == 0, high, low)
    else:
        out_ref[...] = acc[...]


def elementals(stage, last, tables, slab_list, prior, block_rows):
    parts_colours, plane, vectors = slab_list[0].shape
    colours = parts_colours // 2
    slots = len(slab_list)
    operators = tables[0].shape[1]
    wide = jax.ShapeDtypeStruct((operators, vectors, 2 * vectors), F32)
    if last:
        piece = jax.ShapeDtypeStruct((2, operators, block_rows, LANES), BF16)
        outs = (jax.ShapeDtypeStruct(wide.shape, BF16), piece, piece)
        out_specs = (VMEM, VMEM, VMEM)
    else:
        outs, out_specs = wide, VMEM
    priors = [prior] if stage else []
    return pl.pallas_call(
        functools.partial(elemental_kernel, slots, slots, stage, last),
        out_shape=outs,
        in_specs=[SMEM] * 5 + [VMEM] + [ANY] * slots + [VMEM] * len(priors),
        out_specs=out_specs,
        scratch_shapes=[
            pltpu.VMEM((slots + 1, parts_colours, plane + LX, vectors), BF16),
            pltpu.VMEM((colours, vectors, 2 * plane), BF16),
            pltpu.VMEM(wide.shape, F32),
            pltpu.SemaphoreType.DMA((2 * slots,)),
        ],
        compiler_params=params(),
        cost_estimate=pl.CostEstimate(
            flops=2 * slots * operators * parts_colours * plane * vectors * 2 * vectors // 2,
            bytes_accessed=slots * parts_colours * plane * vectors * 2,
            transcendentals=0,
        ),
        name="elementals_last" if last else "elementals_first",
    )(*tables, *slab_list, *priors)


def both_kernel(blocks, where_ref, order_ref, e_ref, *refs):
    peram_refs = refs[:blocks]
    keep_ref, send_ref, whole, left, turned, middle, sems = refs[blocks:]
    sources, _, vectors, _ = whole.shape
    operators = e_ref.shape[0]
    block_rows = keep_ref.shape[3]
    copies = []
    for m in range(blocks):
        begin = pl.multiple_of(order_ref[m] * block_rows, block_rows)
        copies.append(
            pltpu.make_async_copy(
                peram_refs[m], whole.at[:, :, pl.ds(begin, block_rows), :], sems.at[m]
            )
        )
    for copy in copies:
        copy.start()
    for copy in copies:
        copy.wait()
    first = pl.multiple_of(where_ref[0] * block_rows, block_rows)
    half = where_ref[1]
    for s in range(sources):
        for part in range(2):
            turned[part] = whole[s, part].T
        real = turned[0, pl.ds(first, block_rows), :]
        imaginary = turned[1, pl.ds(first, block_rows), :]
        base = 2 * s * block_rows
        left[pl.ds(base, block_rows), :] = jnp.concatenate([real, -imaginary], axis=1)
        left[pl.ds(base + block_rows, block_rows), :] = jnp.concatenate([imaginary, real], axis=1)
    for a in range(operators):
        product = lax.dot_general(
            left[...], e_ref[a], (((1,), (1,)), ((), ())), preferred_element_type=F32
        )
        high = product.astype(BF16)
        low = (product - high.astype(F32)).astype(BF16)
        for s in range(sources):
            for part in range(2):
                base = (2 * s + part) * block_rows
                rows = pl.ds(a * block_rows, block_rows)
                columns = pl.ds(part * vectors, vectors)
                middle[0, s, rows, columns] = high[base : base + block_rows]
                middle[1, s, rows, columns] = low[base : base + block_rows]
    for s in range(sources):
        real, imaginary = whole[s, 0], whole[s, 1]
        right = jnp.concatenate(
            [
                jnp.concatenate([real, -imaginary], axis=1),
                jnp.concatenate([imaginary, real], axis=1),
            ],
            axis=0,
        )
        image = jnp.dot(middle[0, s], right, preferred_element_type=F32)
        image = image + jnp.dot(middle[1, s], right, preferred_element_type=F32)
        image = image.astype(BF16)
        for a in range(operators):
            for part in range(2):
                rows = image[a * block_rows : (a + 1) * block_rows]
                low = rows[:, part * vectors : part * vectors + LANES]
                high = rows[:, part * vectors + LANES : (part + 1) * vectors]
                keep_ref[s, part, a] = jnp.where(half == 0, low, high)
                send_ref[s, part, a] = jnp.where(half == 0, high, low)


def both_sides(where, order, elements, perams):
    blocks = len(perams)
    sources, _, block_rows, vectors = perams[0].shape
    operators = elements.shape[0]
    piece = jax.ShapeDtypeStruct((sources, 2, operators, block_rows, LANES), BF16)
    return pl.pallas_call(
        functools.partial(both_kernel, blocks),
        out_shape=(piece, piece),
        in_specs=[SMEM, SMEM, VMEM] + [ANY] * blocks,
        out_specs=(VMEM, VMEM),
        scratch_shapes=[
            pltpu.VMEM((sources, 2, vectors, vectors), BF16),
            pltpu.VMEM((sources * 2 * block_rows, 2 * vectors), BF16),
            pltpu.VMEM((2, vectors, vectors), BF16),
            pltpu.VMEM((2, sources, operators * block_rows, 2 * vectors), BF16),
            pltpu.SemaphoreType.DMA((blocks,)),
        ],
        compiler_params=params(),
        cost_estimate=pl.CostEstimate(
            flops=2 * 3 * sources * operators * 4 * block_rows * vectors * vectors,
            bytes_accessed=8 * sources * vectors * vectors,
            transcendentals=0,
        ),
        name="both_sides",
    )(where, order, elements, *perams)


def trace_kernel(offsets, pick_ref, *refs):
    count = len(offsets)
    same, other = refs[:count], refs[count : 2 * count]
    own_ref, pair_ref, out_ref, picked, wide_e, wide_g, sems = refs[2 * count :]
    sources = own_ref.shape[0]
    _, operators, block_rows, lanes = same[0].shape
    rows = 2 * operators
    for s in range(sources):
        for cls, pool in enumerate((same, other)):
            for at, distance in enumerate(offsets):

                @pl.when((pick_ref[0, s] == cls) & (pick_ref[1, s] == distance))
                def _(pool=pool, at=at, s=s):
                    pltpu.make_async_copy(pool[at], picked.at[s], sems.at[s]).start()

    def spread(wide, count_rows):
        pieces = [
            wide[pl.ds(k, count_rows, stride=block_rows), :].astype(BF16)
            for k in range(block_rows)
        ]
        return jnp.concatenate(pieces, axis=1)

    for s in range(sources):
        wide_g[pl.ds(0, rows * block_rows), :] = (
            own_ref[s].astype(F32).reshape(rows * block_rows, lanes)
        )
        wide_g[pl.ds(rows * block_rows, rows * block_rows), :] = (
            pair_ref[s].astype(F32).reshape(rows * block_rows, lanes)
        )
        pltpu.make_async_copy(same[0], picked.at[s], sems.at[s]).wait()
        wide_e[...] = picked[s].astype(F32).reshape(rows * block_rows, lanes)
        out_ref[s] = lax.dot_general(
            spread(wide_g, 2 * rows),
            spread(wide_e, rows),
            (((1,), (1,)), ((), ())),
            preferred_element_type=F32,
        )


def traces(pick, offsets, same, other, own, pair):
    sources, _, operators, block_rows, lanes = own.shape
    rows = 2 * operators
    return pl.pallas_call(
        functools.partial(trace_kernel, offsets),
        out_shape=jax.ShapeDtypeStruct((sources, 2 * rows, rows), F32),
        in_specs=[SMEM] + [ANY] * (2 * len(offsets)) + [VMEM, VMEM],
        out_specs=VMEM,
        scratch_shapes=[
            pltpu.VMEM((sources,) + same[0].shape, BF16),
            pltpu.VMEM((rows * block_rows, lanes), F32),
            pltpu.VMEM((2 * rows * block_rows, lanes), F32),
            pltpu.SemaphoreType.DMA((sources,)),
        ],
        compiler_params=params(),
        cost_estimate=pl.CostEstimate(
            flops=4 * sources * rows * rows * block_rows * lanes,
            bytes_accessed=6 * own.size,
            transcendentals=0,
        ),
        name="traces",
    )(pick, *same, *other, own, pair)


def phase_tables(momenta, z_coords, z_extent):
    plane = jnp.arange(PLANE, dtype=jnp.int32)
    along_x = (momenta[:, 0:1] * (plane % LX)[None] % LX).astype(F32) * (2.0 * math.pi / LX)
    along_y = (momenta[:, 1:2] * (plane // LX)[None] % LY).astype(F32) * (2.0 * math.pi / LY)
    angle = along_x + along_y
    table = jnp.stack([jnp.cos(angle), jnp.sin(angle)], axis=1)
    table = jnp.broadcast_to(table[..., None], table.shape + (LANES,))
    along_z = (momenta[:, 2][None, :] * z_coords[:, None] % z_extent).astype(F32) * (
        2.0 * math.pi / z_extent
    )
    return table, jnp.stack([jnp.cos(along_z), jnp.sin(along_z)])


def body(eigenvectors, momenta, displacement, source_times, perambulators):
    _, parts, colours, _, plane, vectors = eigenvectors.shape
    slabs = lax.axis_size("space")
    line = lax.axis_size("tm") // 2
    block_rows = vectors // slabs
    me = lax.axis_index("space").astype(jnp.int32)
    time = lax.axis_index("tm").astype(jnp.int32)
    where = jnp.stack([me, time % 2])
    order = jnp.arange(slabs, dtype=jnp.int32) ^ me
    above = ((order + 1) % slabs) ^ me
    near = min(2, slabs)

    own = eigenvectors.reshape(parts * colours, plane, vectors)
    slab_list = gather_by_swaps(own)
    near_list = [own] + [swap_bit(own, "space", 1)] * (near - 1)

    moves_z = displacement[None, :] == 3
    slot = jnp.arange(slabs, dtype=jnp.int32)[:, None]

    def tables(held):
        source = jnp.where(
            moves_z, above[:held, None], jnp.where(displacement[None, :] == 1, held, slot[:held])
        )
        late = (slot[:held] >= near) | (moves_z & (above[:held, None] >= near))
        plane_phase, z_phase = phase_tables(momenta, order[:held], slabs)
        return (
            late.astype(jnp.int32),
            source.astype(jnp.int32),
            jnp.where(displacement == 2, LX, 0).astype(jnp.int32),
            where,
            z_phase,
            plane_phase,
        )

    early = elementals(0, False, tables(near), near_list, None, block_rows)
    full, keep, send = elementals(1, True, tables(slabs), slab_list, early, block_rows)
    received = swap_bit(send, "tm", 1)

    offsets = [0]
    same, other = [keep], [received]
    for distance in range(1, line):
        for sign in (1, -1):
            offsets.append(-sign * distance)
            same.append(along_line(keep, sign * distance, line))
    for distance in range(1, line):
        for sign in (1, -1):
            other.append(along_line(received, sign * distance, line))

    peram, _ = lax.optimization_barrier((perambulators[0], slab_list[slabs // 2]))
    perams = gather_by_swaps(peram)
    g_keep, g_send = both_sides(where, order, full, perams)
    g_pair = swap_bit(g_send, "tm", 1)

    pick = jnp.stack([(source_times % 2) ^ (time % 2), source_times // 2 - time // 2])
    raw = traces(pick.astype(jnp.int32), offsets, same, other, g_keep, g_pair)
    operators = momenta.shape[0]
    rows = 2 * operators
    mine = raw[:, :rows] + swap_bit(raw[:, rows:], "tm", 1)
    total = lax.psum(mine, "space")
    n = operators
    real = total[:, :n, :n] - total[:, n:, n:]
    imaginary = total[:, :n, n:] + total[:, n:, :n]
    diag_real = jnp.diagonal(real, axis1=1, axis2=2)
    diag_imaginary = jnp.diagonal(imaginary, axis1=1, axis2=2)
    pair_real = (
        diag_real[:, :, None] * diag_real[:, None, :]
        - diag_imaginary[:, :, None] * diag_imaginary[:, None, :]
    )
    pair_imaginary = (
        diag_real[:, :, None] * diag_imaginary[:, None, :]
        + diag_imaginary[:, :, None] * diag_real[:, None, :]
    )
    correlator = jnp.stack([real, imaginary], axis=1)[None]
    two_meson = jnp.stack([pair_real, pair_imaginary], axis=1)[None]
    return (correlator, two_meson)


def solution(mesh):
    placed = (
        P("tm", None, None, "space", None, None),
        P(),
        P(),
        P(),
        P("tm", None, None, "space", None),
    )
    return jax.shard_map(
        body,
        mesh=mesh,
        in_specs=placed,
        out_specs=(P("tm", None, None, None, None), P("tm", None, None, None, None)),
        check_vma=False,
    )
```

```python
import functools
import math

import jax
import jax.numpy as jnp
from jax import lax
from jax.experimental import pallas as pl
from jax.experimental.pallas import tpu as pltpu
from jax.sharding import PartitionSpec as P

LX = 16
LY = 16
PLANE = LX * LY
LANES = 128
F32 = jnp.float32
BF16 = jnp.bfloat16
CHUNK = 32
VMEM_LIMIT = 58 * 1024 * 1024

ANY = pl.BlockSpec(memory_space=pl.ANY)
SMEM = pl.BlockSpec(memory_space=pltpu.SMEM)
VMEM = pl.BlockSpec(memory_space=pltpu.VMEM)


def swap_bit(block, axis, mask):
    count = lax.axis_size(axis)
    return lax.ppermute(block, axis, [(i, i ^ mask) for i in range(count)])


def along_line(block, distance, line):
    route = [
        (2 * z + x, 2 * (z + distance) + x)
        for z in range(line)
        for x in range(2)
        if 0 <= z + distance < line
    ]
    return lax.ppermute(block, "tm", route)


def gather_by_swaps(block):
    count = lax.axis_size("space")
    held = {0: block}
    mask = count // 2
    while mask:
        for key in sorted(held):
            held[key | mask] = swap_bit(held[key], "space", mask)
        mask //= 2
    return [held[key] for key in range(count)]


def params():
    return pltpu.CompilerParams(vmem_limit_bytes=VMEM_LIMIT)


def elemental_kernel(held, near, late, last, whole, first_colour, *refs):
    move_ref, zphase_ref, phase_ref = refs[:3]
    slab_refs = refs[3 : 3 + held]
    rest = refs[3 + held :]
    if late:
        prior_ref, rest = rest[0], rest[1:]
    if last:
        full_ref, keep_ref, send_ref = rest[:3]
        rest = rest[3:]
    else:
        out_ref, rest = rest[0], rest[1:]
    slabs, turned, mixed, acc, sems = rest
    operators = acc.shape[0]
    vectors = acc.shape[2]
    colours = turned.shape[0]
    count = lax.axis_size("space")
    me = lax.axis_index("space")

    copies = []
    for m in range(held):
        source = slab_refs[m]
        if m < whole:
            source = source.at[:, pl.ds(first_colour, colours)]
        copies.append(
            pltpu.make_async_copy(source, slabs.at[m, :, :, pl.ds(0, PLANE), :], sems.at[2 * m])
        )
        copies.append(
            pltpu.make_async_copy(
                source.at[:, :, pl.ds(0, LX), :],
                slabs.at[m, :, :, pl.ds(PLANE, LX), :],
                sems.at[2 * m + 1],
            )
        )
    for copy in copies:
        copy.start()
    if late:
        acc[...] = prior_ref[...]
    else:
        acc[...] = jnp.zeros_like(acc)
    for copy in copies:
        copy.wait()

    row = lax.broadcasted_iota(jnp.int32, (PLANE, PLANE), 0)
    column = lax.broadcasted_iota(jnp.int32, (PLANE, PLANE), 1)
    wanted = jnp.where(row % LX == LX - 1, row - (LX - 1), row + 1)
    step_x = (column == wanted).astype(F32).astype(BF16)

    def one_slab(m, carry):
        here = me ^ m
        above = lax.rem(here + 1, count) ^ me
        far = above >= near

        @pl.when((m >= near) | far if late else m >= 0)
        def _():
            for colour in range(colours):
                for part in range(2):
                    block = slabs[m, part, colour, pl.ds(0, PLANE), :]
                    flat = block.T
                    same = flat if part == 0 else -flat
                    turned[colour, pl.ds(0, vectors), pl.ds(part * PLANE, PLANE)] = flat
                    turned[colour, pl.ds(vectors, vectors), pl.ds((1 - part) * PLANE, PLANE)] = same
                    moved = jnp.dot(step_x, block, preferred_element_type=F32)
                    slabs[held, part, colour, pl.ds(0, PLANE), :] = moved.astype(BF16)

            def one_operator(o, inner):
                move = move_ref[o]
                waits = (m >= near) | ((move == 3) & far)

                @pl.when(waits if late else jnp.logical_not(waits))
                def _():
                    src = jnp.where(move == 3, above, jnp.where(move == 1, held, m))
                    off = pl.multiple_of(jnp.where(move == 2, LX, 0), LX)
                    cos_z, sin_z = zphase_ref[0, here, o], zphase_ref[1, here, o]
                    for begin in range(0, PLANE, CHUNK):
                        cos_p = phase_ref[o, 0, pl.ds(begin, CHUNK), :]
                        sin_p = phase_ref[o, 1, pl.ds(begin, CHUNK), :]
                        cosine = cos_p * cos_z - sin_p * sin_z
                        sine = sin_p * cos_z + cos_p * sin_z
                        cosine = jnp.concatenate([cosine] * (vectors // LANES), axis=1)
                        sine = jnp.concatenate([sine] * (vectors // LANES), axis=1)
                        for colour in range(colours):
                            real = slabs[src, 0, colour, pl.ds(off + begin, CHUNK), :].astype(F32)
                            imag = slabs[src, 1, colour, pl.ds(off + begin, CHUNK), :].astype(F32)
                            mixed[colour, pl.ds(begin, CHUNK), :] = (
                                cosine * real + sine * imag
                            ).astype(BF16)
                            mixed[colour, pl.ds(PLANE + begin, CHUNK), :] = (
                                cosine * imag - sine * real
                            ).astype(BF16)
                    total = None
                    for colour in range(colours):
                        term = jnp.dot(turned[colour], mixed[colour], preferred_element_type=F32)
                        total = term if total is None else total + term
                    acc[o] += total

                return inner

            lax.fori_loop(0, operators, one_operator, 0)

        return carry

    lax.fori_loop(0, held, one_slab, 0)

    if last:
        block_rows = keep_ref.shape[2]
        first = pl.multiple_of(me * block_rows, block_rows)
        half = lax.rem(lax.axis_index("tm"), 2)
        for o in range(operators):
            full_ref[o] = acc[o].astype(BF16)
        for o in range(operators):
            for part in range(2):
                own = full_ref[o, pl.ds(part * vectors + first, block_rows), :]
                low, high = own[:, :LANES], own[:, LANES:]
                keep_ref[part, o] = jnp.where(half == 0, low, high)
                send_ref[part, o] = jnp.where(half == 0, high, low)
    else:
        out_ref[...] = acc[...]


def elementals(tables, slab_list, near, prior, last, colours, whole, first_colour, block_rows):
    _, _, plane, vectors = slab_list[0].shape
    held = len(slab_list)
    operators = tables[0].shape[0]
    late = prior is not None
    wide = jax.ShapeDtypeStruct((operators, 2 * vectors, vectors), F32)
    if last:
        piece = jax.ShapeDtypeStruct((2, operators, block_rows, LANES), BF16)
        outs = (jax.ShapeDtypeStruct(wide.shape, BF16), piece, piece)
        out_specs = (VMEM, VMEM, VMEM)
    else:
        outs, out_specs = wide, VMEM
    priors = [prior] if late else []
    return pl.pallas_call(
        functools.partial(elemental_kernel, held, near, late, last, whole, first_colour),
        out_shape=outs,
        in_specs=[SMEM, SMEM, VMEM] + [ANY] * held + [VMEM] * len(priors),
        out_specs=out_specs,
        scratch_shapes=[
            pltpu.VMEM((held + 1, 2, colours, plane + LX, vectors), BF16),
            pltpu.VMEM((colours, 2 * vectors, 2 * plane), BF16),
            pltpu.VMEM((colours, 2 * plane, vectors), BF16),
            pltpu.VMEM(wide.shape, F32),
            pltpu.SemaphoreType.DMA((2 * held,)),
        ],
        compiler_params=params(),
        cost_estimate=pl.CostEstimate(
            flops=8 * held * operators * colours * plane * vectors * vectors,
            bytes_accessed=held * 2 * colours * plane * vectors * 2,
            transcendentals=0,
        ),
        name="elementals_late" if late else "elementals_early",
    )(*tables, *slab_list, *priors)


def both_kernel(blocks, e_ref, *refs):
    peram_refs = refs[:blocks]
    keep_ref, send_ref, whole, left, middle, sems = refs[blocks:]
    sources, _, vectors, _ = whole.shape
    operators = e_ref.shape[0]
    block_rows = keep_ref.shape[3]
    me = lax.axis_index("space")
    half = lax.rem(lax.axis_index("tm"), 2)
    copies = []
    for m in range(blocks):
        begin = pl.multiple_of((me ^ m) * block_rows, block_rows)
        copies.append(
            pltpu.make_async_copy(
                peram_refs[m], whole.at[:, :, pl.ds(begin, block_rows), :], sems.at[m]
            )
        )
    for copy in copies:
        copy.start()
    for copy in copies:
        copy.wait()
    row = lax.broadcasted_iota(jnp.int32, (block_rows, vectors), 0)
    column = lax.broadcasted_iota(jnp.int32, (block_rows, vectors), 1)
    chosen = (column == row + me * block_rows).astype(F32).astype(BF16)
    for s in range(sources):
        for part in range(2):
            flat = lax.dot_general(
                chosen, whole[s, part], (((1,), (1,)), ((), ())), preferred_element_type=F32
            )
            left[pl.ds((part * sources + s) * block_rows, block_rows), :] = flat.astype(BF16)
    group = sources * block_rows
    for a in range(operators):
        product = lax.dot_general(
            left[...], e_ref[a], (((1,), (1,)), ((), ())), preferred_element_type=F32
        )
        real = product[:group, :vectors] - product[group:, vectors:]
        imaginary = product[:group, vectors:] + product[group:, :vectors]
        for part, block in enumerate((real, imaginary)):
            high = block.astype(BF16)
            low = (block - high.astype(F32)).astype(BF16)
            for s in range(sources):
                base = s * block_rows
                rows = pl.ds(a * block_rows, block_rows)
                columns = pl.ds(part * vectors, vectors)
                middle[0, s, rows, columns] = high[base : base + block_rows]
                middle[1, s, rows, columns] = low[base : base + block_rows]
    for s in range(sources):
        real, imaginary = whole[s, 0], whole[s, 1]
        right = jnp.concatenate(
            [
                jnp.concatenate([real, -imaginary], axis=1),
                jnp.concatenate([imaginary, real], axis=1),
            ],
            axis=0,
        )
        image = jnp.dot(middle[0, s], right, preferred_element_type=F32)
        image = image + jnp.dot(middle[1, s], right, preferred_element_type=F32)
        image = image.astype(BF16)
        for a in range(operators):
            for part in range(2):
                rows = image[a * block_rows : (a + 1) * block_rows]
                low = rows[:, part * vectors : part * vectors + LANES]
                high = rows[:, part * vectors + LANES : (part + 1) * vectors]
                keep_ref[s, part, a] = jnp.where(half == 0, low, high)
                send_ref[s, part, a] = jnp.where(half == 0, high, low)


def both_sides(elements, perams):
    blocks = len(perams)
    sources, _, block_rows, vectors = perams[0].shape
    operators = elements.shape[0]
    piece = jax.ShapeDtypeStruct((sources, 2, operators, block_rows, LANES), BF16)
    return pl.pallas_call(
        functools.partial(both_kernel, blocks),
        out_shape=(piece, piece),
        in_specs=[VMEM] + [ANY] * blocks,
        out_specs=(VMEM, VMEM),
        scratch_shapes=[
            pltpu.VMEM((sources, 2, vectors, vectors), BF16),
            pltpu.VMEM((2 * sources * block_rows, vectors), BF16),
            pltpu.VMEM((2, sources, operators * block_rows, 2 * vectors), BF16),
            pltpu.SemaphoreType.DMA((blocks,)),
        ],
        compiler_params=params(),
        cost_estimate=pl.CostEstimate(
            flops=2 * 3 * sources * operators * 4 * block_rows * vectors * vectors,
            bytes_accessed=8 * sources * vectors * vectors,
            transcendentals=0,
        ),
        name="both_sides",
    )(elements, *perams)


def spread(wide, count_rows, block_rows):
    pieces = [
        wide[pl.ds(k, count_rows, stride=block_rows), :].astype(BF16) for k in range(block_rows)
    ]
    return jnp.concatenate(pieces, axis=1)


def lay_kernel(own_ref, pair_ref, out_ref, wide):
    sources, _, operators, block_rows, lanes = own_ref.shape
    rows = 2 * operators
    for s in range(sources):
        for at, ref in enumerate((own_ref, pair_ref)):
            wide[pl.ds(at * rows * block_rows, rows * block_rows), :] = (
                ref[s].astype(F32).reshape(rows * block_rows, lanes)
            )
        out_ref[s] = spread(wide, 2 * rows, block_rows)


def lay_out(own, pair):
    sources, _, operators, block_rows, lanes = own.shape
    rows = 2 * operators
    return pl.pallas_call(
        lay_kernel,
        out_shape=jax.ShapeDtypeStruct((sources, 2 * rows, block_rows * lanes), BF16),
        in_specs=[VMEM, VMEM],
        out_specs=VMEM,
        scratch_shapes=[pltpu.VMEM((2 * rows * block_rows, lanes), F32)],
        compiler_params=params(),
        cost_estimate=pl.CostEstimate(
            flops=own.size, bytes_accessed=8 * own.size, transcendentals=0
        ),
        name="lay_out",
    )(own, pair)


def trace_kernel(offsets, times_ref, *refs):
    count = len(offsets)
    pools = refs[:count]
    laid_ref, mine_ref, pair_ref, picked, wide, sems = refs[count:]
    sources = laid_ref.shape[0]
    _, _, operators, block_rows, lanes = pools[0].shape
    rows = 2 * operators
    time = lax.axis_index("tm")
    for s in range(sources):
        source = times_ref[s]
        away = source // 2 - time // 2
        side = lax.rem(source + time, 2)
        for at, distance in enumerate(offsets):

            @pl.when(away == distance)
            def _(at=at, s=s, side=side):
                pltpu.make_async_copy(pools[at].at[side], picked.at[s], sems.at[s]).start()

    for s in range(sources):
        pltpu.make_async_copy(pools[0].at[0], picked.at[s], sems.at[s]).wait()
        wide[...] = picked[s].astype(F32).reshape(rows * block_rows, lanes)
        product = lax.dot_general(
            laid_ref[s],
            spread(wide, rows, block_rows),
            (((1,), (1,)), ((), ())),
            preferred_element_type=F32,
        )
        mine_ref[s] = product[:rows]
        pair_ref[s] = product[rows:]


def traces(source_times, offsets, pools, laid):
    sources = laid.shape[0]
    _, _, operators, block_rows, lanes = pools[0].shape
    rows = 2 * operators
    result = jax.ShapeDtypeStruct((sources, rows, rows), F32)
    return pl.pallas_call(
        functools.partial(trace_kernel, offsets),
        out_shape=(result, result),
        in_specs=[SMEM] + [ANY] * len(offsets) + [VMEM],
        out_specs=(VMEM, VMEM),
        scratch_shapes=[
            pltpu.VMEM((sources,) + pools[0].shape[1:], BF16),
            pltpu.VMEM((rows * block_rows, lanes), F32),
            pltpu.SemaphoreType.DMA((sources,)),
        ],
        compiler_params=params(),
        cost_estimate=pl.CostEstimate(
            flops=4 * sources * rows * rows * block_rows * lanes,
            bytes_accessed=2 * laid.size,
            transcendentals=0,
        ),
        name="traces",
    )(source_times, *pools, laid)


def finish_kernel(count, *refs):
    parts = refs[:count]
    correlator_ref, pairs_ref = refs[count:]
    sources, rows, _ = parts[0].shape
    n = rows // 2
    eye = lax.broadcasted_iota(jnp.int32, (n, n), 0) == lax.broadcasted_iota(jnp.int32, (n, n), 1)
    for s in range(sources):
        terms = [ref[s] for ref in parts]
        while len(terms) > 1:
            terms = [one + two for one, two in zip(terms[::2], terms[1::2])]
        total = terms[0]
        real = total[:n, :n] - total[n:, n:]
        imaginary = total[:n, n:] + total[n:, :n]
        correlator_ref[0, s, 0] = real
        correlator_ref[0, s, 1] = imaginary
        down_real, down_imaginary, over_real, over_imaginary = (
            jnp.sum(jnp.where(eye, block, 0.0), axis=axis, keepdims=True)
            for axis in (1, 0)
            for block in (real, imaginary)
        )
        pairs_ref[0, s, 0] = down_real * over_real - down_imaginary * over_imaginary
        pairs_ref[0, s, 1] = down_real * over_imaginary + down_imaginary * over_real


def finish(parts):
    sources, rows, _ = parts[0].shape
    result = jax.ShapeDtypeStruct((1, sources, 2, rows // 2, rows // 2), F32)
    return pl.pallas_call(
        functools.partial(finish_kernel, len(parts)),
        out_shape=(result, result),
        in_specs=[VMEM] * len(parts),
        out_specs=(VMEM, VMEM),
        compiler_params=params(),
        name="finish",
    )(*parts)


def phase_tables(momenta, z_coords, z_extent):
    plane = jnp.arange(PLANE, dtype=jnp.int32)
    along_x = (momenta[:, 0:1] * (plane % LX)[None] % LX).astype(F32) * (2.0 * math.pi / LX)
    along_y = (momenta[:, 1:2] * (plane // LX)[None] % LY).astype(F32) * (2.0 * math.pi / LY)
    angle = along_x + along_y
    table = jnp.stack([jnp.cos(angle), jnp.sin(angle)], axis=1)
    table = jnp.broadcast_to(table[..., None], table.shape + (LANES,))
    along_z = (momenta[:, 2][None, :] * z_coords[:, None] % z_extent).astype(F32) * (
        2.0 * math.pi / z_extent
    )
    return table, jnp.stack([jnp.cos(along_z), jnp.sin(along_z)])


def body(eigenvectors, momenta, displacement, source_times, perambulators):
    _, parts, colours, _, plane, vectors = eigenvectors.shape
    slabs = lax.axis_size("space")
    line = lax.axis_size("tm") // 2
    block_rows = vectors // slabs
    near = 2

    own = eigenvectors.reshape(parts, colours, plane, vectors)
    cut = colours - 1
    groups = [(0, cut), (cut, colours - cut)]
    far = [own[:, begin : begin + size] for begin, size in groups]
    held = [{0: block} for block in far]
    beside = swap_bit(own, "space", 1)
    mask = slabs // 2
    while mask >= near:
        for keys in held:
            for key in sorted(keys):
                keys[key | mask] = swap_bit(keys[key], "space", mask)
        mask //= 2

    plane_phase, z_phase = phase_tables(momenta, jnp.arange(slabs, dtype=jnp.int32), slabs)
    tables = (displacement, z_phase, plane_phase)
    total = elementals(tables, [own, beside], near, None, False, colours, near, 0, block_rows)

    for at, (begin, size) in enumerate(groups):
        last = at == len(groups) - 1
        keys = held[at]
        arrived = sorted(key for key in keys if key >= near)
        if at == 0:
            tied = lax.optimization_barrier(tuple(keys[key] for key in arrived) + (total,))
            keys.update(zip(arrived, tied))
            total = tied[-1]
        for key in arrived:
            keys[key | 1] = swap_bit(keys[key], "space", 1)
        slab_list = [own, beside] + [keys[key] for key in range(near, slabs)]
        total = elementals(tables, slab_list, near, total, last, size, near, begin, block_rows)
    full, keep, send = total

    peram, _ = lax.optimization_barrier((perambulators[0], held[-1][slabs // 2]))
    perams = gather_by_swaps(peram)

    received = swap_bit(send, "tm", 1)
    piece = jnp.stack([keep, received])
    offsets, pools = [0], [piece]
    for distance in range(1, line):
        for sign in (1, -1):
            offsets.append(-sign * distance)
            pools.append(along_line(piece, sign * distance, line))

    g_keep, g_send = both_sides(full, perams)
    laid = lay_out(g_keep, swap_bit(g_send, "tm", 1))
    mine, pair = traces(source_times, offsets, pools, laid)

    both = jnp.stack([mine, pair])
    both = both + swap_bit(both, "space", 1)
    mine, pair = both[0], both[1]
    sums = [mine]
    sums += [swap_bit(mine, "space", mask) for mask in range(2, slabs, 2)]
    sums += [swap_bit(pair, "tm", 1)]
    sums += [across(pair, mask) for mask in range(2, slabs, 2)]
    return finish(sums)


def across(block, mask):
    rows, times = lax.axis_size("space"), lax.axis_size("tm")
    route = [
        (i * times + t, (i ^ mask) * times + (t ^ 1)) for i in range(rows) for t in range(times)
    ]
    return lax.ppermute(block, ("space", "tm"), route)


def solution(mesh):
    placed = (
        P("tm", None, None, "space", None, None),
        P(),
        P(),
        P(),
        P("tm", None, None, "space", None),
    )
    return jax.shard_map(
        body,
        mesh=mesh,
        in_specs=placed,
        out_specs=(P("tm", None, None, None, None), P("tm", None, None, None, None)),
        check_vma=False,
    )
```

```python
import functools
import math

import jax
import jax.numpy as jnp
from jax import lax
from jax.experimental import pallas as pl
from jax.experimental.pallas import tpu as pltpu
from jax.sharding import PartitionSpec as P

LX = 16
LY = 16
PLANE = LX * LY
LANES = 128
F32 = jnp.float32
BF16 = jnp.bfloat16
CHUNK = 32
MEGA = 1024 * 1024

ANY = pl.BlockSpec(memory_space=pl.ANY)
SMEM = pl.BlockSpec(memory_space=pltpu.SMEM)
VMEM = pl.BlockSpec(memory_space=pltpu.VMEM)


def swap_bit(block, axis, mask):
    count = lax.axis_size(axis)
    return lax.ppermute(block, axis, [(i, i ^ mask) for i in range(count)])


def along_line(block, moves):
    route = [(2 * z + x, 2 * to + x) for z, to in moves.items() for x in range(2)]
    return lax.ppermute(block, "tm", route)


def share_line(keep, received, line):
    piece = jnp.stack([keep, received])
    if line != 4:
        arrays, table = [keep, received], {0: (0, None), 1: (1, None)}
        for distance in range(1, line):
            moved = along_line(piece, {z: (z + distance) % line for z in range(line)})
            for side in range(2):
                table[2 * distance + side] = (len(arrays), side)
            arrays.append(moved)
        return arrays, table
    between = along_line(piece, {1: 2, 2: 1})
    far = along_line(piece, {0: 3, 3: 0})
    skip = along_line(piece, {0: 2, 3: 1})
    near = along_line(piece, {0: 1, 1: 0, 2: 3, 3: 2})
    passed = along_line(between, {1: 0, 2: 3})
    arrays = [keep, received, near, skip, between, passed, far]
    table = {0: (0, None), 1: (1, None)}
    for code in range(2, 12):
        table[code] = (1 + code // 2, code % 2)
    return arrays, table


def line_code(here, there, side, line):
    if line != 4:
        return 2 * lax.rem(here - there + line, line) + side
    apart = here ^ there
    ends = (here == 0) | (here == line - 1)
    return 2 * jnp.where(ends & (apart >= 2), apart + 2, apart) + side


def swap_far(block):
    held = {0: block}
    mask = lax.axis_size("space") // 2
    while mask >= 2:
        for key in sorted(held):
            held[key | mask] = swap_bit(held[key], "space", mask)
        mask //= 2
    return held


def swap_near(held):
    both = dict(held)
    for key in sorted(held):
        both[key | 1] = swap_bit(held[key], "space", 1)
    return [both[key] for key in sorted(both)]


def params(megabytes):
    return pltpu.CompilerParams(vmem_limit_bytes=megabytes * MEGA)


def elemental_kernel(held, near, late, *refs):
    move_ref, zphase_ref, phase_ref = refs[:3]
    slab_refs = refs[3 : 3 + held]
    rest = refs[3 + held :]
    if late:
        prior_ref, acc_out, keep_ref, send_ref, slabs, turned, mixed, table, acc, before, sems = rest
    else:
        acc, slabs, turned, mixed, table, sems = rest
    operators, _, vectors = acc.shape
    colours = turned.shape[0]
    count = lax.axis_size("space")
    me = lax.axis_index("space")

    def arriving(m):
        return (
            pltpu.make_async_copy(
                slab_refs[m], slabs.at[m, :, :, pl.ds(0, PLANE), :], sems.at[2 * m]
            ),
            pltpu.make_async_copy(
                slab_refs[m].at[:, :, pl.ds(0, LX), :],
                slabs.at[m, :, :, pl.ds(PLANE, LX), :],
                sems.at[2 * m + 1],
            ),
        )

    for m in reversed(range(held)):
        for copy in arriving(m):
            copy.start()
    if late:
        prior = pltpu.make_async_copy(prior_ref, before, sems.at[2 * held])
        prior.start()
    acc[...] = jnp.zeros_like(acc)
    upright = phase_ref[...].T
    for o in range(operators):
        for part in range(2):
            at = 2 * o + part
            table[o, part] = jnp.broadcast_to(upright[:, at : at + 1], (PLANE, LANES))
    for m in range(held):
        for copy in arriving(m):
            copy.wait()

    def one_slab(m, carry):
        here = me ^ m
        above = lax.rem(here + 1, count) ^ me
        far = above >= near

        @pl.when((m >= near) | far if late else m >= 0)
        def _():
            for colour in range(colours):
                for part in range(2):
                    block = slabs[m, part, colour, pl.ds(0, PLANE), :]
                    flat = block.T
                    same = flat if part == 0 else -flat
                    turned[colour, pl.ds(0, vectors), pl.ds(part * PLANE, PLANE)] = flat
                    turned[colour, pl.ds(vectors, vectors), pl.ds((1 - part) * PLANE, PLANE)] = same
                    for begin in range(0, PLANE, CHUNK):
                        rows = slabs[m, part, colour, pl.ds(begin, CHUNK), :].astype(F32)
                        rows = pltpu.roll(rows.reshape(CHUNK // LX, LX, vectors), LX - 1, 1)
                        slabs[held, part, colour, pl.ds(begin, CHUNK), :] = rows.reshape(
                            CHUNK, vectors
                        ).astype(BF16)

            def one_operator(o, inner):
                move = move_ref[o]
                waits = (m >= near) | ((move == 3) & far)

                @pl.when(waits if late else jnp.logical_not(waits))
                def _():
                    src = jnp.where(move == 3, above, jnp.where(move == 1, held, m))
                    off = pl.multiple_of(jnp.where(move == 2, LX, 0), LX)
                    cos_z, sin_z = zphase_ref[0, here, o], zphase_ref[1, here, o]
                    for begin in range(0, PLANE, CHUNK):
                        cos_p = table[o, 0, pl.ds(begin, CHUNK), :]
                        sin_p = table[o, 1, pl.ds(begin, CHUNK), :]
                        cosine = cos_p * cos_z - sin_p * sin_z
                        sine = sin_p * cos_z + cos_p * sin_z
                        cosine = jnp.concatenate([cosine] * (vectors // LANES), axis=1)
                        sine = jnp.concatenate([sine] * (vectors // LANES), axis=1)
                        for colour in range(colours):
                            real = slabs[src, 0, colour, pl.ds(off + begin, CHUNK), :].astype(F32)
                            imag = slabs[src, 1, colour, pl.ds(off + begin, CHUNK), :].astype(F32)
                            mixed[colour, pl.ds(begin, CHUNK), :] = (
                                cosine * real + sine * imag
                            ).astype(BF16)
                            mixed[colour, pl.ds(PLANE + begin, CHUNK), :] = (
                                cosine * imag - sine * real
                            ).astype(BF16)
                    total = None
                    for colour in range(colours):
                        term = jnp.dot(turned[colour], mixed[colour], preferred_element_type=F32)
                        total = term if total is None else total + term
                    acc[o] += total

                return inner

            lax.fori_loop(0, operators, one_operator, 0)

        return carry

    lax.fori_loop(0, held, one_slab, 0)

    if late:
        block_rows = keep_ref.shape[2]
        first = pl.multiple_of(me * block_rows, block_rows)
        half = lax.rem(lax.axis_index("tm"), 2)
        prior.wait()
        for o in range(operators):
            acc_out[o] = (acc[o] + before[o]).astype(BF16)
            for part in range(2):
                rows = pl.ds(part * vectors + first, block_rows)
                own = (acc[o, rows, :] + before[o, rows, :]).astype(BF16)
                low, high = own[:, :LANES], own[:, LANES:]
                keep_ref[part, o] = jnp.where(half == 0, low, high)
                send_ref[part, o] = jnp.where(half == 0, high, low)


def elementals(tables, slab_list, near, prior, block_rows):
    _, colours, plane, vectors = slab_list[0].shape
    held = len(slab_list)
    operators = tables[0].shape[0]
    late = prior is not None
    wide = jax.ShapeDtypeStruct((operators, 2 * vectors, vectors), F32)
    scratch = [
        pltpu.VMEM((held + 1, 2, colours, plane + LX, vectors), BF16),
        pltpu.VMEM((colours, 2 * vectors, 2 * plane), BF16),
        pltpu.VMEM((colours, 2 * plane, vectors), BF16),
        pltpu.VMEM((operators, 2, plane, LANES), F32),
    ]
    if late:
        piece = jax.ShapeDtypeStruct((2, operators, block_rows, LANES), BF16)
        outs = (jax.ShapeDtypeStruct(wide.shape, BF16), piece, piece)
        out_specs = (VMEM, VMEM, VMEM)
        scratch += [pltpu.VMEM(wide.shape, F32)] * 2
    else:
        outs, out_specs = wide, VMEM
    priors = [prior] if late else []
    return pl.pallas_call(
        functools.partial(elemental_kernel, held, near, late),
        out_shape=outs,
        in_specs=[SMEM, SMEM, VMEM] + [ANY] * (held + len(priors)),
        out_specs=out_specs,
        scratch_shapes=scratch + [pltpu.SemaphoreType.DMA((2 * held + 1,))],
        compiler_params=params(20 + held),
        cost_estimate=pl.CostEstimate(
            flops=8 * held * operators * colours * plane * vectors * vectors,
            bytes_accessed=held * 2 * colours * plane * vectors * 2,
            transcendentals=0,
        ),
        name="elementals_late" if late else "elementals_early",
    )(*tables, *slab_list, *priors)


def both_kernel(blocks, e_ref, *refs):
    peram_refs = refs[:blocks]
    keep_ref, send_ref, whole, left, middle, sems = refs[blocks:]
    sources, _, vectors, _ = whole.shape
    operators = e_ref.shape[0]
    block_rows = keep_ref.shape[3]
    me = lax.axis_index("space")
    half = lax.rem(lax.axis_index("tm"), 2)
    copies = []
    for m in range(blocks):
        begin = pl.multiple_of((me ^ m) * block_rows, block_rows)
        copies.append(
            pltpu.make_async_copy(
                peram_refs[m], whole.at[:, :, pl.ds(begin, block_rows), :], sems.at[m]
            )
        )
    for copy in copies:
        copy.start()
    for copy in copies:
        copy.wait()
    row = lax.broadcasted_iota(jnp.int32, (block_rows, vectors), 0)
    column = lax.broadcasted_iota(jnp.int32, (block_rows, vectors), 1)
    chosen = (column == row + me * block_rows).astype(F32).astype(BF16)
    for s in range(sources):
        for part in range(2):
            flat = lax.dot_general(
                chosen, whole[s, part], (((1,), (1,)), ((), ())), preferred_element_type=F32
            )
            left[pl.ds((part * sources + s) * block_rows, block_rows), :] = flat.astype(BF16)
    group = sources * block_rows
    for a in range(operators):
        product = lax.dot_general(
            left[...], e_ref[a], (((1,), (1,)), ((), ())), preferred_element_type=F32
        )
        real = product[:group, :vectors] - product[group:, vectors:]
        imaginary = product[:group, vectors:] + product[group:, :vectors]
        for part, block in enumerate((real, imaginary)):
            high = block.astype(BF16)
            low = (block - high.astype(F32)).astype(BF16)
            for s in range(sources):
                base = s * block_rows
                rows = pl.ds(a * block_rows, block_rows)
                columns = pl.ds(part * vectors, vectors)
                middle[0, s, rows, columns] = high[base : base + block_rows]
                middle[1, s, rows, columns] = low[base : base + block_rows]
    for s in range(sources):
        real, imaginary = whole[s, 0], whole[s, 1]
        right = jnp.concatenate(
            [
                jnp.concatenate([real, -imaginary], axis=1),
                jnp.concatenate([imaginary, real], axis=1),
            ],
            axis=0,
        )
        image = jnp.dot(middle[0, s], right, preferred_element_type=F32)
        image = image + jnp.dot(middle[1, s], right, preferred_element_type=F32)
        image = image.astype(BF16)
        for a in range(operators):
            for part in range(2):
                rows = image[a * block_rows : (a + 1) * block_rows]
                low = rows[:, part * vectors : part * vectors + LANES]
                high = rows[:, part * vectors + LANES : (part + 1) * vectors]
                keep_ref[s, part, a] = jnp.where(half == 0, low, high)
                send_ref[s, part, a] = jnp.where(half == 0, high, low)


def both_sides(elements, perams):
    blocks = len(perams)
    sources, _, block_rows, vectors = perams[0].shape
    operators = elements.shape[0]
    piece = jax.ShapeDtypeStruct((sources, 2, operators, block_rows, LANES), BF16)
    return pl.pallas_call(
        functools.partial(both_kernel, blocks),
        out_shape=(piece, piece),
        in_specs=[VMEM] + [ANY] * blocks,
        out_specs=(VMEM, VMEM),
        scratch_shapes=[
            pltpu.VMEM((sources, 2, vectors, vectors), BF16),
            pltpu.VMEM((2 * sources * block_rows, vectors), BF16),
            pltpu.VMEM((2, sources, operators * block_rows, 2 * vectors), BF16),
            pltpu.SemaphoreType.DMA((blocks,)),
        ],
        compiler_params=params(16),
        cost_estimate=pl.CostEstimate(flops=0, bytes_accessed=0, transcendentals=0),
        name="both_sides",
    )(elements, *perams)


def spread(wide, count_rows, block_rows):
    pieces = [
        wide[pl.ds(k, count_rows, stride=block_rows), :].astype(BF16) for k in range(block_rows)
    ]
    return jnp.concatenate(pieces, axis=1)


def lay_kernel(own_ref, pair_ref, out_ref, wide):
    sources, _, operators, block_rows, lanes = own_ref.shape
    rows = 2 * operators
    for s in range(sources):
        for at, ref in enumerate((own_ref, pair_ref)):
            wide[pl.ds(at * rows * block_rows, rows * block_rows), :] = (
                ref[s].astype(F32).reshape(rows * block_rows, lanes)
            )
        out_ref[s] = spread(wide, 2 * rows, block_rows)


def lay_out(own, pair):
    sources, _, operators, block_rows, lanes = own.shape
    rows = 2 * operators
    return pl.pallas_call(
        lay_kernel,
        out_shape=jax.ShapeDtypeStruct((sources, 2 * rows, block_rows * lanes), BF16),
        in_specs=[VMEM, VMEM],
        out_specs=VMEM,
        scratch_shapes=[pltpu.VMEM((2 * rows * block_rows, lanes), F32)],
        compiler_params=params(12),
        cost_estimate=pl.CostEstimate(flops=0, bytes_accessed=0, transcendentals=0),
        name="lay_out",
    )(own, pair)


def trace_kernel(count, table, line, times_ref, *refs):
    pools = refs[:count]
    laid_ref, out_ref, picked, wide, sems = refs[count:]
    sources = laid_ref.shape[0]
    _, operators, block_rows, lanes = pools[0].shape
    rows = 2 * operators
    time = lax.axis_index("tm")
    for s in range(sources):
        source = times_ref[s]
        code = line_code(time // 2, source // 2, lax.rem(source + time, 2), line)
        for index, (at, inside) in table.items():

            @pl.when(code == index)
            def _(at=at, inside=inside, s=s):
                block = pools[at] if inside is None else pools[at].at[inside]
                pltpu.make_async_copy(block, picked.at[s], sems.at[s]).start()

    for s in range(sources):
        pltpu.make_async_copy(pools[0], picked.at[s], sems.at[s]).wait()
        wide[...] = picked[s].astype(F32).reshape(rows * block_rows, lanes)
        product = lax.dot_general(
            laid_ref[s],
            spread(wide, rows, block_rows),
            (((1,), (1,)), ((), ())),
            preferred_element_type=F32,
        )
        out_ref[0, s] = product[:rows]
        out_ref[1, s] = product[rows:]


def traces(source_times, pools, table, line, laid):
    sources = laid.shape[0]
    _, operators, block_rows, lanes = pools[0].shape
    rows = 2 * operators
    return pl.pallas_call(
        functools.partial(trace_kernel, len(pools), table, line),
        out_shape=jax.ShapeDtypeStruct((2, sources, rows, rows), F32),
        in_specs=[SMEM] + [ANY] * len(pools) + [VMEM],
        out_specs=VMEM,
        scratch_shapes=[
            pltpu.VMEM((sources,) + pools[0].shape, BF16),
            pltpu.VMEM((rows * block_rows, lanes), F32),
            pltpu.SemaphoreType.DMA((sources,)),
        ],
        compiler_params=params(12),
        cost_estimate=pl.CostEstimate(
            flops=4 * sources * rows * rows * block_rows * lanes,
            bytes_accessed=2 * laid.size,
            transcendentals=0,
        ),
        name="traces",
    )(source_times, *pools, laid)


def finish_kernel(count, *refs):
    parts = refs[:count]
    correlator_ref, pairs_ref = refs[count:]
    sources, rows, _ = parts[1].shape
    n = rows // 2
    eye = lax.broadcasted_iota(jnp.int32, (n, n), 0) == lax.broadcasted_iota(jnp.int32, (n, n), 1)
    for s in range(sources):
        terms = [parts[0][0, s]] + [ref[s] for ref in parts[1:]]
        while len(terms) > 1:
            terms = [one + two for one, two in zip(terms[::2], terms[1::2])]
        total = terms[0]
        real = total[:n, :n] - total[n:, n:]
        imaginary = total[:n, n:] + total[n:, :n]
        correlator_ref[0, s, :, 0, :] = real
        correlator_ref[0, s, :, 1, :] = imaginary
        down_real, down_imaginary, over_real, over_imaginary = (
            jnp.sum(jnp.where(eye, block, 0.0), axis=axis, keepdims=True)
            for axis in (1, 0)
            for block in (real, imaginary)
        )
        pairs_ref[0, s, :, 0, :] = down_real * over_real - down_imaginary * over_imaginary
        pairs_ref[0, s, :, 1, :] = down_real * over_imaginary + down_imaginary * over_real


def finish(parts):
    sources, rows, _ = parts[1].shape
    result = jax.ShapeDtypeStruct((1, sources, rows // 2, 2, rows // 2), F32)
    correlator, pairs = pl.pallas_call(
        functools.partial(finish_kernel, len(parts)),
        out_shape=(result, result),
        in_specs=[VMEM] * len(parts),
        out_specs=(VMEM, VMEM),
        compiler_params=params(4),
        name="finish",
    )(*parts)
    return jnp.swapaxes(correlator, 2, 3), jnp.swapaxes(pairs, 2, 3)


def phase_tables(momenta, z_coords, z_extent):
    plane = jnp.arange(PLANE, dtype=jnp.int32)
    along_x = (momenta[:, 0:1] * (plane % LX)[None] % LX).astype(F32) * (2.0 * math.pi / LX)
    along_y = (momenta[:, 1:2] * (plane // LX)[None] % LY).astype(F32) * (2.0 * math.pi / LY)
    angle = along_x + along_y
    table = jnp.stack([jnp.cos(angle), jnp.sin(angle)], axis=1).reshape(-1, PLANE)
    along_z = (momenta[:, 2][None, :] * z_coords[:, None] % z_extent).astype(F32) * (
        2.0 * math.pi / z_extent
    )
    return table, jnp.stack([jnp.cos(along_z), jnp.sin(along_z)])


def body(eigenvectors, momenta, displacement, source_times, perambulators):
    _, parts, colours, _, plane, vectors = eigenvectors.shape
    slabs = lax.axis_size("space")
    line = lax.axis_size("tm") // 2
    block_rows = vectors // slabs
    near = 2

    own = eigenvectors.reshape(parts, colours, plane, vectors)
    beside = swap_bit(own, "space", 1)
    keys = swap_far(own)

    plane_phase, z_phase = phase_tables(momenta, jnp.arange(slabs, dtype=jnp.int32), slabs)
    tables = (displacement, z_phase, plane_phase)
    total = elementals(tables, [own, beside], near, None, block_rows)

    keys, total = lax.optimization_barrier((keys, total))
    slab_list = swap_near(keys)
    slab_list[1] = beside
    peram, _ = lax.optimization_barrier((perambulators[0], keys[slabs // 2]))
    perams = swap_far(peram)
    full, keep, send = elementals(tables, slab_list, near, total, block_rows)

    perams = swap_near(lax.optimization_barrier((perams, full))[0])

    received = swap_bit(send, "tm", 1)
    g_keep, g_send = both_sides(full, perams)
    g_send, received = lax.optimization_barrier((g_send, received))
    arrays, table = share_line(keep, received, line)
    laid = lay_out(g_keep, swap_bit(g_send, "tm", 1))
    both = traces(source_times, arrays, table, line, laid)
    both = both + swap_bit(both, "space", 1)
    mine, pair = both[0], both[1]
    near_sums = [swap_bit(mine, "space", mask) for mask in range(2, slabs, 2)]
    pair_sums = [swap_bit(pair, "tm", 1)]
    pair_sums += [across(pair, mask) for mask in range(2, slabs, 2)]
    return finish([both] + near_sums + pair_sums)


def across(block, mask):
    rows, times = lax.axis_size("space"), lax.axis_size("tm")
    route = [
        (i * times + t, (i ^ mask) * times + (t ^ 1)) for i in range(rows) for t in range(times)
    ]
    return lax.ppermute(block, ("space", "tm"), route)


def solution(mesh):
    placed = (
        P("tm", None, None, "space", None, None),
        P(),
        P(),
        P(),
        P("tm", None, None, "space", None),
    )
    return jax.shard_map(
        body,
        mesh=mesh,
        in_specs=placed,
        out_specs=(P("tm", None, None, None, None), P("tm", None, None, None, None)),
        check_vma=False,
    )
```

```python
import functools
import math

import jax
import jax.numpy as jnp
from jax import lax
from jax.experimental import pallas as pl
from jax.experimental.pallas import tpu as pltpu
from jax.sharding import PartitionSpec as P

LX = 16
LY = 16
PLANE = LX * LY
LANES = 128
F32 = jnp.float32
BF16 = jnp.bfloat16
CHUNK = 32
FOLD = 8
MEGA = 1024 * 1024

ANY = pl.BlockSpec(memory_space=pl.ANY)
SMEM = pl.BlockSpec(memory_space=pltpu.SMEM)
VMEM = pl.BlockSpec(memory_space=pltpu.VMEM)


def swap_bit(block, axis, mask):
    count = lax.axis_size(axis)
    return lax.ppermute(block, axis, [(i, i ^ mask) for i in range(count)])


def along_line(block, moves):
    route = [(2 * z + x, 2 * to + x) for z, to in moves.items() for x in range(2)]
    return lax.ppermute(block, "tm", route)


def share_line(keep, received, g_send, line):
    piece = jnp.stack([keep, received])
    if line != 4:
        arrays, table = [keep, received], {0: (0, None), 1: (1, None)}
        for distance in range(1, line):
            moved = along_line(piece, {z: (z + distance) % line for z in range(line)})
            for side in range(2):
                table[2 * distance + side] = (len(arrays), side)
            arrays.append(moved)
        return arrays, table, g_send
    outward = {1: 0, 2: 3}
    received, g_send = lax.optimization_barrier((received, g_send))
    piece = jnp.stack([keep, received])
    opposite = along_line(piece, {1: 2, 2: 1, 0: 3, 3: 0})
    skip = along_line(piece, {0: 2, 3: 1})
    near = along_line(piece, {0: 1, 1: 0, 2: 3, 3: 2})
    passed = along_line(opposite, outward)
    arrays = [keep, received, near, skip, opposite, passed]
    table = {0: (0, None), 1: (1, None)}
    for code in range(2, 10):
        table[code] = (1 + code // 2, code % 2)
    return arrays, table, g_send


def line_code(here, there, side, line):
    if line != 4:
        return 2 * lax.rem(here - there + line, line) + side
    apart = here ^ there
    ends = (here == 0) | (here == line - 1)
    return 2 * jnp.where(ends & (apart == 2), 4, apart) + side


def swap_far(block):
    held = {0: block}
    mask = lax.axis_size("space") // 2
    while mask >= 2:
        for key in sorted(held):
            held[key | mask] = swap_bit(held[key], "space", mask)
        mask //= 2
    return held


def swap_near(held):
    both = dict(held)
    for key in sorted(held):
        both[key | 1] = swap_bit(held[key], "space", 1)
    return [both[key] for key in sorted(both)]


def params(megabytes):
    return pltpu.CompilerParams(vmem_limit_bytes=megabytes * MEGA)


def elemental_kernel(held, near, late, block_rows, *refs):
    move_ref, zphase_ref, phase_ref = refs[:3]
    slab_refs = refs[3 : 3 + held]
    rest = refs[3 + held :]
    if late:
        prior_ref, acc_out, keep_ref, send_ref, slabs, turned, mixed, table, acc, before, sems = rest
    else:
        acc, slabs, turned, mixed, table, sems = rest
    operators, half_rows, vectors = acc.shape
    half_rows //= 2
    colours = turned.shape[0]
    count = lax.axis_size("space")
    me = lax.axis_index("space")
    core = lax.rem(me, 2)

    def arriving(m):
        return (
            pltpu.make_async_copy(
                slab_refs[m], slabs.at[m, :, :, pl.ds(0, PLANE), :], sems.at[2 * m]
            ),
            pltpu.make_async_copy(
                slab_refs[m].at[:, :, pl.ds(0, LX), :],
                slabs.at[m, :, :, pl.ds(PLANE, LX), :],
                sems.at[2 * m + 1],
            ),
        )

    order = list(range(near, held)) + list(range(min(near, held)))
    for m in order:
        for copy in arriving(m):
            copy.start()
    if late:
        prior = pltpu.make_async_copy(prior_ref, before, sems.at[2 * held])
        prior.start()
    acc[...] = jnp.zeros_like(acc)
    upright = phase_ref[...].T
    for o in range(operators):
        for part in range(2):
            at = 2 * o + part
            table[o, part] = jnp.broadcast_to(upright[:, at : at + 1], (PLANE, LANES))
    first_slab = order[0]
    for copy in arriving(first_slab):
        copy.wait()

    def one_slab(step, carry):
        m = lax.rem(step + first_slab, held)
        here = me ^ m
        above = lax.rem(here + 1, count) ^ me
        far = above >= near

        def wait_others():
            for other in order[1:]:
                for copy in arriving(other):
                    copy.wait()

        def one_operator(o, inner):
            move = move_ref[o]
            waits = (m >= near) | ((move == 3) & far)

            @pl.when((waits if late else jnp.logical_not(waits)) & ((move == 3) == inner))
            def _():
                src = jnp.where(move == 3, above, jnp.where(move == 1, held, m))
                off = pl.multiple_of(jnp.where(move == 2, LX, 0), LX)
                cos_z, sin_z = zphase_ref[0, here, o], zphase_ref[1, here, o]
                total = None
                for colour in range(colours):
                    for begin in range(0, PLANE, CHUNK):
                        cos_p = table[o, 0, pl.ds(begin, CHUNK), :]
                        sin_p = table[o, 1, pl.ds(begin, CHUNK), :]
                        cosine = cos_p * cos_z - sin_p * sin_z
                        sine = sin_p * cos_z + cos_p * sin_z
                        cosine = jnp.concatenate([cosine] * (vectors // LANES), axis=1)
                        sine = jnp.concatenate([sine] * (vectors // LANES), axis=1)
                        real = slabs[src, 0, colour, pl.ds(off + begin, CHUNK), :].astype(F32)
                        imag = slabs[src, 1, colour, pl.ds(off + begin, CHUNK), :].astype(F32)
                        mixed[colour, pl.ds(begin, CHUNK), :] = (
                            cosine * real + sine * imag
                        ).astype(BF16)
                        mixed[colour, pl.ds(PLANE + begin, CHUNK), :] = (
                            cosine * imag - sine * real
                        ).astype(BF16)
                    term = jnp.dot(turned[colour], mixed[colour], preferred_element_type=F32)
                    total = term if total is None else total + term
                acc[o] += total

            return inner

        @pl.when((m >= near) | far if late else m >= 0)
        def _():
            for colour in range(colours):
                for part in range(2):
                    block = slabs[m, part, colour, pl.ds(0, PLANE), :]
                    flat = block.T.reshape(half_rows // block_rows, 2, block_rows, PLANE)
                    flat = jnp.where(core == 0, flat[:, 0], flat[:, 1]).reshape(half_rows, PLANE)
                    same = flat if part == 0 else -flat
                    lower = pl.ds(half_rows, half_rows)
                    turned[colour, pl.ds(0, half_rows), pl.ds(part * PLANE, PLANE)] = flat
                    turned[colour, lower, pl.ds((1 - part) * PLANE, PLANE)] = same
                    for begin in range(0, PLANE, CHUNK):
                        rows = slabs[m, part, colour, pl.ds(begin, CHUNK), :].astype(F32)
                        rows = pltpu.roll(rows.reshape(CHUNK // LX, LX, vectors), LX - 1, 1)
                        slabs[held, part, colour, pl.ds(begin, CHUNK), :] = rows.reshape(
                            CHUNK, vectors
                        ).astype(BF16)
            lax.fori_loop(0, operators, one_operator, False)

        @pl.when(step == 0)
        def _():
            wait_others()

        @pl.when((m >= near) | far if late else m >= 0)
        def _():
            lax.fori_loop(0, operators, one_operator, True)

        return carry

    lax.fori_loop(0, held, one_slab, 0)

    if late:
        first = pl.multiple_of(me // 2 * block_rows, block_rows)
        half = lax.rem(lax.axis_index("tm"), 2)
        prior.wait()
        for o in range(operators):
            acc_out[o] = (acc[o] + before[o]).astype(BF16)
            for part in range(2):
                rows = pl.ds(part * half_rows + first, block_rows)
                own = (acc[o, rows, :] + before[o, rows, :]).astype(BF16)
                low, high = own[:, :LANES], own[:, LANES:]
                keep_ref[part, o] = jnp.where(half == 0, low, high)
                send_ref[part, o] = jnp.where(half == 0, high, low)


def elementals(tables, slab_list, near, prior, block_rows):
    _, colours, plane, vectors = slab_list[0].shape
    held = len(slab_list)
    operators = tables[0].shape[0]
    late = prior is not None
    wide = jax.ShapeDtypeStruct((operators, vectors, vectors), F32)
    scratch = [
        pltpu.VMEM((held + 1, 2, colours, plane + LX, vectors), BF16),
        pltpu.VMEM((colours, vectors, 2 * plane), BF16),
        pltpu.VMEM((colours, 2 * plane, vectors), BF16),
        pltpu.VMEM((operators, 2, plane, LANES), F32),
    ]
    if late:
        piece = jax.ShapeDtypeStruct((2, operators, block_rows, LANES), BF16)
        outs = (jax.ShapeDtypeStruct(wide.shape, BF16), piece, piece)
        out_specs = (VMEM, VMEM, VMEM)
        scratch += [pltpu.VMEM(wide.shape, F32)] * 2
    else:
        outs, out_specs = wide, VMEM
    priors = [prior] if late else []
    return pl.pallas_call(
        functools.partial(elemental_kernel, held, near, late, block_rows),
        out_shape=outs,
        in_specs=[SMEM, SMEM, VMEM] + [ANY] * (held + len(priors)),
        out_specs=out_specs,
        scratch_shapes=scratch + [pltpu.SemaphoreType.DMA((2 * held + 1,))],
        compiler_params=params(20 + held),
        cost_estimate=pl.CostEstimate(
            flops=8 * held * operators * colours * plane * vectors * vectors,
            bytes_accessed=held * 2 * colours * plane * vectors * 2,
            transcendentals=0,
        ),
        name="elementals_late" if late else "elementals_early",
    )(*tables, *slab_list, *priors)


def both_kernel(blocks, e_ref, other_ref, *refs):
    peram_refs = refs[:blocks]
    keep_ref, send_ref, whole, sorted_rows, left, middle, sems = refs[blocks:]
    sources, _, vectors, _ = whole.shape
    operators = e_ref.shape[0]
    block_rows = keep_ref.shape[3]
    me = lax.axis_index("space")
    half = lax.rem(lax.axis_index("tm"), 2)
    copies = []
    for m in range(blocks):
        begin = pl.multiple_of((me ^ m) * block_rows, block_rows)
        copies.append(
            pltpu.make_async_copy(
                peram_refs[m], whole.at[:, :, pl.ds(begin, block_rows), :], sems.at[2 * m]
            )
        )
        begin = (m % 2) * (vectors // 2) + (me ^ m) // 2 * block_rows
        begin = pl.multiple_of(begin, block_rows)
        copies.append(
            pltpu.make_async_copy(
                peram_refs[m], sorted_rows.at[:, :, pl.ds(begin, block_rows), :], sems.at[2 * m + 1]
            )
        )
    for copy in copies:
        copy.start()
    for copy in copies:
        copy.wait()
    row = lax.broadcasted_iota(jnp.int32, (block_rows, vectors), 0)
    column = lax.broadcasted_iota(jnp.int32, (block_rows, vectors), 1)
    chosen = (column == row + me * block_rows).astype(F32).astype(BF16)
    for s in range(sources):
        for part in range(2):
            flat = lax.dot_general(
                chosen, whole[s, part], (((1,), (1,)), ((), ())), preferred_element_type=F32
            )
            left[pl.ds((part * sources + s) * block_rows, block_rows), :] = flat.astype(BF16)
    group = sources * block_rows
    cut = vectors // 2
    for a in range(operators):
        sides = []
        for ref in (e_ref, other_ref):
            product = lax.dot_general(
                left[...], ref[a], (((1,), (1,)), ((), ())), preferred_element_type=F32
            )
            sides.append(
                (
                    product[:group, :cut] - product[group:, cut:],
                    product[:group, cut:] + product[group:, :cut],
                )
            )
        real, imaginary = (
            jnp.concatenate([one, two], axis=1) for one, two in zip(*sides)
        )
        for part, block in enumerate((real, imaginary)):
            high = block.astype(BF16)
            low = (block - high.astype(F32)).astype(BF16)
            for s in range(sources):
                base = s * block_rows
                rows = pl.ds(a * block_rows, block_rows)
                columns = pl.ds(part * vectors, vectors)
                middle[0, s, rows, columns] = high[base : base + block_rows]
                middle[1, s, rows, columns] = low[base : base + block_rows]
    for s in range(sources):
        real, imaginary = sorted_rows[s, 0], sorted_rows[s, 1]
        right = jnp.concatenate(
            [
                jnp.concatenate([real, -imaginary], axis=1),
                jnp.concatenate([imaginary, real], axis=1),
            ],
            axis=0,
        )
        image = jnp.dot(middle[0, s], right, preferred_element_type=F32)
        image = image + jnp.dot(middle[1, s], right, preferred_element_type=F32)
        image = image.astype(BF16)
        for a in range(operators):
            for part in range(2):
                rows = image[a * block_rows : (a + 1) * block_rows]
                low = rows[:, part * vectors : part * vectors + LANES]
                high = rows[:, part * vectors + LANES : (part + 1) * vectors]
                keep_ref[s, part, a] = jnp.where(half == 0, low, high)
                send_ref[s, part, a] = jnp.where(half == 0, high, low)


def both_sides(elements, others, perams):
    blocks = len(perams)
    sources, _, block_rows, vectors = perams[0].shape
    operators = elements.shape[0]
    piece = jax.ShapeDtypeStruct((sources, 2, operators, block_rows, LANES), BF16)
    return pl.pallas_call(
        functools.partial(both_kernel, blocks),
        out_shape=(piece, piece),
        in_specs=[VMEM, VMEM] + [ANY] * blocks,
        out_specs=(VMEM, VMEM),
        scratch_shapes=[
            pltpu.VMEM((sources, 2, vectors, vectors), BF16),
            pltpu.VMEM((sources, 2, vectors, vectors), BF16),
            pltpu.VMEM((2 * sources * block_rows, vectors), BF16),
            pltpu.VMEM((2, sources, operators * block_rows, 2 * vectors), BF16),
            pltpu.SemaphoreType.DMA((2 * blocks,)),
        ],
        compiler_params=params(16),
        cost_estimate=pl.CostEstimate(flops=0, bytes_accessed=0, transcendentals=0),
        name="both_sides",
    )(elements, others, *perams)


def spread(wide, count_rows, block_rows):
    pieces = [
        wide[pl.ds(k, count_rows * block_rows // FOLD, stride=FOLD), :].astype(BF16)
        for k in range(FOLD)
    ]
    return jnp.concatenate(pieces, axis=1)


def lay_kernel(own_ref, pair_ref, out_ref, wide):
    sources, _, operators, block_rows, lanes = own_ref.shape
    rows = 2 * operators
    for s in range(sources):
        for at, ref in enumerate((own_ref, pair_ref)):
            wide[pl.ds(at * rows * block_rows, rows * block_rows), :] = (
                ref[s].astype(F32).reshape(rows * block_rows, lanes)
            )
        out_ref[s] = spread(wide, 2 * rows, block_rows)


def lay_out(own, pair):
    sources, _, operators, block_rows, lanes = own.shape
    rows = 2 * operators
    return pl.pallas_call(
        lay_kernel,
        out_shape=jax.ShapeDtypeStruct(
            (sources, 2 * rows * block_rows // FOLD, FOLD * lanes), BF16
        ),
        in_specs=[VMEM, VMEM],
        out_specs=VMEM,
        scratch_shapes=[pltpu.VMEM((2 * rows * block_rows, lanes), F32)],
        compiler_params=params(12),
        cost_estimate=pl.CostEstimate(flops=0, bytes_accessed=0, transcendentals=0),
        name="lay_out",
    )(own, pair)


def trace_kernel(count, table, line, times_ref, *refs):
    pools = refs[:count]
    laid_ref, out_ref, picked, wide, sems = refs[count:]
    sources = laid_ref.shape[0]
    _, operators, block_rows, lanes = pools[0].shape
    rows = 2 * operators
    time = lax.axis_index("tm")
    for s in range(sources):
        source = times_ref[s]
        code = line_code(time // 2, source // 2, lax.rem(source + time, 2), line)
        for index, (at, inside) in table.items():

            @pl.when(code == index)
            def _(at=at, inside=inside, s=s):
                block = pools[at] if inside is None else pools[at].at[inside]
                pltpu.make_async_copy(block, picked.at[s], sems.at[s]).start()

    groups = block_rows // FOLD
    shape = (2 * rows * groups, rows * groups)
    down = lax.broadcasted_iota(jnp.int32, shape, 0)
    over = lax.broadcasted_iota(jnp.int32, shape, 1)
    same = down % groups == over % groups
    shape = (rows * groups, rows)
    down = lax.broadcasted_iota(jnp.int32, shape, 0)
    over = lax.broadcasted_iota(jnp.int32, shape, 1)
    gather = (down // groups == over).astype(F32)
    for s in range(sources):
        pltpu.make_async_copy(pools[0], picked.at[s], sems.at[s]).wait()
        wide[s] = picked[s].astype(F32).reshape(rows * block_rows, lanes)
    sums = []
    for s in range(sources):
        product = lax.dot_general(
            laid_ref[s],
            spread(wide.at[s], rows, block_rows),
            (((1,), (1,)), ((), ())),
            preferred_element_type=F32,
        )
        product = jnp.where(same, product, 0.0).reshape(2 * rows, groups, rows * groups)
        sums.append(jnp.sum(product, axis=1))
    folded = jnp.dot(
        jnp.concatenate(sums, axis=0),
        gather,
        precision=lax.Precision.HIGHEST,
        preferred_element_type=F32,
    )
    for s in range(sources):
        out_ref[0, s] = folded[2 * rows * s : 2 * rows * s + rows]
        out_ref[1, s] = folded[2 * rows * s + rows : 2 * rows * (s + 1)]


def traces(source_times, pools, table, line, laid):
    sources = laid.shape[0]
    _, operators, block_rows, lanes = pools[0].shape
    rows = 2 * operators
    return pl.pallas_call(
        functools.partial(trace_kernel, len(pools), table, line),
        out_shape=jax.ShapeDtypeStruct((2, sources, rows, rows), F32),
        in_specs=[SMEM] + [ANY] * len(pools) + [VMEM],
        out_specs=VMEM,
        scratch_shapes=[
            pltpu.VMEM((sources,) + pools[0].shape, BF16),
            pltpu.VMEM((sources, rows * block_rows, lanes), F32),
            pltpu.SemaphoreType.DMA((sources,)),
        ],
        compiler_params=params(12),
        cost_estimate=pl.CostEstimate(
            flops=4 * sources * rows * rows * block_rows * lanes,
            bytes_accessed=2 * laid.size,
            transcendentals=0,
        ),
        name="traces",
    )(source_times, *pools, laid)


def finish_kernel(count, *refs):
    parts = refs[:count]
    correlator_ref, pairs_ref = refs[count:]
    sources, rows, _ = parts[1].shape
    n = rows // 2
    eye = lax.broadcasted_iota(jnp.int32, (n, n), 0) == lax.broadcasted_iota(jnp.int32, (n, n), 1)
    for s in range(sources):
        terms = [parts[0][0, s]] + [ref[s] for ref in parts[1:]]
        while len(terms) > 1:
            terms = [one + two for one, two in zip(terms[::2], terms[1::2])]
        total = terms[0]
        real = total[:n, :n] - total[n:, n:]
        imaginary = total[:n, n:] + total[n:, :n]
        correlator_ref[0, s, :, 0, :] = real
        correlator_ref[0, s, :, 1, :] = imaginary
        down_real, down_imaginary, over_real, over_imaginary = (
            jnp.sum(jnp.where(eye, block, 0.0), axis=axis, keepdims=True)
            for axis in (1, 0)
            for block in (real, imaginary)
        )
        pairs_ref[0, s, :, 0, :] = down_real * over_real - down_imaginary * over_imaginary
        pairs_ref[0, s, :, 1, :] = down_real * over_imaginary + down_imaginary * over_real


def finish(parts):
    sources, rows, _ = parts[1].shape
    result = jax.ShapeDtypeStruct((1, sources, rows // 2, 2, rows // 2), F32)
    correlator, pairs = pl.pallas_call(
        functools.partial(finish_kernel, len(parts)),
        out_shape=(result, result),
        in_specs=[VMEM] * len(parts),
        out_specs=(VMEM, VMEM),
        compiler_params=params(4),
        name="finish",
    )(*parts)
    return jnp.swapaxes(correlator, 2, 3), jnp.swapaxes(pairs, 2, 3)


def phase_tables(momenta, z_coords, z_extent):
    plane = jnp.arange(PLANE, dtype=jnp.int32)
    along_x = (momenta[:, 0:1] * (plane % LX)[None] % LX).astype(F32) * (2.0 * math.pi / LX)
    along_y = (momenta[:, 1:2] * (plane // LX)[None] % LY).astype(F32) * (2.0 * math.pi / LY)
    angle = along_x + along_y
    table = jnp.stack([jnp.cos(angle), jnp.sin(angle)], axis=1).reshape(-1, PLANE)
    along_z = (momenta[:, 2][None, :] * z_coords[:, None] % z_extent).astype(F32) * (
        2.0 * math.pi / z_extent
    )
    return table, jnp.stack([jnp.cos(along_z), jnp.sin(along_z)])


def body(eigenvectors, momenta, displacement, source_times, perambulators):
    _, parts, colours, _, plane, vectors = eigenvectors.shape
    slabs = lax.axis_size("space")
    line = lax.axis_size("tm") // 2
    block_rows = vectors // slabs
    near = 2

    own = eigenvectors.reshape(parts, colours, plane, vectors)
    beside = swap_bit(own, "space", 1)
    keys = swap_far(own)

    plane_phase, z_phase = phase_tables(momenta, jnp.arange(slabs, dtype=jnp.int32), slabs)
    tables = (displacement, z_phase, plane_phase)
    total = elementals(tables, [own, beside], near, None, block_rows)

    keys, total = lax.optimization_barrier((keys, total))
    slab_list = swap_near(keys)
    slab_list[1] = beside
    peram, _ = lax.optimization_barrier((perambulators[0], keys[slabs // 2]))
    perams = swap_far(peram)
    full, keep, send = elementals(tables, slab_list, near, total, block_rows)

    perams, full, send = lax.optimization_barrier((perams, full, send))
    perams = swap_near(perams)

    received = swap_bit(send, "tm", 1)
    g_keep, g_send = both_sides(full, swap_bit(full, "space", 1), perams)
    arrays, table, g_send = share_line(keep, received, g_send, line)
    laid = lay_out(g_keep, swap_bit(g_send, "tm", 1))
    both = traces(source_times, arrays, table, line, laid)
    both = both + swap_bit(both, "space", 1)
    mine, pair = both[0], both[1]
    near_sums = [swap_bit(mine, "space", mask) for mask in range(2, slabs, 2)]
    pair_sums = [swap_bit(pair, "tm", 1)]
    pair_sums += [across(pair, mask) for mask in range(2, slabs, 2)]
    return finish([both] + near_sums + pair_sums)


def across(block, mask):
    rows, times = lax.axis_size("space"), lax.axis_size("tm")
    route = [
        (i * times + t, (i ^ mask) * times + (t ^ 1)) for i in range(rows) for t in range(times)
    ]
    return lax.ppermute(block, ("space", "tm"), route)


def solution(mesh):
    placed = (
        P("tm", None, None, "space", None, None),
        P(),
        P(),
        P(),
        P("tm", None, None, "space", None),
    )
    return jax.shard_map(
        body,
        mesh=mesh,
        in_specs=placed,
        out_specs=(P("tm", None, None, None, None), P("tm", None, None, None, None)),
        check_vma=False,
    )
```

```python
import functools
import math

import jax
import jax.numpy as jnp
from jax import lax
from jax.experimental import pallas as pl
from jax.experimental.pallas import tpu as pltpu
from jax.sharding import PartitionSpec as P

LX = 16
LY = 16
PLANE = LX * LY
LANES = 128
F32 = jnp.float32
BF16 = jnp.bfloat16
CHUNK = 32
GROUPS = 8
MEGA = 1024 * 1024

SMEM = pl.BlockSpec(memory_space=pltpu.SMEM)
VMEM = pl.BlockSpec(memory_space=pltpu.VMEM)


def swap_bit(block, axis, mask):
    count = lax.axis_size(axis)
    return lax.ppermute(block, axis, [(i, i ^ mask) for i in range(count)])


def along_line(block, moves):
    route = [(2 * z + x, 2 * to + x) for z, to in moves.items() for x in range(2)]
    return lax.ppermute(block, "tm", route)


def share_line(keep, received, g_send, line):
    piece = jnp.stack([keep, received])
    if line != 4:
        arrays, table = [keep, received], {0: (0, None), 1: (1, None)}
        for distance in range(1, line):
            moved = along_line(piece, {z: (z + distance) % line for z in range(line)})
            for side in range(2):
                table[2 * distance + side] = (len(arrays), side)
            arrays.append(moved)
        return arrays, table, g_send
    outward = {1: 0, 2: 3}
    received, g_send = lax.optimization_barrier((received, g_send))
    piece = jnp.stack([keep, received])
    opposite = along_line(piece, {1: 2, 2: 1, 0: 3, 3: 0})
    skip = along_line(piece, {0: 2, 3: 1})
    near = along_line(piece, {0: 1, 1: 0, 2: 3, 3: 2})
    passed = along_line(opposite, outward)
    arrays = [keep, received, near, skip, opposite, passed]
    table = {0: (0, None), 1: (1, None)}
    for code in range(2, 10):
        table[code] = (1 + code // 2, code % 2)
    return arrays, table, g_send


def line_code(here, there, side, line):
    if line != 4:
        return 2 * lax.rem(here - there + line, line) + side
    apart = here ^ there
    ends = (here == 0) | (here == line - 1)
    return 2 * jnp.where(ends & (apart == 2), 4, apart) + side


def swap_far(block):
    held = {0: block}
    mask = lax.axis_size("space") // 2
    while mask >= 2:
        for key in sorted(held):
            held[key | mask] = swap_bit(held[key], "space", mask)
        mask //= 2
    return held


def swap_near(held):
    both = dict(held)
    for key in sorted(held):
        both[key | 1] = swap_bit(held[key], "space", 1)
    return [both[key] for key in sorted(both)]


def params(megabytes):
    return pltpu.CompilerParams(vmem_limit_bytes=megabytes * MEGA)


def elemental_kernel(held, near, late, block_rows, *refs):
    move_ref, zphase_ref = refs[:2]
    slab_refs = refs[2 : 2 + held]
    rest = refs[2 + held :]
    if not late:
        phase_ref, rest = rest[0], rest[1:]
    if late:
        table, prior_ref, acc_out, keep_ref, send_ref = rest[:5]
        slabs, turned, mixed_a, mixed_b, todo, acc, wide = rest[5:]
    else:
        acc, table, slabs, turned, mixed_a, mixed_b, todo = rest
    operators, half_rows, vectors = acc.shape
    half_rows //= 2
    colours = turned.shape[0]
    count = lax.axis_size("space")
    me = lax.axis_index("space")
    core = lax.rem(me, 2)

    for m in range(held):
        slabs[m, :, :, pl.ds(0, PLANE), :] = slab_refs[m][...]
        slabs[m, :, :, pl.ds(PLANE, LX), :] = slab_refs[m][:, :, pl.ds(0, LX), :]
    acc[...] = jnp.zeros_like(acc)
    if not late:
        upright = phase_ref[...].T
        for o in range(operators):
            for part in range(2):
                at = 2 * o + part
                table[o, part] = jnp.broadcast_to(upright[:, at : at + 1], (PLANE, LANES))
    def one_slab(m, carry):
        here = me ^ m
        above = lax.rem(here + 1, count) ^ me
        far = above >= near

        def collect(o, found):
            waits = (m >= near) | ((move_ref[o] == 3) & far)
            chosen = waits if late else jnp.logical_not(waits)

            @pl.when(chosen)
            def _():
                todo[found] = o

            return found + chosen.astype(jnp.int32)

        def turn_phases(o, mixed, colour):
            move = move_ref[o]
            src = jnp.where(move == 3, above, jnp.where(move == 1, held, m))
            off = pl.multiple_of(jnp.where(move == 2, LX, 0), LX)
            cos_z, sin_z = zphase_ref[0, here, o], zphase_ref[1, here, o]
            for begin in range(0, PLANE, CHUNK):
                cos_p = table[o, 0, pl.ds(begin, CHUNK), :]
                sin_p = table[o, 1, pl.ds(begin, CHUNK), :]
                cosine = cos_p * cos_z - sin_p * sin_z
                sine = sin_p * cos_z + cos_p * sin_z
                cosine = jnp.concatenate([cosine] * (vectors // LANES), axis=1)
                sine = jnp.concatenate([sine] * (vectors // LANES), axis=1)
                real = slabs[src, 0, colour, pl.ds(off + begin, CHUNK), :].astype(F32)
                imag = slabs[src, 1, colour, pl.ds(off + begin, CHUNK), :].astype(F32)
                mixed[colour, pl.ds(begin, CHUNK), :] = (cosine * real + sine * imag).astype(BF16)
                mixed[colour, pl.ds(PLANE + begin, CHUNK), :] = (
                    cosine * imag - sine * real
                ).astype(BF16)

        def step(o, mixed, later, following):
            total = None
            for colour in range(colours):
                turn_phases(later, following, colour)
            for colour in range(colours):
                term = jnp.dot(turned[colour], mixed[colour], preferred_element_type=F32)
                total = term if total is None else total + term
            acc[o] += total

        found = lax.fori_loop(0, operators, collect, jnp.int32(0))

        @pl.when(found > 0)
        def _():
            for colour in range(colours):
                for part in range(2):
                    block = slabs[m, part, colour, pl.ds(0, PLANE), :]
                    flat = block.T.reshape(half_rows // block_rows, 2, block_rows, PLANE)
                    flat = jnp.where(core == 0, flat[:, 0], flat[:, 1]).reshape(half_rows, PLANE)
                    same = flat if part == 0 else -flat
                    lower = pl.ds(half_rows, half_rows)
                    turned[colour, pl.ds(0, half_rows), pl.ds(part * PLANE, PLANE)] = flat
                    turned[colour, lower, pl.ds((1 - part) * PLANE, PLANE)] = same

        @pl.when((found > 0) & (m >= near if late else m >= 0))
        def _():
            for colour in range(colours):
                for part in range(2):
                    for begin in range(0, PLANE, CHUNK):
                        rows = slabs[m, part, colour, pl.ds(begin, CHUNK), :].astype(F32)
                        rows = pltpu.roll(rows.reshape(CHUNK // LX, LX, vectors), LX - 1, 1)
                        slabs[held, part, colour, pl.ds(begin, CHUNK), :] = rows.reshape(
                            CHUNK, vectors
                        ).astype(BF16)

        @pl.when(found > 0)
        def _():
            for colour in range(colours):
                turn_phases(todo[0], mixed_a, colour)

            def two(i, inner):
                step(todo[2 * i], mixed_a, todo[jnp.minimum(2 * i + 1, found - 1)], mixed_b)

                @pl.when(2 * i + 1 < found)
                def _():
                    after = todo[jnp.minimum(2 * i + 2, found - 1)]
                    step(todo[2 * i + 1], mixed_b, after, mixed_a)

                return inner

            lax.fori_loop(0, (found + 1) // 2, two, 0)

        return carry

    lax.fori_loop(0, held, one_slab, 0)

    if late:
        first = pl.multiple_of(me // 2 * block_rows, block_rows)
        half = lax.rem(lax.axis_index("tm"), 2)
        for o in range(operators):
            acc_out[o] = (acc[o] + prior_ref[o]).astype(BF16)
        for part in range(2):
            for o in range(operators):
                rows = pl.ds(part * half_rows + first, block_rows)
                own = acc[o, rows, :] + prior_ref[o, rows, :]
                at = pl.ds((part * operators + o) * block_rows, block_rows)
                wide[0, at, :] = own[:, :LANES]
                wide[1, at, :] = own[:, LANES:]
        keep_ref[...] = spread(wide.at[half], 2 * operators, block_rows)
        send_ref[...] = spread(wide.at[1 - half], 2 * operators, block_rows)


def elementals(tables, slab_list, near, prior, block_rows):
    _, colours, plane, vectors = slab_list[0].shape
    held = len(slab_list)
    operators = tables[0].shape[0]
    late = prior is not None
    wide = jax.ShapeDtypeStruct((operators, vectors, vectors), F32)
    scratch = [
        pltpu.VMEM((held + 1, 2, colours, plane + LX, vectors), BF16),
        pltpu.VMEM((colours, vectors, 2 * plane), BF16),
        pltpu.VMEM((colours, 2 * plane, vectors), BF16),
        pltpu.VMEM((colours, 2 * plane, vectors), BF16),
        pltpu.SMEM((operators,), jnp.int32),
    ]
    if late:
        piece = jax.ShapeDtypeStruct(
            (2 * operators * GROUPS, block_rows // GROUPS * LANES), BF16
        )
        outs = (jax.ShapeDtypeStruct(wide.shape, BF16), piece, piece)
        out_specs = (VMEM, VMEM, VMEM)
        scratch.append(pltpu.VMEM(wide.shape, F32))
        scratch.append(pltpu.VMEM((2, 2 * operators * block_rows, LANES), F32))
    else:
        outs = (wide, jax.ShapeDtypeStruct((operators, 2, plane, LANES), F32))
        out_specs = (VMEM, VMEM)
    move, z_phase, phases = tables
    priors = [phases, prior] if late else [phases]
    return pl.pallas_call(
        functools.partial(elemental_kernel, held, near, late, block_rows),
        out_shape=outs,
        in_specs=[SMEM, SMEM] + [VMEM] * (held + len(priors)),
        out_specs=out_specs,
        scratch_shapes=scratch,
        compiler_params=params(20 + held),
        cost_estimate=pl.CostEstimate(
            flops=8 * held * operators * colours * plane * vectors * vectors,
            bytes_accessed=held * 2 * colours * plane * vectors * 2,
            transcendentals=0,
        ),
        name="elementals_late" if late else "elementals_early",
    )(move, z_phase, *slab_list, *priors)


def both_kernel(blocks, e_ref, other_ref, *refs):
    peram_refs = refs[:blocks]
    keep_ref, rest = refs[blocks], refs[blocks + 1 :]
    whole, sorted_rows, left, middle = rest[-4:]
    send_refs = rest[:-4]
    each = keep_ref.shape[0] // len(send_refs)
    sources, _, vectors, _ = whole.shape
    operators = e_ref.shape[0]
    block_rows = keep_ref.shape[3]
    me = lax.axis_index("space")
    half = lax.rem(lax.axis_index("tm"), 2)
    for m in range(blocks):
        begin = pl.multiple_of((me ^ m) * block_rows, block_rows)
        whole[:, :, pl.ds(begin, block_rows), :] = peram_refs[m][...]
        begin = (m % 2) * (vectors // 2) + (me ^ m) // 2 * block_rows
        begin = pl.multiple_of(begin, block_rows)
        sorted_rows[:, :, pl.ds(begin, block_rows), :] = peram_refs[m][...]
    row = lax.broadcasted_iota(jnp.int32, (block_rows, vectors), 0)
    column = lax.broadcasted_iota(jnp.int32, (block_rows, vectors), 1)
    chosen = (column == row + me * block_rows).astype(F32).astype(BF16)
    for s in range(sources):
        for part in range(2):
            flat = lax.dot_general(
                chosen, whole[s, part], (((1,), (1,)), ((), ())), preferred_element_type=F32
            )
            left[pl.ds((part * sources + s) * block_rows, block_rows), :] = flat.astype(BF16)
    group = sources * block_rows
    cut = vectors // 2
    for a in range(operators):
        sides = []
        for ref in (e_ref, other_ref):
            product = lax.dot_general(
                left[...], ref[a], (((1,), (1,)), ((), ())), preferred_element_type=F32
            )
            sides.append(
                (
                    product[:group, :cut] - product[group:, cut:],
                    product[:group, cut:] + product[group:, :cut],
                )
            )
        real, imaginary = (
            jnp.concatenate([one, two], axis=1) for one, two in zip(*sides)
        )
        for part, block in enumerate((real, imaginary)):
            high = block.astype(BF16)
            low = (block - high.astype(F32)).astype(BF16)
            for s in range(sources):
                base = s * block_rows
                rows = pl.ds(a * block_rows, block_rows)
                columns = pl.ds(part * vectors, vectors)
                middle[0, s, rows, columns] = high[base : base + block_rows]
                middle[1, s, rows, columns] = low[base : base + block_rows]
    for s in range(sources):
        real, imaginary = sorted_rows[s, 0], sorted_rows[s, 1]
        right = jnp.concatenate(
            [
                jnp.concatenate([real, -imaginary], axis=1),
                jnp.concatenate([imaginary, real], axis=1),
            ],
            axis=0,
        )
        image = jnp.dot(middle[0, s], right, preferred_element_type=F32)
        image = image + jnp.dot(middle[1, s], right, preferred_element_type=F32)
        image = image.astype(BF16)
        for a in range(operators):
            for part in range(2):
                rows = image[a * block_rows : (a + 1) * block_rows]
                low = rows[:, part * vectors : part * vectors + LANES]
                high = rows[:, part * vectors + LANES : (part + 1) * vectors]
                keep_ref[s, part, a] = jnp.where(half == 0, low, high)
                send_refs[s // each][s % each, part, a] = jnp.where(half == 0, high, low)


def both_sides(elements, others, perams):
    blocks = len(perams)
    sources, _, block_rows, vectors = perams[0].shape
    operators = elements.shape[0]
    piece = jax.ShapeDtypeStruct((sources, 2, operators, block_rows, LANES), BF16)
    sends = 2 - sources % 2
    part = jax.ShapeDtypeStruct((sources // sends,) + piece.shape[1:], BF16)
    return pl.pallas_call(
        functools.partial(both_kernel, blocks),
        out_shape=(piece,) + (part,) * sends,
        in_specs=[VMEM] * (2 + blocks),
        out_specs=(VMEM,) * (1 + sends),
        scratch_shapes=[
            pltpu.VMEM((sources, 2, vectors, vectors), BF16),
            pltpu.VMEM((sources, 2, vectors, vectors), BF16),
            pltpu.VMEM((2 * sources * block_rows, vectors), BF16),
            pltpu.VMEM((2, sources, operators * block_rows, 2 * vectors), BF16),
        ],
        compiler_params=params(16),
        cost_estimate=pl.CostEstimate(flops=0, bytes_accessed=0, transcendentals=0),
        name="both_sides",
    )(elements, others, *perams)


def spread(wide, count_rows, block_rows):
    fold = block_rows // GROUPS
    pieces = [
        wide[pl.ds(k, count_rows * GROUPS, stride=fold), :].astype(BF16) for k in range(fold)
    ]
    return jnp.concatenate(pieces, axis=1)


def lay_kernel(own_ref, *refs):
    pair_refs, out_ref, wide = refs[:-2], refs[-2], refs[-1]
    each = own_ref.shape[0] // len(pair_refs)
    sources, _, operators, block_rows, lanes = own_ref.shape
    rows = 2 * operators
    for s in range(sources):
        for at, ref in enumerate((own_ref.at[s], pair_refs[s // each].at[s % each])):
            wide[pl.ds(at * rows * block_rows, rows * block_rows), :] = (
                ref[...].astype(F32).reshape(rows * block_rows, lanes)
            )
        out_ref[s] = spread(wide, 2 * rows, block_rows)


def lay_out(own, pair):
    sources, _, operators, block_rows, lanes = own.shape
    rows = 2 * operators
    return pl.pallas_call(
        lay_kernel,
        out_shape=jax.ShapeDtypeStruct(
            (sources, 2 * rows * GROUPS, block_rows // GROUPS * lanes), BF16
        ),
        in_specs=[VMEM] * (1 + len(pair)),
        out_specs=VMEM,
        scratch_shapes=[pltpu.VMEM((2 * rows * block_rows, lanes), F32)],
        compiler_params=params(12),
        cost_estimate=pl.CostEstimate(flops=0, bytes_accessed=0, transcendentals=0),
        name="lay_out",
    )(own, *pair)


def trace_kernel(count, table, line, times_ref, *refs):
    pools = refs[:count]
    laid_ref, out_ref, picked = refs[count:]
    sources = laid_ref.shape[0]
    groups = GROUPS
    rows = pools[0].shape[0] // groups
    time = lax.axis_index("tm")
    for s in range(sources):
        source = times_ref[s]
        code = line_code(time // 2, source // 2, lax.rem(source + time, 2), line)
        for index, (at, inside) in table.items():

            @pl.when(code == index)
            def _(at=at, inside=inside, s=s):
                block = pools[at] if inside is None else pools[at].at[inside]
                picked[s] = block[...]

    shape = (2 * rows * groups, rows * groups)
    down = lax.broadcasted_iota(jnp.int32, shape, 0)
    over = lax.broadcasted_iota(jnp.int32, shape, 1)
    same = down % groups == over % groups
    shape = (rows * groups, rows)
    down = lax.broadcasted_iota(jnp.int32, shape, 0)
    over = lax.broadcasted_iota(jnp.int32, shape, 1)
    gather = (down // groups == over).astype(F32)
    sums = []
    for s in range(sources):
        product = lax.dot_general(
            laid_ref[s],
            picked[s],
            (((1,), (1,)), ((), ())),
            preferred_element_type=F32,
        )
        product = jnp.where(same, product, 0.0).reshape(2 * rows, groups, rows * groups)
        sums.append(jnp.sum(product, axis=1))
    folded = jnp.dot(
        jnp.concatenate(sums, axis=0),
        gather,
        precision=lax.Precision.HIGHEST,
        preferred_element_type=F32,
    )
    for s in range(sources):
        out_ref[0, s] = folded[2 * rows * s : 2 * rows * s + rows]
        out_ref[1, s] = folded[2 * rows * s + rows : 2 * rows * (s + 1)]


def traces(source_times, pools, table, line, laid):
    sources = laid.shape[0]
    rows = pools[0].shape[0] // GROUPS
    return pl.pallas_call(
        functools.partial(trace_kernel, len(pools), table, line),
        out_shape=jax.ShapeDtypeStruct((2, sources, rows, rows), F32),
        in_specs=[SMEM] + [VMEM] * (len(pools) + 1),
        out_specs=VMEM,
        scratch_shapes=[
            pltpu.VMEM((sources,) + pools[0].shape, BF16),
        ],
        compiler_params=params(12),
        cost_estimate=pl.CostEstimate(
            flops=4 * laid.size * rows,
            bytes_accessed=2 * laid.size,
            transcendentals=0,
        ),
        name="traces",
    )(source_times, *pools, laid)


def finish_kernel(count, *refs):
    parts = refs[:count]
    correlator_ref, pairs_ref = refs[count:]
    sources, rows, _ = parts[1].shape
    n = rows // 2
    eye = lax.broadcasted_iota(jnp.int32, (n, n), 0) == lax.broadcasted_iota(jnp.int32, (n, n), 1)
    for s in range(sources):
        terms = [parts[0][0, s]] + [ref[s] for ref in parts[1:]]
        while len(terms) > 1:
            terms = [one + two for one, two in zip(terms[::2], terms[1::2])]
        total = terms[0]
        real = total[:n, :n] - total[n:, n:]
        imaginary = total[:n, n:] + total[n:, :n]
        correlator_ref[0, s, :, 0, :] = real
        correlator_ref[0, s, :, 1, :] = imaginary
        down_real, down_imaginary, over_real, over_imaginary = (
            jnp.sum(jnp.where(eye, block, 0.0), axis=axis, keepdims=True)
            for axis in (1, 0)
            for block in (real, imaginary)
        )
        pairs_ref[0, s, :, 0, :] = down_real * over_real - down_imaginary * over_imaginary
        pairs_ref[0, s, :, 1, :] = down_real * over_imaginary + down_imaginary * over_real


def finish(parts):
    sources, rows, _ = parts[1].shape
    result = jax.ShapeDtypeStruct((1, sources, rows // 2, 2, rows // 2), F32)
    correlator, pairs = pl.pallas_call(
        functools.partial(finish_kernel, len(parts)),
        out_shape=(result, result),
        in_specs=[VMEM] * len(parts),
        out_specs=(VMEM, VMEM),
        compiler_params=params(4),
        name="finish",
    )(*parts)
    return jnp.swapaxes(correlator, 2, 3), jnp.swapaxes(pairs, 2, 3)


def phase_tables(momenta, z_coords, z_extent):
    plane = jnp.arange(PLANE, dtype=jnp.int32)
    along_x = (momenta[:, 0:1] * (plane % LX)[None] % LX).astype(F32) * (2.0 * math.pi / LX)
    along_y = (momenta[:, 1:2] * (plane // LX)[None] % LY).astype(F32) * (2.0 * math.pi / LY)
    angle = along_x + along_y
    table = jnp.stack([jnp.cos(angle), jnp.sin(angle)], axis=1).reshape(-1, PLANE)
    along_z = (momenta[:, 2][None, :] * z_coords[:, None] % z_extent).astype(F32) * (
        2.0 * math.pi / z_extent
    )
    return table, jnp.stack([jnp.cos(along_z), jnp.sin(along_z)])


def body(eigenvectors, momenta, displacement, source_times, perambulators):
    _, parts, colours, _, plane, vectors = eigenvectors.shape
    slabs = lax.axis_size("space")
    line = lax.axis_size("tm") // 2
    block_rows = vectors // slabs
    near = 2

    own = eigenvectors.reshape(parts, colours, plane, vectors)
    beside = swap_bit(own, "space", 1)
    keys = swap_far(own)

    plane_phase, z_phase = phase_tables(momenta, jnp.arange(slabs, dtype=jnp.int32), slabs)
    tables = (displacement, z_phase, plane_phase)
    total, wide_phase = elementals(tables, [own, beside], near, None, block_rows)

    keys, total = lax.optimization_barrier((keys, total))
    slab_list = swap_near(keys)
    slab_list[1] = beside
    peram, _ = lax.optimization_barrier((perambulators[0], keys[slabs // 2]))
    perams = swap_far(peram)
    tables = (displacement, z_phase, wide_phase)
    full, keep, send = elementals(tables, slab_list, near, total, block_rows)

    perams, full, send = lax.optimization_barrier((perams, full, send))
    perams = swap_near(perams)

    received = swap_bit(send, "tm", 1)
    g_keep, *g_send = both_sides(full, swap_bit(full, "space", 1), perams)
    arrays, table, g_send = share_line(keep, received, g_send, line)
    laid = lay_out(g_keep, [swap_bit(block, "tm", 1) for block in g_send])
    both = traces(source_times, arrays, table, line, laid)
    both = both + swap_bit(both, "space", 1)
    mine, pair = both[0], both[1]
    near_sums = [swap_bit(mine, "space", mask) for mask in range(2, slabs, 2)]
    pair_sums = [swap_bit(pair, "tm", 1)]
    pair_sums += [across(pair, mask) for mask in range(2, slabs, 2)]
    return finish([both] + near_sums + pair_sums)


def across(block, mask):
    rows, times = lax.axis_size("space"), lax.axis_size("tm")
    route = [
        (i * times + t, (i ^ mask) * times + (t ^ 1)) for i in range(rows) for t in range(times)
    ]
    return lax.ppermute(block, ("space", "tm"), route)


def solution(mesh):
    placed = (
        P("tm", None, None, "space", None, None),
        P(),
        P(),
        P(),
        P("tm", None, None, "space", None),
    )
    return jax.shard_map(
        body,
        mesh=mesh,
        in_specs=placed,
        out_specs=(P("tm", None, None, None, None), P("tm", None, None, None, None)),
        check_vma=False,
    )
```

```python
import functools
import math

import jax
import jax.numpy as jnp
from jax import lax
from jax.experimental import pallas as pl
from jax.experimental.pallas import tpu as pltpu
from jax.sharding import PartitionSpec as P

LX = 16
LY = 16
PLANE = LX * LY
LANES = 128
F32 = jnp.float32
BF16 = jnp.bfloat16
CHUNK = 32
GROUPS = 8
MEGA = 1024 * 1024

SMEM = pl.BlockSpec(memory_space=pltpu.SMEM)
VMEM = pl.BlockSpec(memory_space=pltpu.VMEM)


def swap_bit(block, axis, mask):
    count = lax.axis_size(axis)
    return lax.ppermute(block, axis, [(i, i ^ mask) for i in range(count)])


def along_line(block, moves):
    route = [(2 * z + x, 2 * to + x) for z, to in moves.items() for x in range(2)]
    return lax.ppermute(block, "tm", route)


def share_line(keep, received, g_send, line):
    piece = jnp.stack([keep, received])
    if line != 4:
        arrays, table = [keep, received], {0: (0, None), 1: (1, None)}
        for distance in range(1, line):
            moved = along_line(piece, {z: (z + distance) % line for z in range(line)})
            for side in range(2):
                table[2 * distance + side] = (len(arrays), side)
            arrays.append(moved)
        return arrays, table, g_send
    outward = {1: 0, 2: 3}
    received, g_send = lax.optimization_barrier((received, g_send))
    piece = jnp.stack([keep, received])
    opposite = along_line(piece, {1: 2, 2: 1, 0: 3, 3: 0})
    skip = along_line(piece, {0: 2, 3: 1})
    near = along_line(piece, {0: 1, 1: 0, 2: 3, 3: 2})
    passed = along_line(opposite, outward)
    arrays = [keep, received, near, skip, opposite, passed]
    table = {0: (0, None), 1: (1, None)}
    for code in range(2, 10):
        table[code] = (1 + code // 2, code % 2)
    return arrays, table, g_send


def line_code(here, there, side, line):
    if line != 4:
        return 2 * lax.rem(here - there + line, line) + side
    apart = here ^ there
    ends = (here == 0) | (here == line - 1)
    return 2 * jnp.where(ends & (apart == 2), 4, apart) + side


def swap_far(block):
    held = {0: block}
    mask = lax.axis_size("space") // 2
    while mask >= 2:
        for key in sorted(held):
            held[key | mask] = swap_bit(held[key], "space", mask)
        mask //= 2
    return held


def swap_near(held):
    both = dict(held)
    for key in sorted(held):
        both[key | 1] = swap_bit(held[key], "space", 1)
    return [both[key] for key in sorted(both)]


def params(megabytes):
    return pltpu.CompilerParams(vmem_limit_bytes=megabytes * MEGA)


def elemental_kernel(held, near, late, block_rows, *refs):
    move_ref, zphase_ref = refs[:2]
    slab_refs = refs[2 : 2 + held]
    rest = refs[2 + held :]
    if not late:
        phase_ref, rest = rest[0], rest[1:]
    if late:
        table, prior_ref, acc_out, keep_ref, send_ref = rest[:5]
        slabs, turned, mixed_a, mixed_b, todo, acc, wide = rest[5:]
    else:
        acc, table, slabs, turned, mixed_a, mixed_b, todo = rest
    operators, half_rows, vectors = acc.shape
    half_rows //= 2
    colours = turned.shape[0]
    count = lax.axis_size("space")
    me = lax.axis_index("space")
    core = lax.rem(me, 2)

    for m in range(held):
        slabs[m, :, :, pl.ds(0, PLANE), :] = slab_refs[m][...]
        slabs[m, :, :, pl.ds(PLANE, LX), :] = slab_refs[m][:, :, pl.ds(0, LX), :]
    acc[...] = prior_ref[...] if late else jnp.zeros_like(acc)
    if not late:
        upright = phase_ref[...].T
        for o in range(operators):
            for part in range(2):
                at = 2 * o + part
                table[o, part] = jnp.broadcast_to(upright[:, at : at + 1], (PLANE, LANES))
    def one_slab(m, carry):
        here = me ^ m
        above = lax.rem(here + 1, count) ^ me
        far = above >= near

        def collect(o, found):
            waits = (m >= near) | ((move_ref[o] == 3) & far)
            chosen = waits if late else jnp.logical_not(waits)

            @pl.when(chosen)
            def _():
                todo[found] = o

            return found + chosen.astype(jnp.int32)

        def turn_phases(o, mixed, colour):
            move = move_ref[o]
            src = jnp.where(move == 3, above, jnp.where(move == 1, held, m))
            off = pl.multiple_of(jnp.where(move == 2, LX, 0), LX)
            cos_z, sin_z = zphase_ref[0, here, o], zphase_ref[1, here, o]
            for begin in range(0, PLANE, CHUNK):
                cos_p = table[o, 0, pl.ds(begin, CHUNK), :]
                sin_p = table[o, 1, pl.ds(begin, CHUNK), :]
                cosine = cos_p * cos_z - sin_p * sin_z
                sine = sin_p * cos_z + cos_p * sin_z
                cosine = jnp.concatenate([cosine] * (vectors // LANES), axis=1)
                sine = jnp.concatenate([sine] * (vectors // LANES), axis=1)
                real = slabs[src, 0, colour, pl.ds(off + begin, CHUNK), :].astype(F32)
                imag = slabs[src, 1, colour, pl.ds(off + begin, CHUNK), :].astype(F32)
                mixed[colour, pl.ds(begin, CHUNK), :] = (cosine * real + sine * imag).astype(BF16)
                mixed[colour, pl.ds(PLANE + begin, CHUNK), :] = (
                    cosine * imag - sine * real
                ).astype(BF16)

        def step(o, mixed, later, following):
            total = None
            for colour in range(colours):
                turn_phases(later, following, colour)
            for colour in range(colours):
                term = jnp.dot(turned[colour], mixed[colour], preferred_element_type=F32)
                total = term if total is None else total + term
            acc[o] += total

        found = lax.fori_loop(0, operators, collect, jnp.int32(0))

        @pl.when((found > 0) & (m >= near if late else m >= 0))
        def _():
            for colour in range(colours):
                for part in range(2):
                    for begin in range(0, PLANE, CHUNK):
                        rows = slabs[m, part, colour, pl.ds(begin, CHUNK), :].astype(F32)
                        rows = pltpu.roll(rows.reshape(CHUNK // LX, LX, vectors), LX - 1, 1)
                        slabs[held, part, colour, pl.ds(begin, CHUNK), :] = rows.reshape(
                            CHUNK, vectors
                        ).astype(BF16)

        @pl.when(found > 0)
        def _():
            for colour in range(colours):
                for part in range(2):
                    block = slabs[m, part, colour, pl.ds(0, PLANE), :]
                    flat = block.T.reshape(half_rows // block_rows, 2, block_rows, PLANE)
                    flat = jnp.where(core == 0, flat[:, 0], flat[:, 1]).reshape(half_rows, PLANE)
                    same = flat if part == 0 else -flat
                    lower = pl.ds(half_rows, half_rows)
                    turned[colour, pl.ds(0, half_rows), pl.ds(part * PLANE, PLANE)] = flat
                    turned[colour, lower, pl.ds((1 - part) * PLANE, PLANE)] = same
            for colour in range(colours):
                turn_phases(todo[0], mixed_a, colour)

            def two(i, inner):
                step(todo[2 * i], mixed_a, todo[jnp.minimum(2 * i + 1, found - 1)], mixed_b)

                @pl.when(2 * i + 1 < found)
                def _():
                    after = todo[jnp.minimum(2 * i + 2, found - 1)]
                    step(todo[2 * i + 1], mixed_b, after, mixed_a)

                return inner

            lax.fori_loop(0, (found + 1) // 2, two, 0)

        return carry

    lax.fori_loop(0, held, one_slab, 0)

    if late:
        first = pl.multiple_of(me // 2 * block_rows, block_rows)
        half = lax.rem(lax.axis_index("tm"), 2)
        for o in range(operators):
            acc_out[o] = acc[o].astype(BF16)
        for part in range(2):
            for o in range(operators):
                rows = pl.ds(part * half_rows + first, block_rows)
                own = acc[o, rows, :]
                at = pl.ds((part * operators + o) * block_rows, block_rows)
                wide[0, at, :] = own[:, :LANES]
                wide[1, at, :] = own[:, LANES:]
        keep_ref[...] = spread(wide.at[half], 2 * operators, block_rows)
        send_ref[...] = spread(wide.at[1 - half], 2 * operators, block_rows)


def elementals(tables, slab_list, near, prior, block_rows):
    _, colours, plane, vectors = slab_list[0].shape
    held = len(slab_list)
    operators = tables[0].shape[0]
    late = prior is not None
    wide = jax.ShapeDtypeStruct((operators, vectors, vectors), F32)
    scratch = [
        pltpu.VMEM((held + 1, 2, colours, plane + LX, vectors), BF16),
        pltpu.VMEM((colours, vectors, 2 * plane), BF16),
        pltpu.VMEM((colours, 2 * plane, vectors), BF16),
        pltpu.VMEM((colours, 2 * plane, vectors), BF16),
        pltpu.SMEM((operators,), jnp.int32),
    ]
    if late:
        piece = jax.ShapeDtypeStruct(
            (2 * operators * GROUPS, block_rows // GROUPS * LANES), BF16
        )
        outs = (jax.ShapeDtypeStruct(wide.shape, BF16), piece, piece)
        out_specs = (VMEM, VMEM, VMEM)
        scratch.append(pltpu.VMEM(wide.shape, F32))
        scratch.append(pltpu.VMEM((2, 2 * operators * block_rows, LANES), F32))
    else:
        outs = (wide, jax.ShapeDtypeStruct((operators, 2, plane, LANES), F32))
        out_specs = (VMEM, VMEM)
    move, z_phase, phases = tables
    priors = [phases, prior] if late else [phases]
    return pl.pallas_call(
        functools.partial(elemental_kernel, held, near, late, block_rows),
        out_shape=outs,
        in_specs=[SMEM, SMEM] + [VMEM] * (held + len(priors)),
        out_specs=out_specs,
        scratch_shapes=scratch,
        compiler_params=params(20 + held),
        cost_estimate=pl.CostEstimate(
            flops=8 * held * operators * colours * plane * vectors * vectors,
            bytes_accessed=held * 2 * colours * plane * vectors * 2,
            transcendentals=0,
        ),
        name="elementals_late" if late else "elementals_early",
    )(move, z_phase, *slab_list, *priors)


def both_kernel(blocks, e_ref, other_ref, *refs):
    peram_refs = refs[:blocks]
    keep_ref, rest = refs[blocks], refs[blocks + 1 :]
    whole, sorted_rows, left, middle = rest[-4:]
    send_refs = rest[:-4]
    each = keep_ref.shape[0] // len(send_refs)
    sources, _, vectors, _ = whole.shape
    operators = e_ref.shape[0]
    block_rows = keep_ref.shape[3]
    me = lax.axis_index("space")
    half = lax.rem(lax.axis_index("tm"), 2)
    for m in range(blocks):
        begin = pl.multiple_of((me ^ m) * block_rows, block_rows)
        whole[:, :, pl.ds(begin, block_rows), :] = peram_refs[m][...]
        begin = (m % 2) * (vectors // 2) + (me ^ m) // 2 * block_rows
        begin = pl.multiple_of(begin, block_rows)
        sorted_rows[:, :, pl.ds(begin, block_rows), :] = peram_refs[m][...]
    row = lax.broadcasted_iota(jnp.int32, (block_rows, vectors), 0)
    column = lax.broadcasted_iota(jnp.int32, (block_rows, vectors), 1)
    chosen = (column == row + me * block_rows).astype(F32).astype(BF16)
    for s in range(sources):
        for part in range(2):
            flat = lax.dot_general(
                chosen, whole[s, part], (((1,), (1,)), ((), ())), preferred_element_type=F32
            )
            left[pl.ds((part * sources + s) * block_rows, block_rows), :] = flat.astype(BF16)
    group = sources * block_rows
    cut = vectors // 2
    for a in range(operators):
        sides = []
        for ref in (e_ref, other_ref):
            product = lax.dot_general(
                left[...], ref[a], (((1,), (1,)), ((), ())), preferred_element_type=F32
            )
            sides.append(
                (
                    product[:group, :cut] - product[group:, cut:],
                    product[:group, cut:] + product[group:, :cut],
                )
            )
        real, imaginary = (
            jnp.concatenate([one, two], axis=1) for one, two in zip(*sides)
        )
        for part, block in enumerate((real, imaginary)):
            high = block.astype(BF16)
            low = (block - high.astype(F32)).astype(BF16)
            for s in range(sources):
                base = s * block_rows
                rows = pl.ds(a * block_rows, block_rows)
                columns = pl.ds(part * vectors, vectors)
                middle[0, s, rows, columns] = high[base : base + block_rows]
                middle[1, s, rows, columns] = low[base : base + block_rows]
    for s in range(sources):
        real, imaginary = sorted_rows[s, 0], sorted_rows[s, 1]
        right = jnp.concatenate(
            [
                jnp.concatenate([real, -imaginary], axis=1),
                jnp.concatenate([imaginary, real], axis=1),
            ],
            axis=0,
        )
        image = jnp.dot(middle[0, s], right, preferred_element_type=F32)
        image = image + jnp.dot(middle[1, s], right, preferred_element_type=F32)
        image = image.astype(BF16)
        for a in range(operators):
            for part in range(2):
                rows = image[a * block_rows : (a + 1) * block_rows]
                low = rows[:, part * vectors : part * vectors + LANES]
                high = rows[:, part * vectors + LANES : (part + 1) * vectors]
                keep_ref[s, part, a] = jnp.where(half == 0, low, high)
                send_refs[s // each][s % each, part, a] = jnp.where(half == 0, high, low)


def both_sides(elements, others, perams):
    blocks = len(perams)
    sources, _, block_rows, vectors = perams[0].shape
    operators = elements.shape[0]
    piece = jax.ShapeDtypeStruct((sources, 2, operators, block_rows, LANES), BF16)
    sends = 2 - sources % 2
    part = jax.ShapeDtypeStruct((sources // sends,) + piece.shape[1:], BF16)
    return pl.pallas_call(
        functools.partial(both_kernel, blocks),
        out_shape=(piece,) + (part,) * sends,
        in_specs=[VMEM] * (2 + blocks),
        out_specs=(VMEM,) * (1 + sends),
        scratch_shapes=[
            pltpu.VMEM((sources, 2, vectors, vectors), BF16),
            pltpu.VMEM((sources, 2, vectors, vectors), BF16),
            pltpu.VMEM((2 * sources * block_rows, vectors), BF16),
            pltpu.VMEM((2, sources, operators * block_rows, 2 * vectors), BF16),
        ],
        compiler_params=params(16),
        cost_estimate=pl.CostEstimate(flops=0, bytes_accessed=0, transcendentals=0),
        name="both_sides",
    )(elements, others, *perams)


def spread(wide, count_rows, block_rows):
    fold = block_rows // GROUPS
    pieces = [
        wide[pl.ds(k, count_rows * GROUPS, stride=fold), :].astype(BF16) for k in range(fold)
    ]
    return jnp.concatenate(pieces, axis=1)


def lay_kernel(own_ref, *refs):
    pair_refs, out_ref, wide = refs[:-2], refs[-2], refs[-1]
    each = own_ref.shape[0] // len(pair_refs)
    sources, _, operators, block_rows, lanes = own_ref.shape
    rows = 2 * operators
    for s in range(sources):
        for at, ref in enumerate((own_ref.at[s], pair_refs[s // each].at[s % each])):
            wide[pl.ds(at * rows * block_rows, rows * block_rows), :] = (
                ref[...].astype(F32).reshape(rows * block_rows, lanes)
            )
        out_ref[s] = spread(wide, 2 * rows, block_rows)


def lay_out(own, pair):
    sources, _, operators, block_rows, lanes = own.shape
    rows = 2 * operators
    return pl.pallas_call(
        lay_kernel,
        out_shape=jax.ShapeDtypeStruct(
            (sources, 2 * rows * GROUPS, block_rows // GROUPS * lanes), BF16
        ),
        in_specs=[VMEM] * (1 + len(pair)),
        out_specs=VMEM,
        scratch_shapes=[pltpu.VMEM((2 * rows * block_rows, lanes), F32)],
        compiler_params=params(12),
        cost_estimate=pl.CostEstimate(flops=0, bytes_accessed=0, transcendentals=0),
        name="lay_out",
    )(own, *pair)


def trace_kernel(count, table, line, times_ref, *refs):
    pools = refs[:count]
    laid_ref, out_ref, picked = refs[count:]
    sources = laid_ref.shape[0]
    groups = GROUPS
    rows = pools[0].shape[0] // groups
    time = lax.axis_index("tm")
    for s in range(sources):
        source = times_ref[s]
        code = line_code(time // 2, source // 2, lax.rem(source + time, 2), line)
        for index, (at, inside) in table.items():

            @pl.when(code == index)
            def _(at=at, inside=inside, s=s):
                block = pools[at] if inside is None else pools[at].at[inside]
                picked[s] = block[...]

    shape = (2 * rows * groups, rows * groups)
    down = lax.broadcasted_iota(jnp.int32, shape, 0)
    over = lax.broadcasted_iota(jnp.int32, shape, 1)
    same = down % groups == over % groups
    shape = (rows * groups, rows)
    down = lax.broadcasted_iota(jnp.int32, shape, 0)
    over = lax.broadcasted_iota(jnp.int32, shape, 1)
    gather = (down // groups == over).astype(F32)
    sums = []
    for s in range(sources):
        product = lax.dot_general(
            laid_ref[s],
            picked[s],
            (((1,), (1,)), ((), ())),
            preferred_element_type=F32,
        )
        product = jnp.where(same, product, 0.0).reshape(2 * rows, groups, rows * groups)
        sums.append(jnp.sum(product, axis=1))
    folded = jnp.dot(
        jnp.concatenate(sums, axis=0),
        gather,
        precision=lax.Precision.HIGHEST,
        preferred_element_type=F32,
    )
    for s in range(sources):
        out_ref[0, s] = folded[2 * rows * s : 2 * rows * s + rows]
        out_ref[1, s] = folded[2 * rows * s + rows : 2 * rows * (s + 1)]


def traces(source_times, pools, table, line, laid):
    sources = laid.shape[0]
    rows = pools[0].shape[0] // GROUPS
    return pl.pallas_call(
        functools.partial(trace_kernel, len(pools), table, line),
        out_shape=jax.ShapeDtypeStruct((2, sources, rows, rows), F32),
        in_specs=[SMEM] + [VMEM] * (len(pools) + 1),
        out_specs=VMEM,
        scratch_shapes=[
            pltpu.VMEM((sources,) + pools[0].shape, BF16),
        ],
        compiler_params=params(12),
        cost_estimate=pl.CostEstimate(
            flops=4 * laid.size * rows,
            bytes_accessed=2 * laid.size,
            transcendentals=0,
        ),
        name="traces",
    )(source_times, *pools, laid)


def finish_kernel(count, *refs):
    parts = refs[:count]
    correlator_ref, pairs_ref = refs[count:]
    sources, rows, _ = parts[1].shape
    n = rows // 2
    eye = lax.broadcasted_iota(jnp.int32, (n, n), 0) == lax.broadcasted_iota(jnp.int32, (n, n), 1)
    for s in range(sources):
        terms = [parts[0][0, s]] + [ref[s] for ref in parts[1:]]
        while len(terms) > 1:
            terms = [one + two for one, two in zip(terms[::2], terms[1::2])]
        total = terms[0]
        real = total[:n, :n] - total[n:, n:]
        imaginary = total[:n, n:] + total[n:, :n]
        correlator_ref[0, s, :, 0, :] = real
        correlator_ref[0, s, :, 1, :] = imaginary
        down_real, down_imaginary, over_real, over_imaginary = (
            jnp.sum(jnp.where(eye, block, 0.0), axis=axis, keepdims=True)
            for axis in (1, 0)
            for block in (real, imaginary)
        )
        pairs_ref[0, s, :, 0, :] = down_real * over_real - down_imaginary * over_imaginary
        pairs_ref[0, s, :, 1, :] = down_real * over_imaginary + down_imaginary * over_real


def finish(parts):
    sources, rows, _ = parts[1].shape
    result = jax.ShapeDtypeStruct((1, sources, rows // 2, 2, rows // 2), F32)
    correlator, pairs = pl.pallas_call(
        functools.partial(finish_kernel, len(parts)),
        out_shape=(result, result),
        in_specs=[VMEM] * len(parts),
        out_specs=(VMEM, VMEM),
        compiler_params=params(4),
        name="finish",
    )(*parts)
    return jnp.swapaxes(correlator, 2, 3), jnp.swapaxes(pairs, 2, 3)


def phase_tables(momenta, z_coords, z_extent):
    plane = jnp.arange(PLANE, dtype=jnp.int32)
    along_x = (momenta[:, 0:1] * (plane % LX)[None] % LX).astype(F32) * (2.0 * math.pi / LX)
    along_y = (momenta[:, 1:2] * (plane // LX)[None] % LY).astype(F32) * (2.0 * math.pi / LY)
    angle = along_x + along_y
    table = jnp.stack([jnp.cos(angle), jnp.sin(angle)], axis=1).reshape(-1, PLANE)
    along_z = (momenta[:, 2][None, :] * z_coords[:, None] % z_extent).astype(F32) * (
        2.0 * math.pi / z_extent
    )
    return table, jnp.stack([jnp.cos(along_z), jnp.sin(along_z)])


def body(eigenvectors, momenta, displacement, source_times, perambulators):
    _, parts, colours, _, plane, vectors = eigenvectors.shape
    slabs = lax.axis_size("space")
    line = lax.axis_size("tm") // 2
    block_rows = vectors // slabs
    near = 2

    own = eigenvectors.reshape(parts, colours, plane, vectors)
    beside = swap_bit(own, "space", 1)
    keys = swap_far(own)

    plane_phase, z_phase = phase_tables(momenta, jnp.arange(slabs, dtype=jnp.int32), slabs)
    tables = (displacement, z_phase, plane_phase)
    total, wide_phase = elementals(tables, [own, beside], near, None, block_rows)

    keys, total = lax.optimization_barrier((keys, total))
    slab_list = swap_near(keys)
    slab_list[1] = beside
    peram, _ = lax.optimization_barrier((perambulators[0], keys[slabs // 2]))
    perams = swap_far(peram)
    tables = (displacement, z_phase, wide_phase)
    full, keep, send = elementals(tables, slab_list, near, total, block_rows)

    perams, full, send = lax.optimization_barrier((perams, full, send))
    perams = swap_near(perams)

    received = swap_bit(send, "tm", 1)
    g_keep, *g_send = both_sides(full, swap_bit(full, "space", 1), perams)
    arrays, table, g_send = share_line(keep, received, g_send, line)
    laid = lay_out(g_keep, [swap_bit(block, "tm", 1) for block in g_send])
    both = traces(source_times, arrays, table, line, laid)
    both = both + swap_bit(both, "space", 1)
    mine, pair = both[0], both[1]
    near_sums = [swap_bit(mine, "space", mask) for mask in range(2, slabs, 2)]
    pair_sums = [swap_bit(pair, "tm", 1)]
    pair_sums += [across(pair, mask) for mask in range(2, slabs, 2)]
    return finish([both] + near_sums + pair_sums)


def across(block, mask):
    rows, times = lax.axis_size("space"), lax.axis_size("tm")
    route = [
        (i * times + t, (i ^ mask) * times + (t ^ 1)) for i in range(rows) for t in range(times)
    ]
    return lax.ppermute(block, ("space", "tm"), route)


def solution(mesh):
    placed = (
        P("tm", None, None, "space", None, None),
        P(),
        P(),
        P(),
        P("tm", None, None, "space", None),
    )
    return jax.shard_map(
        body,
        mesh=mesh,
        in_specs=placed,
        out_specs=(P("tm", None, None, None, None), P("tm", None, None, None, None)),
        check_vma=False,
    )
```

```python
import functools
import math

import jax
import jax.numpy as jnp
from jax import lax
from jax.experimental import pallas as pl
from jax.experimental.pallas import tpu as pltpu
from jax.sharding import PartitionSpec as P

LX = 16
LY = 16
PLANE = LX * LY
LANES = 128
F32 = jnp.float32
BF16 = jnp.bfloat16
CHUNK = 32
GROUPS = 8
MEGA = 1024 * 1024

SMEM = pl.BlockSpec(memory_space=pltpu.SMEM)
VMEM = pl.BlockSpec(memory_space=pltpu.VMEM)


def swap_bit(block, axis, mask):
    count = lax.axis_size(axis)
    return lax.ppermute(block, axis, [(i, i ^ mask) for i in range(count)])


def along_line(block, moves):
    route = [(2 * z + x, 2 * to + x) for z, to in moves.items() for x in range(2)]
    return lax.ppermute(block, "tm", route)


def share_line(keep, received, g_send, line):
    piece = jnp.stack([keep, received])
    if line != 4:
        arrays, table = [keep, received], {0: (0, None), 1: (1, None)}
        for distance in range(1, line):
            moved = along_line(piece, {z: (z + distance) % line for z in range(line)})
            for side in range(2):
                table[2 * distance + side] = (len(arrays), side)
            arrays.append(moved)
        return arrays, table, g_send
    outward = {1: 0, 2: 3}
    piece = jnp.stack([keep, received])
    opposite = along_line(piece, {1: 2, 2: 1, 0: 3, 3: 0})
    skip = along_line(piece, {0: 2, 3: 1})
    near = along_line(piece, {0: 1, 1: 0, 2: 3, 3: 2})
    passed = along_line(opposite, outward)
    arrays = [keep, received, near, skip, opposite, passed]
    table = {0: (0, None), 1: (1, None)}
    for code in range(2, 10):
        table[code] = (1 + code // 2, code % 2)
    return arrays, table, g_send


def line_code(here, there, side, line):
    if line != 4:
        return 2 * lax.rem(here - there + line, line) + side
    apart = here ^ there
    ends = (here == 0) | (here == line - 1)
    return 2 * jnp.where(ends & (apart == 2), 4, apart) + side


def swap_far(block):
    held = {0: block}
    mask = lax.axis_size("space") // 2
    while mask >= 2:
        for key in sorted(held):
            held[key | mask] = swap_bit(held[key], "space", mask)
        mask //= 2
    return held


def swap_near(held):
    both = dict(held)
    for key in sorted(held):
        both[key | 1] = swap_bit(held[key], "space", 1)
    return [both[key] for key in sorted(both)]


def params(megabytes):
    return pltpu.CompilerParams(vmem_limit_bytes=megabytes * MEGA)


def elemental_kernel(held, near, late, block_rows, *refs):
    move_ref, zphase_ref = refs[:2]
    slab_refs = refs[2 : 2 + held]
    rest = refs[2 + held :]
    if not late:
        phase_ref, rest = rest[0], rest[1:]
    if late:
        table, prior_ref, acc_out, keep_ref, send_ref = rest[:5]
        slabs, turned, mixed_a, mixed_b, todo, acc, wide = rest[5:]
    else:
        acc, table, slabs, turned, mixed_a, mixed_b, todo = rest
    operators, half_rows, vectors = acc.shape
    half_rows //= 2
    colours = turned.shape[0]
    count = lax.axis_size("space")
    me = lax.axis_index("space")
    core = lax.rem(me, 2)

    for m in range(held):
        slabs[m, :, :, pl.ds(0, PLANE), :] = slab_refs[m][...]
        slabs[m, :, :, pl.ds(PLANE, LX), :] = slab_refs[m][:, :, pl.ds(0, LX), :]
    acc[...] = prior_ref[...] if late else jnp.zeros_like(acc)
    if not late:
        upright = phase_ref[...].T
        for o in range(operators):
            for part in range(2):
                at = 2 * o + part
                table[o, part] = jnp.broadcast_to(upright[:, at : at + 1], (PLANE, LANES))
    def one_slab(m, carry):
        here = me ^ m
        above = lax.rem(here + 1, count) ^ me
        far = above >= near

        def collect(o, found):
            waits = (m >= near) | ((move_ref[o] == 3) & far)
            chosen = waits if late else jnp.logical_not(waits)

            @pl.when(chosen)
            def _():
                todo[found] = o

            return found + chosen.astype(jnp.int32)

        def turn_phases(o, mixed, colour):
            move = move_ref[o]
            src = jnp.where(move == 3, above, jnp.where(move == 1, held, m))
            off = pl.multiple_of(jnp.where(move == 2, LX, 0), LX)
            cos_z, sin_z = zphase_ref[0, here, o], zphase_ref[1, here, o]
            for begin in range(0, PLANE, CHUNK):
                cos_p = table[o, 0, pl.ds(begin, CHUNK), :]
                sin_p = table[o, 1, pl.ds(begin, CHUNK), :]
                cosine = cos_p * cos_z - sin_p * sin_z
                sine = sin_p * cos_z + cos_p * sin_z
                cosine = jnp.concatenate([cosine] * (vectors // LANES), axis=1)
                sine = jnp.concatenate([sine] * (vectors // LANES), axis=1)
                real = slabs[src, 0, colour, pl.ds(off + begin, CHUNK), :].astype(F32)
                imag = slabs[src, 1, colour, pl.ds(off + begin, CHUNK), :].astype(F32)
                mixed[colour, pl.ds(begin, CHUNK), :] = (cosine * real + sine * imag).astype(BF16)
                mixed[colour, pl.ds(PLANE + begin, CHUNK), :] = (
                    cosine * imag - sine * real
                ).astype(BF16)

        def step(o, mixed, later, following):
            total = None
            for colour in range(colours):
                turn_phases(later, following, colour)
            for colour in range(colours):
                term = jnp.dot(turned[colour], mixed[colour], preferred_element_type=F32)
                total = term if total is None else total + term
            acc[o] += total

        found = lax.fori_loop(0, operators, collect, jnp.int32(0))

        @pl.when((found > 0) & (m >= near if late else m >= 0))
        def _():
            for colour in range(colours):
                for part in range(2):
                    for begin in range(0, PLANE, CHUNK):
                        rows = slabs[m, part, colour, pl.ds(begin, CHUNK), :].astype(F32)
                        rows = pltpu.roll(rows.reshape(CHUNK // LX, LX, vectors), LX - 1, 1)
                        slabs[held, part, colour, pl.ds(begin, CHUNK), :] = rows.reshape(
                            CHUNK, vectors
                        ).astype(BF16)

        @pl.when(found > 0)
        def _():
            for colour in range(colours):
                for part in range(2):
                    block = slabs[m, part, colour, pl.ds(0, PLANE), :]
                    flat = block.T.reshape(half_rows // block_rows, 2, block_rows, PLANE)
                    flat = jnp.where(core == 0, flat[:, 0], flat[:, 1]).reshape(half_rows, PLANE)
                    same = flat if part == 0 else -flat
                    lower = pl.ds(half_rows, half_rows)
                    turned[colour, pl.ds(0, half_rows), pl.ds(part * PLANE, PLANE)] = flat
                    turned[colour, lower, pl.ds((1 - part) * PLANE, PLANE)] = same
            for colour in range(colours):
                turn_phases(todo[0], mixed_a, colour)

            def two(i, inner):
                step(todo[2 * i], mixed_a, todo[jnp.minimum(2 * i + 1, found - 1)], mixed_b)

                @pl.when(2 * i + 1 < found)
                def _():
                    after = todo[jnp.minimum(2 * i + 2, found - 1)]
                    step(todo[2 * i + 1], mixed_b, after, mixed_a)

                return inner

            lax.fori_loop(0, (found + 1) // 2, two, 0)

        return carry

    lax.fori_loop(0, held, one_slab, 0)

    if late:
        first = pl.multiple_of(me // 2 * block_rows, block_rows)
        half = lax.rem(lax.axis_index("tm"), 2)
        for o in range(operators):
            acc_out[o] = acc[o].astype(BF16)
        for part in range(2):
            for o in range(operators):
                rows = pl.ds(part * half_rows + first, block_rows)
                own = acc[o, rows, :]
                at = pl.ds((part * operators + o) * block_rows, block_rows)
                wide[0, at, :] = own[:, :LANES]
                wide[1, at, :] = own[:, LANES:]
        keep_ref[...] = spread(wide.at[half], 2 * operators, block_rows)
        send_ref[...] = spread(wide.at[1 - half], 2 * operators, block_rows)


def elementals(tables, slab_list, near, prior, block_rows):
    _, colours, plane, vectors = slab_list[0].shape
    held = len(slab_list)
    operators = tables[0].shape[0]
    late = prior is not None
    wide = jax.ShapeDtypeStruct((operators, vectors, vectors), F32)
    scratch = [
        pltpu.VMEM((held + 1, 2, colours, plane + LX, vectors), BF16),
        pltpu.VMEM((colours, vectors, 2 * plane), BF16),
        pltpu.VMEM((colours, 2 * plane, vectors), BF16),
        pltpu.VMEM((colours, 2 * plane, vectors), BF16),
        pltpu.SMEM((operators,), jnp.int32),
    ]
    if late:
        piece = jax.ShapeDtypeStruct(
            (2 * operators * GROUPS, block_rows // GROUPS * LANES), BF16
        )
        outs = (jax.ShapeDtypeStruct(wide.shape, BF16), piece, piece)
        out_specs = (VMEM, VMEM, VMEM)
        scratch.append(pltpu.VMEM(wide.shape, F32))
        scratch.append(pltpu.VMEM((2, 2 * operators * block_rows, LANES), F32))
    else:
        outs = (wide, jax.ShapeDtypeStruct((operators, 2, plane, LANES), F32))
        out_specs = (VMEM, VMEM)
    move, z_phase, phases = tables
    priors = [phases, prior] if late else [phases]
    return pl.pallas_call(
        functools.partial(elemental_kernel, held, near, late, block_rows),
        out_shape=outs,
        in_specs=[SMEM, SMEM] + [VMEM] * (held + len(priors)),
        out_specs=out_specs,
        scratch_shapes=scratch,
        compiler_params=params(20 + held),
        cost_estimate=pl.CostEstimate(
            flops=8 * held * operators * colours * plane * vectors * vectors,
            bytes_accessed=held * 2 * colours * plane * vectors * 2,
            transcendentals=0,
        ),
        name="elementals_late" if late else "elementals_early",
    )(move, z_phase, *slab_list, *priors)


def both_kernel(blocks, e_ref, other_ref, *refs):
    peram_refs = refs[:blocks]
    keep_ref, rest = refs[blocks], refs[blocks + 1 :]
    whole, sorted_rows, left, middle = rest[-4:]
    send_refs = rest[:-4]
    each = keep_ref.shape[0] // len(send_refs)
    sources, _, vectors, _ = whole.shape
    operators = e_ref.shape[0]
    block_rows = keep_ref.shape[3]
    me = lax.axis_index("space")
    half = lax.rem(lax.axis_index("tm"), 2)
    for m in range(blocks):
        begin = pl.multiple_of((me ^ m) * block_rows, block_rows)
        whole[:, :, pl.ds(begin, block_rows), :] = peram_refs[m][...]
        begin = (m % 2) * (vectors // 2) + (me ^ m) // 2 * block_rows
        begin = pl.multiple_of(begin, block_rows)
        sorted_rows[:, :, pl.ds(begin, block_rows), :] = peram_refs[m][...]
    row = lax.broadcasted_iota(jnp.int32, (block_rows, vectors), 0)
    column = lax.broadcasted_iota(jnp.int32, (block_rows, vectors), 1)
    chosen = (column == row + me * block_rows).astype(F32).astype(BF16)
    for s in range(sources):
        for part in range(2):
            flat = lax.dot_general(
                chosen, whole[s, part], (((1,), (1,)), ((), ())), preferred_element_type=F32
            )
            left[pl.ds((part * sources + s) * block_rows, block_rows), :] = flat.astype(BF16)
    group = sources * block_rows
    cut = vectors // 2
    for a in range(operators):
        sides = []
        for ref in (e_ref, other_ref):
            product = lax.dot_general(
                left[...], ref[a], (((1,), (1,)), ((), ())), preferred_element_type=F32
            )
            sides.append(
                (
                    product[:group, :cut] - product[group:, cut:],
                    product[:group, cut:] + product[group:, :cut],
                )
            )
        real, imaginary = (
            jnp.concatenate([one, two], axis=1) for one, two in zip(*sides)
        )
        for part, block in enumerate((real, imaginary)):
            high = block.astype(BF16)
            low = (block - high.astype(F32)).astype(BF16)
            for s in range(sources):
                base = s * block_rows
                rows = pl.ds(a * block_rows, block_rows)
                columns = pl.ds(part * vectors, vectors)
                middle[0, s, rows, columns] = high[base : base + block_rows]
                middle[1, s, rows, columns] = low[base : base + block_rows]
    for s in range(sources):
        real, imaginary = sorted_rows[s, 0], sorted_rows[s, 1]
        right = jnp.concatenate(
            [
                jnp.concatenate([real, -imaginary], axis=1),
                jnp.concatenate([imaginary, real], axis=1),
            ],
            axis=0,
        )
        image = jnp.dot(middle[0, s], right, preferred_element_type=F32)
        image = image + jnp.dot(middle[1, s], right, preferred_element_type=F32)
        image = image.astype(BF16)
        for a in range(operators):
            for part in range(2):
                rows = image[a * block_rows : (a + 1) * block_rows]
                low = rows[:, part * vectors : part * vectors + LANES]
                high = rows[:, part * vectors + LANES : (part + 1) * vectors]
                keep_ref[s, part, a] = jnp.where(half == 0, low, high)
                send_refs[s // each][s % each, part, a] = jnp.where(half == 0, high, low)


def both_sides(elements, others, perams):
    blocks = len(perams)
    sources, _, block_rows, vectors = perams[0].shape
    operators = elements.shape[0]
    piece = jax.ShapeDtypeStruct((sources, 2, operators, block_rows, LANES), BF16)
    sends = 2 - sources % 2
    part = jax.ShapeDtypeStruct((sources // sends,) + piece.shape[1:], BF16)
    return pl.pallas_call(
        functools.partial(both_kernel, blocks),
        out_shape=(piece,) + (part,) * sends,
        in_specs=[VMEM] * (2 + blocks),
        out_specs=(VMEM,) * (1 + sends),
        scratch_shapes=[
            pltpu.VMEM((sources, 2, vectors, vectors), BF16),
            pltpu.VMEM((sources, 2, vectors, vectors), BF16),
            pltpu.VMEM((2 * sources * block_rows, vectors), BF16),
            pltpu.VMEM((2, sources, operators * block_rows, 2 * vectors), BF16),
        ],
        compiler_params=params(16),
        cost_estimate=pl.CostEstimate(flops=0, bytes_accessed=0, transcendentals=0),
        name="both_sides",
    )(elements, others, *perams)


def spread(wide, count_rows, block_rows):
    fold = block_rows // GROUPS
    pieces = [
        wide[pl.ds(k, count_rows * GROUPS, stride=fold), :].astype(BF16) for k in range(fold)
    ]
    return jnp.concatenate(pieces, axis=1)


def lay_kernel(own_ref, *refs):
    pair_refs, out_ref, wide = refs[:-2], refs[-2], refs[-1]
    each = own_ref.shape[0] // len(pair_refs)
    sources, _, operators, block_rows, lanes = own_ref.shape
    rows = 2 * operators
    for s in range(sources):
        for at, ref in enumerate((own_ref.at[s], pair_refs[s // each].at[s % each])):
            wide[pl.ds(at * rows * block_rows, rows * block_rows), :] = (
                ref[...].astype(F32).reshape(rows * block_rows, lanes)
            )
        out_ref[s] = spread(wide, 2 * rows, block_rows)


def lay_out(own, pair):
    sources, _, operators, block_rows, lanes = own.shape
    rows = 2 * operators
    return pl.pallas_call(
        lay_kernel,
        out_shape=jax.ShapeDtypeStruct(
            (sources, 2 * rows * GROUPS, block_rows // GROUPS * lanes), BF16
        ),
        in_specs=[VMEM] * (1 + len(pair)),
        out_specs=VMEM,
        scratch_shapes=[pltpu.VMEM((2 * rows * block_rows, lanes), F32)],
        compiler_params=params(12),
        cost_estimate=pl.CostEstimate(flops=0, bytes_accessed=0, transcendentals=0),
        name="lay_out",
    )(own, *pair)


def trace_kernel(count, table, line, times_ref, *refs):
    pools = refs[:count]
    laid_ref, out_ref, picked = refs[count:]
    sources = laid_ref.shape[0]
    groups = GROUPS
    rows = pools[0].shape[0] // groups
    time = lax.axis_index("tm")
    for s in range(sources):
        source = times_ref[s]
        code = line_code(time // 2, source // 2, lax.rem(source + time, 2), line)
        for index, (at, inside) in table.items():

            @pl.when(code == index)
            def _(at=at, inside=inside, s=s):
                block = pools[at] if inside is None else pools[at].at[inside]
                picked[s] = block[...]

    shape = (2 * rows * groups, rows * groups)
    down = lax.broadcasted_iota(jnp.int32, shape, 0)
    over = lax.broadcasted_iota(jnp.int32, shape, 1)
    same = down % groups == over % groups
    shape = (rows * groups, rows)
    down = lax.broadcasted_iota(jnp.int32, shape, 0)
    over = lax.broadcasted_iota(jnp.int32, shape, 1)
    gather = (down // groups == over).astype(F32)
    sums = []
    for s in range(sources):
        product = lax.dot_general(
            laid_ref[s],
            picked[s],
            (((1,), (1,)), ((), ())),
            preferred_element_type=F32,
        )
        product = jnp.where(same, product, 0.0).reshape(2 * rows, groups, rows * groups)
        sums.append(jnp.sum(product, axis=1))
    folded = jnp.dot(
        jnp.concatenate(sums, axis=0),
        gather,
        precision=lax.Precision.HIGHEST,
        preferred_element_type=F32,
    )
    for s in range(sources):
        out_ref[0, s] = folded[2 * rows * s : 2 * rows * s + rows]
        out_ref[1, s] = folded[2 * rows * s + rows : 2 * rows * (s + 1)]


def traces(source_times, pools, table, line, laid):
    sources = laid.shape[0]
    rows = pools[0].shape[0] // GROUPS
    return pl.pallas_call(
        functools.partial(trace_kernel, len(pools), table, line),
        out_shape=jax.ShapeDtypeStruct((2, sources, rows, rows), F32),
        in_specs=[SMEM] + [VMEM] * (len(pools) + 1),
        out_specs=VMEM,
        scratch_shapes=[
            pltpu.VMEM((sources,) + pools[0].shape, BF16),
        ],
        compiler_params=params(12),
        cost_estimate=pl.CostEstimate(
            flops=4 * laid.size * rows,
            bytes_accessed=2 * laid.size,
            transcendentals=0,
        ),
        name="traces",
    )(source_times, *pools, laid)


def finish_kernel(count, *refs):
    parts = refs[:count]
    correlator_ref, pairs_ref = refs[count:]
    sources, rows, _ = parts[1].shape
    n = rows // 2
    eye = lax.broadcasted_iota(jnp.int32, (n, n), 0) == lax.broadcasted_iota(jnp.int32, (n, n), 1)
    for s in range(sources):
        terms = [parts[0][0, s]] + [ref[s] for ref in parts[1:]]
        while len(terms) > 1:
            terms = [one + two for one, two in zip(terms[::2], terms[1::2])]
        total = terms[0]
        real = total[:n, :n] - total[n:, n:]
        imaginary = total[:n, n:] + total[n:, :n]
        correlator_ref[0, s, :, 0, :] = real
        correlator_ref[0, s, :, 1, :] = imaginary
        down_real, down_imaginary, over_real, over_imaginary = (
            jnp.sum(jnp.where(eye, block, 0.0), axis=axis, keepdims=True)
            for axis in (1, 0)
            for block in (real, imaginary)
        )
        pairs_ref[0, s, :, 0, :] = down_real * over_real - down_imaginary * over_imaginary
        pairs_ref[0, s, :, 1, :] = down_real * over_imaginary + down_imaginary * over_real


def finish(parts):
    sources, rows, _ = parts[1].shape
    result = jax.ShapeDtypeStruct((1, sources, rows // 2, 2, rows // 2), F32)
    correlator, pairs = pl.pallas_call(
        functools.partial(finish_kernel, len(parts)),
        out_shape=(result, result),
        in_specs=[VMEM] * len(parts),
        out_specs=(VMEM, VMEM),
        compiler_params=params(4),
        name="finish",
    )(*parts)
    return jnp.swapaxes(correlator, 2, 3), jnp.swapaxes(pairs, 2, 3)


def phase_tables(momenta, z_coords, z_extent):
    plane = jnp.arange(PLANE, dtype=jnp.int32)
    along_x = (momenta[:, 0:1] * (plane % LX)[None] % LX).astype(F32) * (2.0 * math.pi / LX)
    along_y = (momenta[:, 1:2] * (plane // LX)[None] % LY).astype(F32) * (2.0 * math.pi / LY)
    angle = along_x + along_y
    table = jnp.stack([jnp.cos(angle), jnp.sin(angle)], axis=1).reshape(-1, PLANE)
    along_z = (momenta[:, 2][None, :] * z_coords[:, None] % z_extent).astype(F32) * (
        2.0 * math.pi / z_extent
    )
    return table, jnp.stack([jnp.cos(along_z), jnp.sin(along_z)])


def body(eigenvectors, momenta, displacement, source_times, perambulators):
    _, parts, colours, _, plane, vectors = eigenvectors.shape
    slabs = lax.axis_size("space")
    line = lax.axis_size("tm") // 2
    block_rows = vectors // slabs
    near = 2

    own = eigenvectors.reshape(parts, colours, plane, vectors)
    beside = swap_bit(own, "space", 1)
    keys = swap_far(own)

    plane_phase, z_phase = phase_tables(momenta, jnp.arange(slabs, dtype=jnp.int32), slabs)
    tables = (displacement, z_phase, plane_phase)
    total, wide_phase = elementals(tables, [own, beside], near, None, block_rows)

    keys, total = lax.optimization_barrier((keys, total))
    slab_list = swap_near(keys)
    slab_list[1] = beside
    peram, _ = lax.optimization_barrier((perambulators[0], keys[slabs // 2]))
    perams = swap_far(peram)
    tables = (displacement, z_phase, wide_phase)
    full, keep, send = elementals(tables, slab_list, near, total, block_rows)

    perams, full, send = lax.optimization_barrier((perams, full, send))
    perams = swap_near(perams)

    received = swap_bit(send, "tm", 1)
    g_keep, *g_send = both_sides(full, swap_bit(full, "space", 1), perams)
    arrays, table, g_send = share_line(keep, received, g_send, line)
    laid = lay_out(g_keep, [swap_bit(block, "tm", 1) for block in g_send])
    both = traces(source_times, arrays, table, line, laid)
    both = both + swap_bit(both, "space", 1)
    mine, pair = both[0], both[1]
    near_sums = [swap_bit(mine, "space", mask) for mask in range(2, slabs, 2)]
    pair_sums = [swap_bit(pair, "tm", 1)]
    pair_sums += [across(pair, mask) for mask in range(2, slabs, 2)]
    return finish([both] + near_sums + pair_sums)


def across(block, mask):
    rows, times = lax.axis_size("space"), lax.axis_size("tm")
    route = [
        (i * times + t, (i ^ mask) * times + (t ^ 1)) for i in range(rows) for t in range(times)
    ]
    return lax.ppermute(block, ("space", "tm"), route)


def solution(mesh):
    placed = (
        P("tm", None, None, "space", None, None),
        P(),
        P(),
        P(),
        P("tm", None, None, "space", None),
    )
    return jax.shard_map(
        body,
        mesh=mesh,
        in_specs=placed,
        out_specs=(P("tm", None, None, None, None), P("tm", None, None, None, None)),
        check_vma=False,
    )
```

```python
import functools
import math

import jax
import jax.numpy as jnp
from jax import lax
from jax.experimental import pallas as pl
from jax.experimental.pallas import tpu as pltpu
from jax.sharding import PartitionSpec as P

LX = 16
LY = 16
PLANE = LX * LY
LANES = 128
F32 = jnp.float32
BF16 = jnp.bfloat16
CHUNK = 32
GROUPS = 8
MEGA = 1024 * 1024

SMEM = pl.BlockSpec(memory_space=pltpu.SMEM)
VMEM = pl.BlockSpec(memory_space=pltpu.VMEM)


def swap_bit(block, axis, mask):
    count = lax.axis_size(axis)
    return lax.ppermute(block, axis, [(i, i ^ mask) for i in range(count)])


def along_line(block, moves):
    route = [(2 * z + x, 2 * to + x) for z, to in moves.items() for x in range(2)]
    return lax.ppermute(block, "tm", route)


def share_line(keep, received, g_send, line):
    piece = jnp.stack([keep, received])
    if line != 4:
        arrays, table = [keep, received], {0: (0, None), 1: (1, None)}
        for distance in range(1, line):
            moved = along_line(piece, {z: (z + distance) % line for z in range(line)})
            for side in range(2):
                table[2 * distance + side] = (len(arrays), side)
            arrays.append(moved)
        return arrays, table, g_send
    outward = {1: 0, 2: 3}
    piece = jnp.stack([keep, received])
    opposite = along_line(piece, {1: 2, 2: 1, 0: 3, 3: 0})
    skip = along_line(piece, {0: 2, 3: 1})
    near = along_line(piece, {0: 1, 1: 0, 2: 3, 3: 2})
    passed = along_line(opposite, outward)
    arrays = [keep, received, near, skip, opposite, passed]
    table = {0: (0, None), 1: (1, None)}
    for code in range(2, 10):
        table[code] = (1 + code // 2, code % 2)
    return arrays, table, g_send


def line_code(here, there, side, line):
    if line != 4:
        return 2 * lax.rem(here - there + line, line) + side
    apart = here ^ there
    ends = (here == 0) | (here == line - 1)
    return 2 * jnp.where(ends & (apart == 2), 4, apart) + side


def swap_far(block):
    held = {0: block}
    mask = lax.axis_size("space") // 2
    while mask >= 2:
        for key in sorted(held):
            held[key | mask] = swap_bit(held[key], "space", mask)
        mask //= 2
    return held


def swap_near(held):
    both = dict(held)
    for key in sorted(held):
        both[key | 1] = swap_bit(held[key], "space", 1)
    return [both[key] for key in sorted(both)]


def params(megabytes):
    return pltpu.CompilerParams(vmem_limit_bytes=megabytes * MEGA)


def elemental_kernel(held, near, late, block_rows, *refs):
    move_ref, zphase_ref = refs[:2]
    slab_refs = refs[2 : 2 + held]
    rest = refs[2 + held :]
    if not late:
        phase_ref, rest = rest[0], rest[1:]
    if late:
        table, prior_ref, acc_out, keep_ref, send_ref = rest[:5]
        slabs, turned, mixed_a, mixed_b, todo, acc, wide = rest[5:]
    else:
        acc, table, slabs, turned, mixed_a, mixed_b, todo = rest
    operators, half_rows, vectors = acc.shape
    half_rows //= 2
    colours = turned.shape[0]
    count = lax.axis_size("space")
    me = lax.axis_index("space")
    core = lax.rem(me, 2)

    for m in range(held):
        slabs[m, :, :, pl.ds(0, PLANE), :] = slab_refs[m][...]
        slabs[m, :, :, pl.ds(PLANE, LX), :] = slab_refs[m][:, :, pl.ds(0, LX), :]
    acc[...] = prior_ref[...] if late else jnp.zeros_like(acc)
    if not late:
        upright = phase_ref[...].T
        for o in range(operators):
            for part in range(2):
                at = 2 * o + part
                table[o, part] = jnp.broadcast_to(upright[:, at : at + 1], (PLANE, LANES))
    def one_slab(m, carry):
        here = me ^ m
        above = lax.rem(here + 1, count) ^ me
        far = above >= near

        def collect(o, found):
            waits = (m >= near) | ((move_ref[o] == 3) & far)
            chosen = waits if late else jnp.logical_not(waits)

            @pl.when(chosen)
            def _():
                todo[found] = o

            return found + chosen.astype(jnp.int32)

        def turn_phases(o, mixed, colour):
            move = move_ref[o]
            src = jnp.where(move == 3, above, jnp.where(move == 1, held, m))
            off = pl.multiple_of(jnp.where(move == 2, LX, 0), LX)
            cos_z, sin_z = zphase_ref[0, here, o], zphase_ref[1, here, o]
            for begin in range(0, PLANE, CHUNK):
                cos_p = table[o, 0, pl.ds(begin, CHUNK), :]
                sin_p = table[o, 1, pl.ds(begin, CHUNK), :]
                cosine = cos_p * cos_z - sin_p * sin_z
                sine = sin_p * cos_z + cos_p * sin_z
                cosine = jnp.concatenate([cosine] * (vectors // LANES), axis=1)
                sine = jnp.concatenate([sine] * (vectors // LANES), axis=1)
                real = slabs[src, 0, colour, pl.ds(off + begin, CHUNK), :].astype(F32)
                imag = slabs[src, 1, colour, pl.ds(off + begin, CHUNK), :].astype(F32)
                mixed[colour, pl.ds(begin, CHUNK), :] = (cosine * real + sine * imag).astype(BF16)
                mixed[colour, pl.ds(PLANE + begin, CHUNK), :] = (
                    cosine * imag - sine * real
                ).astype(BF16)

        def step(o, mixed, later, following):
            total = None
            for colour in range(colours):
                turn_phases(later, following, colour)
            for colour in range(colours):
                term = jnp.dot(turned[colour], mixed[colour], preferred_element_type=F32)
                total = term if total is None else total + term
            acc[o] += total

        found = lax.fori_loop(0, operators, collect, jnp.int32(0))

        @pl.when((found > 0) & (m >= near if late else m >= 0))
        def _():
            for colour in range(colours):
                for part in range(2):
                    for begin in range(0, PLANE, CHUNK):
                        rows = slabs[m, part, colour, pl.ds(begin, CHUNK), :].astype(F32)
                        rows = pltpu.roll(rows.reshape(CHUNK // LX, LX, vectors), LX - 1, 1)
                        slabs[held, part, colour, pl.ds(begin, CHUNK), :] = rows.reshape(
                            CHUNK, vectors
                        ).astype(BF16)

        @pl.when(found > 0)
        def _():
            for colour in range(colours):
                for part in range(2):
                    block = slabs[m, part, colour, pl.ds(0, PLANE), :]
                    flat = block.T.reshape(half_rows // block_rows, 2, block_rows, PLANE)
                    flat = jnp.where(core == 0, flat[:, 0], flat[:, 1]).reshape(half_rows, PLANE)
                    same = flat if part == 0 else -flat
                    lower = pl.ds(half_rows, half_rows)
                    turned[colour, pl.ds(0, half_rows), pl.ds(part * PLANE, PLANE)] = flat
                    turned[colour, lower, pl.ds((1 - part) * PLANE, PLANE)] = same
            for colour in range(colours):
                turn_phases(todo[0], mixed_a, colour)

            def two(i, inner):
                step(todo[2 * i], mixed_a, todo[jnp.minimum(2 * i + 1, found - 1)], mixed_b)

                @pl.when(2 * i + 1 < found)
                def _():
                    after = todo[jnp.minimum(2 * i + 2, found - 1)]
                    step(todo[2 * i + 1], mixed_b, after, mixed_a)

                return inner

            lax.fori_loop(0, (found + 1) // 2, two, 0)

        return carry

    lax.fori_loop(0, held, one_slab, 0)

    if late:
        first = pl.multiple_of(me // 2 * block_rows, block_rows)
        half = lax.rem(lax.axis_index("tm"), 2)
        for o in range(operators):
            acc_out[o] = acc[o].astype(BF16)
        for part in range(2):
            for o in range(operators):
                rows = pl.ds(part * half_rows + first, block_rows)
                own = acc[o, rows, :]
                at = pl.ds((part * operators + o) * block_rows, block_rows)
                wide[0, at, :] = own[:, :LANES]
                wide[1, at, :] = own[:, LANES:]
        keep_ref[...] = spread(wide.at[half], 2 * operators, block_rows)
        send_ref[...] = spread(wide.at[1 - half], 2 * operators, block_rows)


def elementals(tables, slab_list, near, prior, block_rows):
    _, colours, plane, vectors = slab_list[0].shape
    held = len(slab_list)
    operators = tables[0].shape[0]
    late = prior is not None
    wide = jax.ShapeDtypeStruct((operators, vectors, vectors), F32)
    scratch = [
        pltpu.VMEM((held + 1, 2, colours, plane + LX, vectors), BF16),
        pltpu.VMEM((colours, vectors, 2 * plane), BF16),
        pltpu.VMEM((colours, 2 * plane, vectors), BF16),
        pltpu.VMEM((colours, 2 * plane, vectors), BF16),
        pltpu.SMEM((operators,), jnp.int32),
    ]
    if late:
        piece = jax.ShapeDtypeStruct(
            (2 * operators * GROUPS, block_rows // GROUPS * LANES), BF16
        )
        outs = (jax.ShapeDtypeStruct(wide.shape, BF16), piece, piece)
        out_specs = (VMEM, VMEM, VMEM)
        scratch.append(pltpu.VMEM(wide.shape, F32))
        scratch.append(pltpu.VMEM((2, 2 * operators * block_rows, LANES), F32))
    else:
        outs = (wide, jax.ShapeDtypeStruct((operators, 2, plane, LANES), F32))
        out_specs = (VMEM, VMEM)
    move, z_phase, phases = tables
    priors = [phases, prior] if late else [phases]
    return pl.pallas_call(
        functools.partial(elemental_kernel, held, near, late, block_rows),
        out_shape=outs,
        in_specs=[SMEM, SMEM] + [VMEM] * (held + len(priors)),
        out_specs=out_specs,
        scratch_shapes=scratch,
        compiler_params=params(20 + held),
        cost_estimate=pl.CostEstimate(
            flops=8 * held * operators * colours * plane * vectors * vectors,
            bytes_accessed=held * 2 * colours * plane * vectors * 2,
            transcendentals=0,
        ),
        name="elementals_late" if late else "elementals_early",
    )(move, z_phase, *slab_list, *priors)


def both_kernel(blocks, e_ref, other_ref, *refs):
    peram_refs = refs[:blocks]
    keep_ref, rest = refs[blocks], refs[blocks + 1 :]
    whole, sorted_rows, left, middle = rest[-4:]
    send_refs = rest[:-4]
    each = keep_ref.shape[0] // len(send_refs)
    sources, _, vectors, _ = whole.shape
    operators = e_ref.shape[0]
    block_rows = keep_ref.shape[3]
    me = lax.axis_index("space")
    half = lax.rem(lax.axis_index("tm"), 2)
    for m in range(blocks):
        begin = pl.multiple_of((me ^ m) * block_rows, block_rows)
        whole[:, :, pl.ds(begin, block_rows), :] = peram_refs[m][...]
        begin = (m % 2) * (vectors // 2) + (me ^ m) // 2 * block_rows
        begin = pl.multiple_of(begin, block_rows)
        sorted_rows[:, :, pl.ds(begin, block_rows), :] = peram_refs[m][...]
    row = lax.broadcasted_iota(jnp.int32, (block_rows, vectors), 0)
    column = lax.broadcasted_iota(jnp.int32, (block_rows, vectors), 1)
    chosen = (column == row + me * block_rows).astype(F32).astype(BF16)
    for s in range(sources):
        for part in range(2):
            flat = lax.dot_general(
                chosen, whole[s, part], (((1,), (1,)), ((), ())), preferred_element_type=F32
            )
            left[pl.ds((part * sources + s) * block_rows, block_rows), :] = flat.astype(BF16)
    group = sources * block_rows
    cut = vectors // 2
    for a in range(operators):
        sides = []
        for ref in (e_ref, other_ref):
            product = lax.dot_general(
                left[...], ref[a], (((1,), (1,)), ((), ())), preferred_element_type=F32
            )
            sides.append(
                (
                    product[:group, :cut] - product[group:, cut:],
                    product[:group, cut:] + product[group:, :cut],
                )
            )
        real, imaginary = (
            jnp.concatenate([one, two], axis=1) for one, two in zip(*sides)
        )
        for part, block in enumerate((real, imaginary)):
            block = block.astype(BF16)
            for s in range(sources):
                base = s * block_rows
                rows = pl.ds(a * block_rows, block_rows)
                columns = pl.ds(part * vectors, vectors)
                middle[s, rows, columns] = block[base : base + block_rows]
    for s in range(sources):
        real, imaginary = sorted_rows[s, 0], sorted_rows[s, 1]
        right = jnp.concatenate(
            [
                jnp.concatenate([real, -imaginary], axis=1),
                jnp.concatenate([imaginary, real], axis=1),
            ],
            axis=0,
        )
        image = jnp.dot(middle[s], right, preferred_element_type=F32)
        image = image.astype(BF16)
        for a in range(operators):
            for part in range(2):
                rows = image[a * block_rows : (a + 1) * block_rows]
                low = rows[:, part * vectors : part * vectors + LANES]
                high = rows[:, part * vectors + LANES : (part + 1) * vectors]
                keep_ref[s, part, a] = jnp.where(half == 0, low, high)
                send_refs[s // each][s % each, part, a] = jnp.where(half == 0, high, low)


def both_sides(elements, others, perams):
    blocks = len(perams)
    sources, _, block_rows, vectors = perams[0].shape
    operators = elements.shape[0]
    piece = jax.ShapeDtypeStruct((sources, 2, operators, block_rows, LANES), BF16)
    sends = 2 - sources % 2
    part = jax.ShapeDtypeStruct((sources // sends,) + piece.shape[1:], BF16)
    return pl.pallas_call(
        functools.partial(both_kernel, blocks),
        out_shape=(piece,) + (part,) * sends,
        in_specs=[VMEM] * (2 + blocks),
        out_specs=(VMEM,) * (1 + sends),
        scratch_shapes=[
            pltpu.VMEM((sources, 2, vectors, vectors), BF16),
            pltpu.VMEM((sources, 2, vectors, vectors), BF16),
            pltpu.VMEM((2 * sources * block_rows, vectors), BF16),
            pltpu.VMEM((sources, operators * block_rows, 2 * vectors), BF16),
        ],
        compiler_params=params(16),
        cost_estimate=pl.CostEstimate(flops=0, bytes_accessed=0, transcendentals=0),
        name="both_sides",
    )(elements, others, *perams)


def spread(wide, count_rows, block_rows):
    fold = block_rows // GROUPS
    pieces = [
        wide[pl.ds(k, count_rows * GROUPS, stride=fold), :].astype(BF16) for k in range(fold)
    ]
    return jnp.concatenate(pieces, axis=1)


def lay_kernel(own_ref, *refs):
    pair_refs, out_ref, wide = refs[:-2], refs[-2], refs[-1]
    each = own_ref.shape[0] // len(pair_refs)
    sources, _, operators, block_rows, lanes = own_ref.shape
    rows = 2 * operators
    for s in range(sources):
        for at, ref in enumerate((own_ref.at[s], pair_refs[s // each].at[s % each])):
            wide[pl.ds(at * rows * block_rows, rows * block_rows), :] = (
                ref[...].astype(F32).reshape(rows * block_rows, lanes)
            )
        out_ref[s] = spread(wide, 2 * rows, block_rows)


def lay_out(own, pair):
    sources, _, operators, block_rows, lanes = own.shape
    rows = 2 * operators
    return pl.pallas_call(
        lay_kernel,
        out_shape=jax.ShapeDtypeStruct(
            (sources, 2 * rows * GROUPS, block_rows // GROUPS * lanes), BF16
        ),
        in_specs=[VMEM] * (1 + len(pair)),
        out_specs=VMEM,
        scratch_shapes=[pltpu.VMEM((2 * rows * block_rows, lanes), F32)],
        compiler_params=params(12),
        cost_estimate=pl.CostEstimate(flops=0, bytes_accessed=0, transcendentals=0),
        name="lay_out",
    )(own, *pair)


def trace_kernel(count, table, line, times_ref, *refs):
    pools = refs[:count]
    laid_ref, out_ref, picked = refs[count:]
    sources = laid_ref.shape[0]
    groups = GROUPS
    rows = pools[0].shape[0] // groups
    time = lax.axis_index("tm")
    for s in range(sources):
        source = times_ref[s]
        code = line_code(time // 2, source // 2, lax.rem(source + time, 2), line)
        for index, (at, inside) in table.items():

            @pl.when(code == index)
            def _(at=at, inside=inside, s=s):
                block = pools[at] if inside is None else pools[at].at[inside]
                picked[s] = block[...]

    shape = (2 * rows * groups, rows * groups)
    down = lax.broadcasted_iota(jnp.int32, shape, 0)
    over = lax.broadcasted_iota(jnp.int32, shape, 1)
    same = down % groups == over % groups
    shape = (rows * groups, rows)
    down = lax.broadcasted_iota(jnp.int32, shape, 0)
    over = lax.broadcasted_iota(jnp.int32, shape, 1)
    gather = (down // groups == over).astype(F32)
    sums = []
    for s in range(sources):
        product = lax.dot_general(
            laid_ref[s],
            picked[s],
            (((1,), (1,)), ((), ())),
            preferred_element_type=F32,
        )
        product = jnp.where(same, product, 0.0).reshape(2 * rows, groups, rows * groups)
        sums.append(jnp.sum(product, axis=1))
    folded = jnp.dot(
        jnp.concatenate(sums, axis=0),
        gather,
        precision=lax.Precision.HIGHEST,
        preferred_element_type=F32,
    )
    for s in range(sources):
        out_ref[0, s] = folded[2 * rows * s : 2 * rows * s + rows]
        out_ref[1, s] = folded[2 * rows * s + rows : 2 * rows * (s + 1)]


def traces(source_times, pools, table, line, laid):
    sources = laid.shape[0]
    rows = pools[0].shape[0] // GROUPS
    return pl.pallas_call(
        functools.partial(trace_kernel, len(pools), table, line),
        out_shape=jax.ShapeDtypeStruct((2, sources, rows, rows), F32),
        in_specs=[SMEM] + [VMEM] * (len(pools) + 1),
        out_specs=VMEM,
        scratch_shapes=[
            pltpu.VMEM((sources,) + pools[0].shape, BF16),
        ],
        compiler_params=params(12),
        cost_estimate=pl.CostEstimate(
            flops=4 * laid.size * rows,
            bytes_accessed=2 * laid.size,
            transcendentals=0,
        ),
        name="traces",
    )(source_times, *pools, laid)


def finish_kernel(count, *refs):
    parts = refs[:count]
    correlator_ref, pairs_ref = refs[count:]
    sources, rows, _ = parts[1].shape
    n = rows // 2
    eye = lax.broadcasted_iota(jnp.int32, (n, n), 0) == lax.broadcasted_iota(jnp.int32, (n, n), 1)
    for s in range(sources):
        terms = [parts[0][0, s]] + [ref[s] for ref in parts[1:]]
        while len(terms) > 1:
            terms = [one + two for one, two in zip(terms[::2], terms[1::2])]
        total = terms[0]
        real = total[:n, :n] - total[n:, n:]
        imaginary = total[:n, n:] + total[n:, :n]
        correlator_ref[0, s, :, 0, :] = real
        correlator_ref[0, s, :, 1, :] = imaginary
        down_real, down_imaginary, over_real, over_imaginary = (
            jnp.sum(jnp.where(eye, block, 0.0), axis=axis, keepdims=True)
            for axis in (1, 0)
            for block in (real, imaginary)
        )
        pairs_ref[0, s, :, 0, :] = down_real * over_real - down_imaginary * over_imaginary
        pairs_ref[0, s, :, 1, :] = down_real * over_imaginary + down_imaginary * over_real


def finish(parts):
    sources, rows, _ = parts[1].shape
    result = jax.ShapeDtypeStruct((1, sources, rows // 2, 2, rows // 2), F32)
    correlator, pairs = pl.pallas_call(
        functools.partial(finish_kernel, len(parts)),
        out_shape=(result, result),
        in_specs=[VMEM] * len(parts),
        out_specs=(VMEM, VMEM),
        compiler_params=params(4),
        name="finish",
    )(*parts)
    return jnp.swapaxes(correlator, 2, 3), jnp.swapaxes(pairs, 2, 3)


def phase_tables(momenta, z_coords, z_extent):
    plane = jnp.arange(PLANE, dtype=jnp.int32)
    along_x = (momenta[:, 0:1] * (plane % LX)[None] % LX).astype(F32) * (2.0 * math.pi / LX)
    along_y = (momenta[:, 1:2] * (plane // LX)[None] % LY).astype(F32) * (2.0 * math.pi / LY)
    angle = along_x + along_y
    table = jnp.stack([jnp.cos(angle), jnp.sin(angle)], axis=1).reshape(-1, PLANE)
    along_z = (momenta[:, 2][None, :] * z_coords[:, None] % z_extent).astype(F32) * (
        2.0 * math.pi / z_extent
    )
    return table, jnp.stack([jnp.cos(along_z), jnp.sin(along_z)])


def body(eigenvectors, momenta, displacement, source_times, perambulators):
    _, parts, colours, _, plane, vectors = eigenvectors.shape
    slabs = lax.axis_size("space")
    line = lax.axis_size("tm") // 2
    block_rows = vectors // slabs
    near = 2

    own = eigenvectors.reshape(parts, colours, plane, vectors)
    beside = swap_bit(own, "space", 1)
    keys = swap_far(own)

    plane_phase, z_phase = phase_tables(momenta, jnp.arange(slabs, dtype=jnp.int32), slabs)
    tables = (displacement, z_phase, plane_phase)
    total, wide_phase = elementals(tables, [own, beside], near, None, block_rows)

    keys, total = lax.optimization_barrier((keys, total))
    slab_list = swap_near(keys)
    slab_list[1] = beside
    peram, _ = lax.optimization_barrier((perambulators[0], keys[slabs // 2]))
    perams = swap_far(peram)
    tables = (displacement, z_phase, wide_phase)
    full, keep, send = elementals(tables, slab_list, near, total, block_rows)

    perams, full, send = lax.optimization_barrier((perams, full, send))
    perams = swap_near(perams)

    received = swap_bit(send, "tm", 1)
    g_keep, *g_send = both_sides(full, swap_bit(full, "space", 1), perams)
    arrays, table, g_send = share_line(keep, received, g_send, line)
    laid = lay_out(g_keep, [swap_bit(block, "tm", 1) for block in g_send])
    both = traces(source_times, arrays, table, line, laid)
    both = both + swap_bit(both, "space", 1)
    mine, pair = both[0], both[1]
    near_sums = [swap_bit(mine, "space", mask) for mask in range(2, slabs, 2)]
    pair_sums = [swap_bit(pair, "tm", 1)]
    pair_sums += [across(pair, mask) for mask in range(2, slabs, 2)]
    return finish([both] + near_sums + pair_sums)


def across(block, mask):
    rows, times = lax.axis_size("space"), lax.axis_size("tm")
    route = [
        (i * times + t, (i ^ mask) * times + (t ^ 1)) for i in range(rows) for t in range(times)
    ]
    return lax.ppermute(block, ("space", "tm"), route)


def solution(mesh):
    placed = (
        P("tm", None, None, "space", None, None),
        P(),
        P(),
        P(),
        P("tm", None, None, "space", None),
    )
    return jax.shard_map(
        body,
        mesh=mesh,
        in_specs=placed,
        out_specs=(P("tm", None, None, None, None), P("tm", None, None, None, None)),
        check_vma=False,
    )
```

```python
import functools
import math

import jax
import jax.numpy as jnp
from jax import lax
from jax.experimental import pallas as pl
from jax.experimental.pallas import tpu as pltpu
from jax.sharding import PartitionSpec as P

LX = 16
LY = 16
PLANE = LX * LY
LANES = 128
F32 = jnp.float32
BF16 = jnp.bfloat16
CHUNK = 32
GROUPS = 8
MEGA = 1024 * 1024

SMEM = pl.BlockSpec(memory_space=pltpu.SMEM)
VMEM = pl.BlockSpec(memory_space=pltpu.VMEM)


def swap_bit(block, axis, mask):
    count = lax.axis_size(axis)
    return lax.ppermute(block, axis, [(i, i ^ mask) for i in range(count)])


def along_line(block, moves):
    route = [(2 * z + x, 2 * to + x) for z, to in moves.items() for x in range(2)]
    return lax.ppermute(block, "tm", route)


def share_line(keep, received, g_send, line):
    piece = jnp.stack([keep, received])
    if line != 4:
        arrays, table = [keep, received], {0: (0, None), 1: (1, None)}
        for distance in range(1, line):
            moved = along_line(piece, {z: (z + distance) % line for z in range(line)})
            for side in range(2):
                table[2 * distance + side] = (len(arrays), side)
            arrays.append(moved)
        return arrays, table, g_send
    outward = {1: 0, 2: 3}
    piece = jnp.stack([keep, received])
    opposite = along_line(piece, {1: 2, 2: 1, 0: 3, 3: 0})
    near = along_line(piece, {0: 1, 1: 0, 2: 3, 3: 2})
    skip = along_line(piece, {0: 2, 3: 1})
    passed = along_line(opposite, outward)
    arrays = [keep, received, near, skip, opposite, passed]
    table = {0: (0, None), 1: (1, None)}
    for code in range(2, 10):
        table[code] = (1 + code // 2, code % 2)
    return arrays, table, g_send


def line_code(here, there, side, line):
    if line != 4:
        return 2 * lax.rem(here - there + line, line) + side
    apart = here ^ there
    ends = (here == 0) | (here == line - 1)
    return 2 * jnp.where(ends & (apart == 2), 4, apart) + side


def swap_far(block):
    held = {0: block}
    mask = lax.axis_size("space") // 2
    while mask >= 2:
        for key in sorted(held):
            held[key | mask] = swap_bit(held[key], "space", mask)
        mask //= 2
    return held


def swap_near(held):
    both = dict(held)
    for key in sorted(held):
        both[key | 1] = swap_bit(held[key], "space", 1)
    return [both[key] for key in sorted(both)]


def params(megabytes):
    return pltpu.CompilerParams(vmem_limit_bytes=megabytes * MEGA)


def elemental_kernel(held, near, late, block_rows, *refs):
    move_ref, zphase_ref = refs[:2]
    slab_refs = refs[2 : 2 + held]
    rest = refs[2 + held :]
    if not late:
        phase_ref, rest = rest[0], rest[1:]
    if late:
        table, prior_ref, acc_out, keep_ref, send_ref = rest[:5]
        slabs, turned, mixed_a, mixed_b, todo, acc, wide = rest[5:]
    else:
        acc, table, slabs, turned, mixed_a, mixed_b, todo = rest
    operators, half_rows, vectors = acc.shape
    half_rows //= 2
    colours = turned.shape[0]
    count = lax.axis_size("space")
    me = lax.axis_index("space")
    core = lax.rem(me, 2)

    for m in range(held):
        slabs[m, :, :, pl.ds(0, PLANE), :] = slab_refs[m][...]
        slabs[m, :, :, pl.ds(PLANE, LX), :] = slab_refs[m][:, :, pl.ds(0, LX), :]
    acc[...] = prior_ref[...] if late else jnp.zeros_like(acc)
    if not late:
        upright = phase_ref[...].T
        for o in range(operators):
            for part in range(2):
                at = 2 * o + part
                table[o, part] = jnp.broadcast_to(upright[:, at : at + 1], (PLANE, LANES))
    def one_slab(m, carry):
        here = me ^ m
        above = lax.rem(here + 1, count) ^ me
        far = above >= near

        def collect(o, found):
            waits = (m >= near) | ((move_ref[o] == 3) & far)
            chosen = waits if late else jnp.logical_not(waits)

            @pl.when(chosen)
            def _():
                todo[found] = o

            return found + chosen.astype(jnp.int32)

        def turn_phases(o, mixed, colour):
            move = move_ref[o]
            src = jnp.where(move == 3, above, jnp.where(move == 1, held, m))
            off = pl.multiple_of(jnp.where(move == 2, LX, 0), LX)
            cos_z, sin_z = zphase_ref[0, here, o], zphase_ref[1, here, o]
            for begin in range(0, PLANE, CHUNK):
                cos_p = table[o, 0, pl.ds(begin, CHUNK), :]
                sin_p = table[o, 1, pl.ds(begin, CHUNK), :]
                cosine = cos_p * cos_z - sin_p * sin_z
                sine = sin_p * cos_z + cos_p * sin_z
                cosine = jnp.concatenate([cosine] * (vectors // LANES), axis=1)
                sine = jnp.concatenate([sine] * (vectors // LANES), axis=1)
                real = slabs[src, 0, colour, pl.ds(off + begin, CHUNK), :].astype(F32)
                imag = slabs[src, 1, colour, pl.ds(off + begin, CHUNK), :].astype(F32)
                mixed[colour, pl.ds(begin, CHUNK), :] = (cosine * real + sine * imag).astype(BF16)
                mixed[colour, pl.ds(PLANE + begin, CHUNK), :] = (
                    cosine * imag - sine * real
                ).astype(BF16)

        def step(o, mixed, later, following):
            total = None
            for colour in range(colours):
                turn_phases(later, following, colour)
            for colour in range(colours):
                term = jnp.dot(turned[colour], mixed[colour], preferred_element_type=F32)
                total = term if total is None else total + term
            acc[o] += total

        found = lax.fori_loop(0, operators, collect, jnp.int32(0))

        @pl.when((found > 0) & (m >= near if late else m >= 0))
        def _():
            for colour in range(colours):
                for part in range(2):
                    for begin in range(0, PLANE, CHUNK):
                        rows = slabs[m, part, colour, pl.ds(begin, CHUNK), :].astype(F32)
                        rows = pltpu.roll(rows.reshape(CHUNK // LX, LX, vectors), LX - 1, 1)
                        slabs[held, part, colour, pl.ds(begin, CHUNK), :] = rows.reshape(
                            CHUNK, vectors
                        ).astype(BF16)

        @pl.when(found > 0)
        def _():
            for colour in range(colours):
                for part in range(2):
                    block = slabs[m, part, colour, pl.ds(0, PLANE), :]
                    flat = block.T.reshape(half_rows // block_rows, 2, block_rows, PLANE)
                    flat = jnp.where(core == 0, flat[:, 0], flat[:, 1]).reshape(half_rows, PLANE)
                    same = flat if part == 0 else -flat
                    lower = pl.ds(half_rows, half_rows)
                    turned[colour, pl.ds(0, half_rows), pl.ds(part * PLANE, PLANE)] = flat
                    turned[colour, lower, pl.ds((1 - part) * PLANE, PLANE)] = same
            for colour in range(colours):
                turn_phases(todo[0], mixed_a, colour)

            def two(i, inner):
                step(todo[2 * i], mixed_a, todo[jnp.minimum(2 * i + 1, found - 1)], mixed_b)

                @pl.when(2 * i + 1 < found)
                def _():
                    after = todo[jnp.minimum(2 * i + 2, found - 1)]
                    step(todo[2 * i + 1], mixed_b, after, mixed_a)

                return inner

            lax.fori_loop(0, (found + 1) // 2, two, 0)

        return carry

    lax.fori_loop(0, held, one_slab, 0)

    if late:
        first = pl.multiple_of(me // 2 * block_rows, block_rows)
        half = lax.rem(lax.axis_index("tm"), 2)
        for o in range(operators):
            acc_out[o] = acc[o].astype(BF16)
        for part in range(2):
            for o in range(operators):
                rows = pl.ds(part * half_rows + first, block_rows)
                own = acc[o, rows, :]
                at = pl.ds((part * operators + o) * block_rows, block_rows)
                wide[0, at, :] = own[:, :LANES]
                wide[1, at, :] = own[:, LANES:]
        keep_ref[...] = spread(wide.at[half], 2 * operators, block_rows)
        send_ref[...] = spread(wide.at[1 - half], 2 * operators, block_rows)


def elementals(tables, slab_list, near, prior, block_rows):
    _, colours, plane, vectors = slab_list[0].shape
    held = len(slab_list)
    operators = tables[0].shape[0]
    late = prior is not None
    wide = jax.ShapeDtypeStruct((operators, vectors, vectors), F32)
    scratch = [
        pltpu.VMEM((held + 1, 2, colours, plane + LX, vectors), BF16),
        pltpu.VMEM((colours, vectors, 2 * plane), BF16),
        pltpu.VMEM((colours, 2 * plane, vectors), BF16),
        pltpu.VMEM((colours, 2 * plane, vectors), BF16),
        pltpu.SMEM((operators,), jnp.int32),
    ]
    if late:
        piece = jax.ShapeDtypeStruct(
            (2 * operators * GROUPS, block_rows // GROUPS * LANES), BF16
        )
        outs = (jax.ShapeDtypeStruct(wide.shape, BF16), piece, piece)
        out_specs = (VMEM, VMEM, VMEM)
        scratch.append(pltpu.VMEM(wide.shape, F32))
        scratch.append(pltpu.VMEM((2, 2 * operators * block_rows, LANES), F32))
    else:
        outs = (wide, jax.ShapeDtypeStruct((operators, 2, plane, LANES), F32))
        out_specs = (VMEM, VMEM)
    move, z_phase, phases = tables
    priors = [phases, prior] if late else [phases]
    return pl.pallas_call(
        functools.partial(elemental_kernel, held, near, late, block_rows),
        out_shape=outs,
        in_specs=[SMEM, SMEM] + [VMEM] * (held + len(priors)),
        out_specs=out_specs,
        scratch_shapes=scratch,
        compiler_params=params(20 + held),
        cost_estimate=pl.CostEstimate(
            flops=8 * held * operators * colours * plane * vectors * vectors,
            bytes_accessed=held * 2 * colours * plane * vectors * 2,
            transcendentals=0,
        ),
        name="elementals_late" if late else "elementals_early",
    )(move, z_phase, *slab_list, *priors)


def both_kernel(blocks, e_ref, other_ref, *refs):
    peram_refs = refs[:blocks]
    keep_ref, rest = refs[blocks], refs[blocks + 1 :]
    whole, sorted_rows, left, middle = rest[-4:]
    send_refs = rest[:-4]
    each = keep_ref.shape[0] // len(send_refs)
    sources, _, vectors, _ = whole.shape
    operators = e_ref.shape[0]
    block_rows = keep_ref.shape[3]
    me = lax.axis_index("space")
    half = lax.rem(lax.axis_index("tm"), 2)
    for m in range(blocks):
        begin = pl.multiple_of((me ^ m) * block_rows, block_rows)
        whole[:, :, pl.ds(begin, block_rows), :] = peram_refs[m][...]
        begin = (m % 2) * (vectors // 2) + (me ^ m) // 2 * block_rows
        begin = pl.multiple_of(begin, block_rows)
        sorted_rows[:, :, pl.ds(begin, block_rows), :] = peram_refs[m][...]
    row = lax.broadcasted_iota(jnp.int32, (block_rows, vectors), 0)
    column = lax.broadcasted_iota(jnp.int32, (block_rows, vectors), 1)
    chosen = (column == row + me * block_rows).astype(F32).astype(BF16)
    for s in range(sources):
        for part in range(2):
            flat = lax.dot_general(
                chosen, whole[s, part], (((1,), (1,)), ((), ())), preferred_element_type=F32
            )
            left[pl.ds((part * sources + s) * block_rows, block_rows), :] = flat.astype(BF16)
    group = sources * block_rows
    cut = vectors // 2
    for a in range(operators):
        sides = []
        for ref in (e_ref, other_ref):
            product = lax.dot_general(
                left[...], ref[a], (((1,), (1,)), ((), ())), preferred_element_type=F32
            )
            sides.append(
                (
                    product[:group, :cut] - product[group:, cut:],
                    product[:group, cut:] + product[group:, :cut],
                )
            )
        real, imaginary = (
            jnp.concatenate([one, two], axis=1) for one, two in zip(*sides)
        )
        for part, block in enumerate((real, imaginary)):
            high = block.astype(BF16)
            low = (block - high.astype(F32)).astype(BF16)
            for s in range(sources):
                base = s * block_rows
                rows = pl.ds(a * block_rows, block_rows)
                columns = pl.ds(part * vectors, vectors)
                middle[0, s, rows, columns] = high[base : base + block_rows]
                middle[1, s, rows, columns] = low[base : base + block_rows]
    for s in range(sources):
        real, imaginary = sorted_rows[s, 0], sorted_rows[s, 1]
        right = jnp.concatenate(
            [
                jnp.concatenate([real, -imaginary], axis=1),
                jnp.concatenate([imaginary, real], axis=1),
            ],
            axis=0,
        )
        image = jnp.dot(middle[0, s], right, preferred_element_type=F32)
        image = image + jnp.dot(middle[1, s], right, preferred_element_type=F32)
        image = image.astype(BF16)
        for a in range(operators):
            for part in range(2):
                rows = image[a * block_rows : (a + 1) * block_rows]
                low = rows[:, part * vectors : part * vectors + LANES]
                high = rows[:, part * vectors + LANES : (part + 1) * vectors]
                keep_ref[s, part, a] = jnp.where(half == 0, low, high)
                send_refs[s // each][s % each, part, a] = jnp.where(half == 0, high, low)


def both_sides(elements, others, perams):
    blocks = len(perams)
    sources, _, block_rows, vectors = perams[0].shape
    operators = elements.shape[0]
    piece = jax.ShapeDtypeStruct((sources, 2, operators, block_rows, LANES), BF16)
    sends = 2 - sources % 2
    part = jax.ShapeDtypeStruct((sources // sends,) + piece.shape[1:], BF16)
    return pl.pallas_call(
        functools.partial(both_kernel, blocks),
        out_shape=(piece,) + (part,) * sends,
        in_specs=[VMEM] * (2 + blocks),
        out_specs=(VMEM,) * (1 + sends),
        scratch_shapes=[
            pltpu.VMEM((sources, 2, vectors, vectors), BF16),
            pltpu.VMEM((sources, 2, vectors, vectors), BF16),
            pltpu.VMEM((2 * sources * block_rows, vectors), BF16),
            pltpu.VMEM((2, sources, operators * block_rows, 2 * vectors), BF16),
        ],
        compiler_params=params(16),
        cost_estimate=pl.CostEstimate(flops=0, bytes_accessed=0, transcendentals=0),
        name="both_sides",
    )(elements, others, *perams)


def spread(wide, count_rows, block_rows):
    fold = block_rows // GROUPS
    pieces = [
        wide[pl.ds(k, count_rows * GROUPS, stride=fold), :].astype(BF16) for k in range(fold)
    ]
    return jnp.concatenate(pieces, axis=1)


def lay_kernel(own_ref, *refs):
    pair_refs, out_ref, wide = refs[:-2], refs[-2], refs[-1]
    each = own_ref.shape[0] // len(pair_refs)
    sources, _, operators, block_rows, lanes = own_ref.shape
    rows = 2 * operators
    for s in range(sources):
        for at, ref in enumerate((own_ref.at[s], pair_refs[s // each].at[s % each])):
            wide[pl.ds(at * rows * block_rows, rows * block_rows), :] = (
                ref[...].astype(F32).reshape(rows * block_rows, lanes)
            )
        out_ref[s] = spread(wide, 2 * rows, block_rows)


def lay_out(own, pair):
    sources, _, operators, block_rows, lanes = own.shape
    rows = 2 * operators
    return pl.pallas_call(
        lay_kernel,
        out_shape=jax.ShapeDtypeStruct(
            (sources, 2 * rows * GROUPS, block_rows // GROUPS * lanes), BF16
        ),
        in_specs=[VMEM] * (1 + len(pair)),
        out_specs=VMEM,
        scratch_shapes=[pltpu.VMEM((2 * rows * block_rows, lanes), F32)],
        compiler_params=params(12),
        cost_estimate=pl.CostEstimate(flops=0, bytes_accessed=0, transcendentals=0),
        name="lay_out",
    )(own, *pair)


def trace_kernel(count, table, line, times_ref, *refs):
    pools = refs[:count]
    laid_ref, out_ref, picked = refs[count:]
    sources = laid_ref.shape[0]
    groups = GROUPS
    rows = pools[0].shape[0] // groups
    time = lax.axis_index("tm")
    for s in range(sources):
        source = times_ref[s]
        code = line_code(time // 2, source // 2, lax.rem(source + time, 2), line)
        for index, (at, inside) in table.items():

            @pl.when(code == index)
            def _(at=at, inside=inside, s=s):
                block = pools[at] if inside is None else pools[at].at[inside]
                picked[s] = block[...]

    shape = (2 * rows * groups, rows * groups)
    down = lax.broadcasted_iota(jnp.int32, shape, 0)
    over = lax.broadcasted_iota(jnp.int32, shape, 1)
    same = down % groups == over % groups
    shape = (rows * groups, rows)
    down = lax.broadcasted_iota(jnp.int32, shape, 0)
    over = lax.broadcasted_iota(jnp.int32, shape, 1)
    gather = (down // groups == over).astype(F32)
    sums = []
    for s in range(sources):
        product = lax.dot_general(
            laid_ref[s],
            picked[s],
            (((1,), (1,)), ((), ())),
            preferred_element_type=F32,
        )
        product = jnp.where(same, product, 0.0).reshape(2 * rows, groups, rows * groups)
        sums.append(jnp.sum(product, axis=1))
    folded = jnp.dot(
        jnp.concatenate(sums, axis=0),
        gather,
        precision=lax.Precision.HIGHEST,
        preferred_element_type=F32,
    )
    for s in range(sources):
        out_ref[0, s] = folded[2 * rows * s : 2 * rows * s + rows]
        out_ref[1, s] = folded[2 * rows * s + rows : 2 * rows * (s + 1)]


def traces(source_times, pools, table, line, laid):
    sources = laid.shape[0]
    rows = pools[0].shape[0] // GROUPS
    return pl.pallas_call(
        functools.partial(trace_kernel, len(pools), table, line),
        out_shape=jax.ShapeDtypeStruct((2, sources, rows, rows), F32),
        in_specs=[SMEM] + [VMEM] * (len(pools) + 1),
        out_specs=VMEM,
        scratch_shapes=[
            pltpu.VMEM((sources,) + pools[0].shape, BF16),
        ],
        compiler_params=params(12),
        cost_estimate=pl.CostEstimate(
            flops=4 * laid.size * rows,
            bytes_accessed=2 * laid.size,
            transcendentals=0,
        ),
        name="traces",
    )(source_times, *pools, laid)


def finish_kernel(count, *refs):
    parts = refs[:count]
    correlator_ref, pairs_ref = refs[count:]
    sources, rows, _ = parts[1].shape
    n = rows // 2
    eye = lax.broadcasted_iota(jnp.int32, (n, n), 0) == lax.broadcasted_iota(jnp.int32, (n, n), 1)
    for s in range(sources):
        terms = [parts[0][0, s]] + [ref[s] for ref in parts[1:]]
        while len(terms) > 1:
            terms = [one + two for one, two in zip(terms[::2], terms[1::2])]
        total = terms[0]
        real = total[:n, :n] - total[n:, n:]
        imaginary = total[:n, n:] + total[n:, :n]
        correlator_ref[0, s, :, 0, :] = real
        correlator_ref[0, s, :, 1, :] = imaginary
        down_real, down_imaginary, over_real, over_imaginary = (
            jnp.sum(jnp.where(eye, block, 0.0), axis=axis, keepdims=True)
            for axis in (1, 0)
            for block in (real, imaginary)
        )
        pairs_ref[0, s, :, 0, :] = down_real * over_real - down_imaginary * over_imaginary
        pairs_ref[0, s, :, 1, :] = down_real * over_imaginary + down_imaginary * over_real


def finish(parts):
    sources, rows, _ = parts[1].shape
    result = jax.ShapeDtypeStruct((1, sources, rows // 2, 2, rows // 2), F32)
    correlator, pairs = pl.pallas_call(
        functools.partial(finish_kernel, len(parts)),
        out_shape=(result, result),
        in_specs=[VMEM] * len(parts),
        out_specs=(VMEM, VMEM),
        compiler_params=params(4),
        name="finish",
    )(*parts)
    return jnp.swapaxes(correlator, 2, 3), jnp.swapaxes(pairs, 2, 3)


def phase_tables(momenta, z_coords, z_extent):
    plane = jnp.arange(PLANE, dtype=jnp.int32)
    along_x = (momenta[:, 0:1] * (plane % LX)[None] % LX).astype(F32) * (2.0 * math.pi / LX)
    along_y = (momenta[:, 1:2] * (plane // LX)[None] % LY).astype(F32) * (2.0 * math.pi / LY)
    angle = along_x + along_y
    table = jnp.stack([jnp.cos(angle), jnp.sin(angle)], axis=1).reshape(-1, PLANE)
    along_z = (momenta[:, 2][None, :] * z_coords[:, None] % z_extent).astype(F32) * (
        2.0 * math.pi / z_extent
    )
    return table, jnp.stack([jnp.cos(along_z), jnp.sin(along_z)])


def body(eigenvectors, momenta, displacement, source_times, perambulators):
    _, parts, colours, _, plane, vectors = eigenvectors.shape
    slabs = lax.axis_size("space")
    line = lax.axis_size("tm") // 2
    block_rows = vectors // slabs
    near = 2

    own = eigenvectors.reshape(parts, colours, plane, vectors)
    beside = swap_bit(own, "space", 1)
    keys = swap_far(own)

    plane_phase, z_phase = phase_tables(momenta, jnp.arange(slabs, dtype=jnp.int32), slabs)
    tables = (displacement, z_phase, plane_phase)
    total, wide_phase = elementals(tables, [own, beside], near, None, block_rows)

    keys, total = lax.optimization_barrier((keys, total))
    slab_list = swap_near(keys)
    slab_list[1] = beside
    peram, _ = lax.optimization_barrier((perambulators[0], keys[slabs // 2]))
    perams = swap_far(peram)
    tables = (displacement, z_phase, wide_phase)
    full, keep, send = elementals(tables, slab_list, near, total, block_rows)

    perams, full, send = lax.optimization_barrier((perams, full, send))
    perams = swap_near(perams)

    received = swap_bit(send, "tm", 1)
    g_keep, *g_send = both_sides(full, swap_bit(full, "space", 1), perams)
    arrays, table, g_send = share_line(keep, received, g_send, line)
    laid = lay_out(g_keep, [swap_bit(block, "tm", 1) for block in g_send])
    both = traces(source_times, arrays, table, line, laid)
    both = both + swap_bit(both, "space", 1)
    mine, pair = both[0], both[1]
    near_sums = [swap_bit(mine, "space", mask) for mask in range(2, slabs, 2)]
    pair_sums = [swap_bit(pair, "tm", 1)]
    pair_sums += [across(pair, mask) for mask in range(2, slabs, 2)]
    return finish([both] + near_sums + pair_sums)


def across(block, mask):
    rows, times = lax.axis_size("space"), lax.axis_size("tm")
    route = [
        (i * times + t, (i ^ mask) * times + (t ^ 1)) for i in range(rows) for t in range(times)
    ]
    return lax.ppermute(block, ("space", "tm"), route)


def solution(mesh):
    placed = (
        P("tm", None, None, "space", None, None),
        P(),
        P(),
        P(),
        P("tm", None, None, "space", None),
    )
    return jax.shard_map(
        body,
        mesh=mesh,
        in_specs=placed,
        out_specs=(P("tm", None, None, None, None), P("tm", None, None, None, None)),
        check_vma=False,
    )
```
